32 devices in a mesh: replica: 4 (over z), fsdp: 8 (over y, x, core).
Axes of the slice: x: 2, y: 2, z: 4, core: 2. Of those that a mesh axis runs over, the one named last changes fastest.
Arguments:
- grad_parts: bfloat16 [4, 32, 512, 512], P('replica', None, 'fsdp'), may hold values from -6 to 6
- moment: float32 [32, 512, 512], P(('replica', 'fsdp')), may hold values from -4 to 4
- second_moment: float32 [32, 512, 512], P(('replica', 'fsdp')), may hold values from 0.25 to 4
- left_factor: float32 [32, 512, 512], P(('replica', 'fsdp'))
- right_factor: float32 [32, 512, 512], P(('replica', 'fsdp'))
- left_basis: float32 [32, 512, 512], P(('replica', 'fsdp'))
- right_basis: float32 [32, 512, 512], P(('replica', 'fsdp'))
- block_order: int32 [32], replicated, may hold values from 0 to 31, as said below
- refresh_ids: int32 [3], replicated, may hold values from 0 to 29, as said below
Outputs:
- step_dir: bfloat16 [32, 512, 512], P('replica', 'fsdp')
- left_new: float32 [32, 512, 512], P(('replica', 'fsdp'))
- right_new: float32 [32, 512, 512], P(('replica', 'fsdp'))
The draws below stay inside these ranges and needn't reach their ends.
Inputs may be any that keep to these rules, and one draw needn't show every extreme that they name: Slot s holds block block_order[s]; it is a permutation of the 32 blocks in which block_order[s] // 8 == s // 8. refresh_ids[j] lies in [10 j, 10 j + 9]; the ids are distinct and rising; the first is 0 and the last is 29.
All inputs are finite; a program needn't handle non-finite values.
Results may differ from the reference program's by a relative error of at most 0.011.
Values may be sent and summed in bfloat16 or wider, within the bound.
No kernel may reach another device: no remote copies, remote signals or barrier semaphores. Data moves between devices by JAX's collectives and lax.ppermute only.
A program may use at most 128 MiB of HBM per device.

```python
import math
import jax
import jax.numpy as jnp
from jax import lax

B = 512
GB = 8
NB = 32
NREF = 3
N_REPLICA = 4


def butterfly_rows(matrix, angles):
    size = matrix.shape[0]
    for section in range(angles.shape[0]):
        half = 2 ** section
        shaped = matrix.reshape(size // (2 * half), 2, half, -1)
        upper = shaped[:, 0]
        lower = shaped[:, 1]
        theta = angles[section].reshape(size // (2 * half), half, 1)
        cosine = jnp.cos(theta)
        sine = jnp.sin(theta)
        matrix = jnp.stack([cosine * upper - sine * lower, sine * upper + cosine * lower], axis=1).reshape(size, -1)
    return matrix


def draw_basis(key):
    sections = B.bit_length() - 1
    angles = jax.random.uniform(key, (NB, sections, B // 2), jnp.float32, -math.pi, math.pi)
    identity = jnp.eye(B, dtype=jnp.float32)
    return jax.vmap(lambda angle_set: butterfly_rows(identity, angle_set))(angles)


def draw_factor(key, spectrum):
    sections = B.bit_length() - 1
    angles = jax.random.uniform(key, (NB, sections, B // 2), jnp.float32, -math.pi, math.pi)
    identity = jnp.eye(B, dtype=jnp.float32)

    def build(angle_set, values):
        rotated = butterfly_rows(identity * values[None, :], angle_set)
        both = butterfly_rows(rotated.T, angle_set)
        return 0.5 * (both + both.T)
    return jax.vmap(build)(angles, spectrum)


def draw_left_factor(key, part):
    key = jax.random.fold_in(key, 3)
    first, second = jax.random.split(key)
    spectrum = jnp.exp(jax.random.uniform(second, (NB, B), jnp.float32, math.log(2.0), math.log(20.0)))
    return draw_factor(first, spectrum)


def draw_right_factor(key, part):
    key = jax.random.fold_in(key, 5)
    first, second = jax.random.split(key)
    spectrum = jnp.exp(jax.random.uniform(second, (NB, B), jnp.float32, math.log(2.0), math.log(20.0)))
    return draw_factor(first, spectrum)


def draw_left_basis(key, part):
    key = jax.random.fold_in(key, 7)
    return draw_basis(key)


def draw_right_basis(key, part):
    key = jax.random.fold_in(key, 9)
    return draw_basis(key)


def draw_block_order(key, part):
    key = jax.random.fold_in(key, 11)
    groups = NB // GB
    keys = jax.random.split(key, groups)
    orders = jax.vmap(lambda sub: jax.random.permutation(sub, GB))(keys)
    offsets = (jnp.arange(groups, dtype=jnp.int32) * GB)[:, None]
    return (orders.astype(jnp.int32) + offsets).reshape(-1).astype(jnp.int32)


def draw_refresh_ids(key, part):
    key = jax.random.fold_in(key, 13)
    jitter = jax.random.randint(key, (NREF,), 0, 10, dtype=jnp.int32)
    jitter = jitter.at[0].set(0).at[NREF - 1].set(9)
    return (jnp.arange(NREF, dtype=jnp.int32) * 10 + jitter).astype(jnp.int32)


def level_of(rng, dims, cuts, smallest, top_value):
    def one(dim, shards_of):
        heights = jax.random.uniform(jax.random.fold_in(jax.random.fold_in(rng, 6), dim), (shards_of,), jnp.float32, smallest / len(cuts), top_value / len(cuts))
        return jnp.repeat(jnp.exp(heights), dims[dim] // shards_of).reshape((-1,) + (1,) * (len(dims) - dim - 1))

    loudness = one(*cuts[0])
    for cut in cuts[1:]:
        loudness = loudness * one(*cut)
    return loudness


def noise(own_key, shape, spread, most, cuts=(), kind=jnp.bfloat16):
    entries = jax.random.normal(own_key, shape, jnp.float32) * spread
    if len(cuts) > 0:
        entries = level_of(own_key, shape, cuts, -0.22, 0.18) * entries
    return jnp.clip(entries, min=-most, max=most).astype(kind)


def setup_inputs(seed: int = 0) -> dict:
    arg_keys = jax.random.split(jax.random.key(seed), 10)
    return {
        "grad_parts": noise(arg_keys[0], (N_REPLICA, NB, B, B), 1.0, 6.0, ((0, 4), (2, 8))),
        "moment": noise(arg_keys[1], (NB, B, B), 0.3, 4.0, ((0, 32),), jnp.float32),
        "second_moment": jnp.clip(jnp.exp(math.log(4.0) - 2.7725887 * jax.random.uniform(arg_keys[2], (NB, B, B), jnp.float32) ** level_of(arg_keys[2], (NB, B, B), ((0, 32),), -0.2, 0.2)), 0.25, 4.0),
        "left_factor": draw_left_factor(jax.random.fold_in(arg_keys[9], 71), 0),
        "right_factor": draw_right_factor(jax.random.fold_in(arg_keys[9], 71), 0),
        "left_basis": draw_left_basis(jax.random.fold_in(arg_keys[9], 71), 0),
        "right_basis": draw_right_basis(jax.random.fold_in(arg_keys[9], 71), 0),
        "block_order": draw_block_order(jax.random.fold_in(arg_keys[9], 71), 0),
        "refresh_ids": draw_refresh_ids(jax.random.fold_in(arg_keys[9], 71), 0),
    }


highest = lax.Precision.HIGHEST

def orthonormal(product):
    gram = jnp.dot(product.T, product, precision=highest)
    lower = jnp.linalg.cholesky(gram)
    return jax.scipy.linalg.solve_triangular(lower, product.T, lower=True).T

def soap_block(items):
    gradient, first, second, left_fac, right_fac, left_old, right_old, refresh_flag = items
    left_new = 0.95 * left_fac + 0.05 * jnp.dot(gradient, gradient.T, precision=highest) / B
    right_new = 0.95 * right_fac + 0.05 * jnp.dot(gradient.T, gradient, precision=highest) / B
    left_q = lax.cond(refresh_flag, lambda: orthonormal(jnp.dot(left_new, left_old, precision=highest)), lambda: left_old)
    right_q = lax.cond(refresh_flag, lambda: orthonormal(jnp.dot(right_new, right_old, precision=highest)), lambda: right_old)
    moment_next = 0.9 * first + 0.1 * gradient
    rot_grad = jnp.dot(jnp.dot(left_q.T, gradient, precision=highest), right_q, precision=highest)
    rot_moment = jnp.dot(jnp.dot(left_q.T, moment_next, precision=highest), right_q, precision=highest)
    second_next = 0.95 * second + 0.05 * rot_grad * rot_grad
    scaled = rot_moment / (jnp.sqrt(second_next) + 1e-08)
    back = jnp.dot(jnp.dot(left_q, scaled, precision=highest), right_q.T, precision=highest)
    return (back.astype(jnp.bfloat16), left_new, right_new)

def reference(grad_parts, moment, second_moment, left_factor, right_factor, left_basis, right_basis, block_order, refresh_ids):
    grad = lax.optimization_barrier(jnp.sum(grad_parts, axis=0, dtype=jnp.float32))
    slot_grad = jnp.take(grad, block_order, axis=0)
    refresh_flags = jnp.any(block_order[:, None] == refresh_ids[None, :], axis=1)
    slot_update, left_new, right_new = lax.map(soap_block, (slot_grad, moment, second_moment, left_factor, right_factor, left_basis, right_basis, refresh_flags))
    step_dir = jnp.zeros_like(slot_update).at[block_order].set(slot_update)
    return (step_dir, left_new, right_new)
```

```python
import jax
import jax.numpy as jnp
from jax import lax
from jax.sharding import PartitionSpec as P

highest = lax.Precision.HIGHEST
high = lax.Precision.HIGH


def orthonormal(product):
    gram = jnp.dot(product.T, product, precision=highest)
    lower = jnp.linalg.cholesky(gram)
    return jax.scipy.linalg.solve_triangular(lower, product.T, lower=True).T


def refresh_bases(factor, basis, refresh_flags):

    def single(items):
        factor_one, basis_one, flag_one = items
        return lax.cond(
            flag_one,
            lambda: orthonormal(jnp.dot(factor_one, basis_one, precision=highest)),
            lambda: basis_one,
        )

    return lax.map(single, (factor, basis, refresh_flags))


def soap_update(gradient, moment, second_moment, left_q, right_q):
    moment_next = 0.9 * moment + 0.1 * gradient
    rot_grad = jnp.einsum(
        "kil,klm->kim",
        jnp.einsum("kji,kjl->kil", left_q, gradient, precision=high),
        right_q,
        precision=high,
    )
    rot_moment = jnp.einsum(
        "kil,klm->kim",
        jnp.einsum("kji,kjl->kil", left_q, moment_next, precision=high),
        right_q,
        precision=high,
    )
    second_next = 0.95 * second_moment + 0.05 * rot_grad * rot_grad
    scaled = rot_moment / (jnp.sqrt(second_next) + 1e-08)
    back = jnp.einsum("kil,klm->kim", left_q, scaled, precision=high)
    return jnp.einsum("kim,knm->kin", back, right_q, precision=high)


def on_device(
    grad_parts,
    moment,
    second_moment,
    left_factor,
    right_factor,
    left_basis,
    right_basis,
    block_order,
    refresh_ids,
):
    replicas = lax.axis_size("replica")
    replica_at = lax.axis_index("replica")
    owner_at = lax.axis_index("fsdp")
    total_blocks = grad_parts.shape[1]
    group_size = total_blocks // replicas
    per_owner = moment.shape[0]
    block_width = moment.shape[2]
    group_start = replica_at * group_size
    local_order = lax.dynamic_slice_in_dim(block_order, group_start, group_size) - group_start
    summed = lax.psum_scatter(grad_parts[0], "replica", scatter_dimension=0, tiled=True)
    arranged = jnp.take(summed, local_order, axis=0)
    gradient = lax.all_to_all(arranged, "fsdp", split_axis=0, concat_axis=1, tiled=True).astype(
        jnp.float32
    )
    slot_blocks = lax.dynamic_slice_in_dim(
        block_order, group_start + owner_at * per_owner, per_owner
    )
    own_flags = jnp.any(slot_blocks[:, None] == refresh_ids[None, :], axis=1)
    left_new = (
        0.95 * left_factor
        + 0.05 * jnp.einsum("kij,klj->kil", gradient, gradient, precision=high) / block_width
    )
    right_new = (
        0.95 * right_factor
        + 0.05 * jnp.einsum("kji,kjl->kil", gradient, gradient, precision=high) / block_width
    )
    left_next = refresh_bases(left_new, left_basis, own_flags)
    right_next = refresh_bases(right_new, right_basis, own_flags)
    update = soap_update(gradient, moment, second_moment, left_next, right_next).astype(
        jnp.bfloat16
    )
    returned = lax.all_to_all(update, "fsdp", split_axis=1, concat_axis=0, tiled=True)
    positions = (
        jnp.zeros((group_size,), jnp.int32)
        .at[local_order]
        .set(jnp.arange(group_size, dtype=jnp.int32))
    )
    return (jnp.take(returned, positions, axis=0), left_new, right_new)


def solution(mesh):
    placed = (
        P("replica", None, "fsdp", None),
        P(("replica", "fsdp"), None, None),
        P(("replica", "fsdp"), None, None),
        P(("replica", "fsdp"), None, None),
        P(("replica", "fsdp"), None, None),
        P(("replica", "fsdp"), None, None),
        P(("replica", "fsdp"), None, None),
        P(),
        P(),
    )
    return jax.shard_map(
        on_device,
        mesh=mesh,
        in_specs=placed,
        out_specs=(
            P("replica", "fsdp", None),
            P(("replica", "fsdp"), None, None),
            P(("replica", "fsdp"), None, None),
        ),
        check_vma=False,
    )
```

```python
import jax
import jax.numpy as jnp
from jax import lax
from jax.experimental import pallas as pl
from jax.experimental.pallas import tpu as pltpu
from jax.sharding import PartitionSpec as P

F32 = jnp.float32
BF16 = jnp.bfloat16
NN = (((1,), (0,)), ((), ()))
NT = (((1,), (1,)), ((), ()))
VMEM_LIMIT = 40 * 1024 * 1024

START_BOUND = 0.5
ROUGH_BOUND = 0.5
FINE_BOUND = 0.016


def dot(a, b, form=NN):
    return lax.dot_general(a, b, form, preferred_element_type=F32)


def split(x):
    hi = x.astype(BF16)
    return hi, (x - hi.astype(F32)).astype(BF16)


def store_split(hi_ref, lo_ref, x):
    hi, lo = split(x)
    hi_ref[...] = hi
    lo_ref[...] = lo


def halves(width):
    half = width // 2
    return ((slice(half, width), width), (slice(0, half), half))


def lower_step(gram, first_row):
    rows = lax.broadcasted_iota(jnp.int32, gram.shape, 0) + first_row
    cols = lax.broadcasted_iota(jnp.int32, gram.shape, 1)
    return jnp.where(rows > cols, gram, jnp.where(rows == cols, 0.5 * gram - 0.5, 0.0))


def triangle(hi_ref, lo_ref, step_ref):
    width = hi_ref.shape[0]
    total = 0.0
    for rows, reach in halves(width):
        gram = dot(hi_ref[rows, :], hi_ref[:reach, :], NT)
        if lo_ref is not None:
            gram += dot(hi_ref[rows, :], lo_ref[:reach, :], NT)
            gram += dot(lo_ref[rows, :], hi_ref[:reach, :], NT)
        step = lower_step(gram, rows.start)
        total += jnp.sum(step * step)
        step_ref[rows, :reach] = step.astype(BF16)
    return total


def apply_step(q_ref, hi_ref, lo_ref, step_ref, low_part):
    for rows, reach in halves(q_ref.shape[0]):
        change = dot(step_ref[rows, :reach], hi_ref[:reach, :])
        if low_part:
            change += dot(step_ref[rows, :reach], lo_ref[:reach, :])
        q_new = q_ref[rows, :] - change
        q_ref[rows, :] = q_new
        hi, lo = split(q_new)
        hi_ref[rows, :] = hi
        if lo_ref is not None:
            lo_ref[rows, :] = lo


def prepare_kernel(flag_ref, lf_ref, rf_ref, lb_ref, rb_ref,
                   lw_ref, lq_ref, rw_ref, rq_ref,
                   q2, h2, s2, t2, th2):

    @pl.when(flag_ref[0] != 0)
    def _():
        width = lf_ref.shape[0]
        eye = (
            lax.broadcasted_iota(jnp.int32, (width, width), 0)
            == lax.broadcasted_iota(jnp.int32, (width, width), 1)
        )
        for side, (factor, basis) in enumerate(((lf_ref, lb_ref), (rf_ref, rb_ref))):
            p = dot(factor[...].astype(BF16), basis[...].astype(BF16))
            scale = lax.rsqrt(jnp.sum(p * p, axis=0, keepdims=True))
            y = (p * scale).astype(BF16)
            h2[side] = y.T
            gram = dot(h2[side], h2[side], NT)
            reach = jnp.max(jnp.sum(jnp.abs(gram), axis=0, keepdims=True), axis=1, keepdims=True)
            factor_all = lax.rsqrt(0.5 * reach)
            start = h2[side].astype(F32) * factor_all
            q2[side] = start
            h2[side] = start.astype(BF16)
            diagonal = jnp.where(eye, scale * (factor_all / 0.95), 0.0)
            t2[side] = diagonal
            th2[side] = diagonal.astype(BF16)

        def body(carry):
            count, _ = carry
            worst = 0.0
            for side in range(2):
                total = triangle(h2.at[side], None, s2.at[side])
                worst = jnp.maximum(worst, total)
            for side in range(2):
                apply_step(q2.at[side], h2.at[side], None, s2.at[side], False)
                apply_step(t2.at[side], th2.at[side], None, s2.at[side], False)
            return count + 1, worst

        lax.while_loop(
            lambda carry: (carry[0] < 24) & (carry[1] > START_BOUND),
            body,
            (jnp.int32(0), jnp.float32(1e30)),
        )
        for side, (factor, basis, w_ref, q_ref) in enumerate(
            ((lf_ref, lb_ref, lw_ref, lq_ref), (rf_ref, rb_ref, rw_ref, rq_ref))
        ):
            basis_hi, basis_lo = split(basis[...].T)
            w = dot(th2[side], basis_hi) + dot(th2[side], basis_lo)
            w_hi, w_lo = split(w)
            factor_hi, factor_lo = split(factor[...])
            w_ref[...] = w_hi
            q_ref[...] = 0.95 * (
                dot(w_hi, factor_hi, NT) + dot(w_hi, factor_lo, NT) + dot(w_lo, factor_hi, NT)
            )


def gram_schmidt(q_ref, hi_ref, lo_ref):
    width = q_ref.shape[0]
    rows = lax.broadcasted_iota(jnp.int32, (width, 1), 0)

    def one(at, carry):
        row = q_ref[pl.ds(at, 1), :]
        row = row * lax.rsqrt(jnp.sum(row * row))
        q = q_ref[...]
        share = jnp.sum(q * row, axis=1, keepdims=True)
        q_ref[...] = q - jnp.where(rows > at, share, 0.0) * row
        q_ref[pl.ds(at, 1), :] = row
        return carry

    lax.fori_loop(0, width, one, 0)
    store_split(hi_ref, lo_ref, q_ref[...])


def update_kernel(flag_ref, grad_ref, moment_ref, second_ref, lf_ref, rf_ref, lb_ref, rb_ref,
                  lw_ref, lq_ref, rw_ref, rq_ref,
                  update_ref, left_ref, right_ref,
                  q2, h2, l2, s2):
    width = grad_ref.shape[0]
    weight = 0.05 / width
    grad = grad_ref[...]
    grad_t = grad.T
    left_ref[...] = 0.95 * lf_ref[...] + weight * dot(grad, grad, NT)
    right_ref[...] = 0.95 * rf_ref[...] + weight * dot(grad_t, grad_t, NT)

    @pl.when(flag_ref[0] == 0)
    def _():
        store_split(h2.at[0], l2.at[0], lb_ref[...].T)
        store_split(h2.at[1], l2.at[1], rb_ref[...].T)

    @pl.when(flag_ref[0] != 0)
    def _():
        part = dot(lw_ref[...], grad).astype(BF16)
        q_left = lq_ref[...] + weight * dot(part, grad, NT)
        part = dot(rw_ref[...], grad, NT).astype(BF16)
        q_right = rq_ref[...] + weight * dot(part, grad)
        q2[0] = q_left
        store_split(h2.at[0], l2.at[0], q_left)
        q2[1] = q_right
        store_split(h2.at[1], l2.at[1], q_right)

        def rough(carry):
            count, _ = carry
            worst = 0.0
            for side in range(2):
                worst = jnp.maximum(worst, triangle(h2.at[side], None, s2.at[side]))
            for side in range(2):
                apply_step(q2.at[side], h2.at[side], l2.at[side], s2.at[side], True)
            return count + 1, worst

        def fine(carry):
            count, _ = carry
            worst = 0.0
            for side in range(2):
                worst = jnp.maximum(worst, triangle(h2.at[side], l2.at[side], s2.at[side]))
            for side in range(2):
                apply_step(q2.at[side], h2.at[side], l2.at[side], s2.at[side], False)
            return count + 1, worst

        start = (jnp.int32(0), jnp.float32(1e30))
        lax.while_loop(lambda carry: (carry[0] < 16) & (carry[1] > ROUGH_BOUND), rough, start)
        _, worst = lax.while_loop(
            lambda carry: (carry[0] < 5) & (carry[1] > FINE_BOUND), fine, start
        )

        @pl.when(jnp.logical_not(worst <= FINE_BOUND))
        def _():
            for side, (new_ref, basis) in enumerate(((left_ref, lb_ref), (right_ref, rb_ref))):
                q2[side] = lax.dot_general(
                    new_ref[...], basis[...], NN,
                    precision=lax.Precision.HIGHEST, preferred_element_type=F32,
                ).T
                gram_schmidt(q2.at[side], h2.at[side], l2.at[side])

    left_hi = h2[0]
    left_lo = l2[0]
    right_hi = h2[1]
    right_lo = l2[1]
    rotated = dot(dot(left_hi, grad).astype(BF16), right_hi, NT)
    moment_hi, moment_lo = split(0.9 * moment_ref[...] + 0.1 * grad.astype(F32))
    part = dot(left_hi, moment_hi) + dot(left_lo, moment_hi) + dot(left_hi, moment_lo)
    part_hi, part_lo = split(part)
    moment = (
        dot(part_hi, right_hi, NT) + dot(part_hi, right_lo, NT) + dot(part_lo, right_hi, NT)
    )
    second = 0.95 * second_ref[...] + 0.05 * rotated * rotated
    scaled_hi, scaled_lo = split(moment / (jnp.sqrt(second) + 1e-8))
    left_hi = left_hi.T
    left_lo = left_lo.T
    part = dot(left_hi, scaled_hi) + dot(left_lo, scaled_hi) + dot(left_hi, scaled_lo)
    part_hi, part_lo = split(part)
    update_ref[...] = (
        dot(part_hi, right_hi) + dot(part_hi, right_lo) + dot(part_lo, right_hi)
    ).astype(BF16)


SMEM_SPEC = pl.BlockSpec(memory_space=pltpu.SMEM)
VMEM_SPEC = pl.BlockSpec(memory_space=pltpu.VMEM)


def prepare(flag, left_factor, right_factor, left_basis, right_basis):
    width = left_factor.shape[0]
    square = (width, width)
    return pl.pallas_call(
        prepare_kernel,
        out_shape=[
            jax.ShapeDtypeStruct(square, BF16),
            jax.ShapeDtypeStruct(square, F32),
            jax.ShapeDtypeStruct(square, BF16),
            jax.ShapeDtypeStruct(square, F32),
        ],
        in_specs=[SMEM_SPEC] + [VMEM_SPEC] * 4,
        out_specs=[VMEM_SPEC] * 4,
        scratch_shapes=[
            pltpu.VMEM((2,) + square, F32),
            pltpu.VMEM((2,) + square, BF16),
            pltpu.VMEM((2,) + square, BF16),
            pltpu.VMEM((2,) + square, F32),
            pltpu.VMEM((2,) + square, BF16),
        ],
        compiler_params=pltpu.CompilerParams(vmem_limit_bytes=VMEM_LIMIT),
        cost_estimate=pl.CostEstimate(
            flops=120 * width**3, bytes_accessed=28 * width**2, transcendentals=0
        ),
        name="prepare",
    )(flag, left_factor, right_factor, left_basis, right_basis)


def update_slot(flag, gradient, *arrays):
    width = gradient.shape[0]
    square = (width, width)
    return pl.pallas_call(
        update_kernel,
        out_shape=[
            jax.ShapeDtypeStruct(square, BF16),
            jax.ShapeDtypeStruct(square, F32),
            jax.ShapeDtypeStruct(square, F32),
        ],
        in_specs=[SMEM_SPEC] + [VMEM_SPEC] * 11,
        out_specs=[VMEM_SPEC] * 3,
        scratch_shapes=[
            pltpu.VMEM((2,) + square, F32),
            pltpu.VMEM((2,) + square, BF16),
            pltpu.VMEM((2,) + square, BF16),
            pltpu.VMEM((2,) + square, BF16),
        ],
        compiler_params=pltpu.CompilerParams(vmem_limit_bytes=VMEM_LIMIT),
        cost_estimate=pl.CostEstimate(
            flops=100 * width**3, bytes_accessed=50 * width**2, transcendentals=width**2
        ),
        name="update",
    )(flag, gradient, *arrays)


def on_device(
    grad_parts,
    moment,
    second_moment,
    left_factor,
    right_factor,
    left_basis,
    right_basis,
    block_order,
    refresh_ids,
):
    replicas = lax.axis_size("replica")
    replica_at = lax.axis_index("replica")
    owner_at = lax.axis_index("fsdp")
    group_size = grad_parts.shape[1] // replicas
    group_start = replica_at * group_size
    local_order = lax.dynamic_slice_in_dim(block_order, group_start, group_size) - group_start
    own_block = lax.dynamic_slice_in_dim(block_order, group_start + owner_at, 1)
    flag = jnp.any(own_block == refresh_ids).astype(jnp.int32).reshape(1)
    summed = lax.psum_scatter(grad_parts[0], "replica", scatter_dimension=0, tiled=True)
    prepared = prepare(flag, left_factor[0], right_factor[0], left_basis[0], right_basis[0])
    arranged = jnp.take(summed, local_order, axis=0, mode="clip")
    gradient = lax.all_to_all(arranged, "fsdp", split_axis=0, concat_axis=1, tiled=True)[0]
    update, left_new, right_new = update_slot(
        flag,
        gradient,
        moment[0],
        second_moment[0],
        left_factor[0],
        right_factor[0],
        left_basis[0],
        right_basis[0],
        *prepared,
    )
    rows = update.reshape(group_size, -1, update.shape[1])
    returned = lax.all_to_all(rows, "fsdp", split_axis=0, concat_axis=0, tiled=True)
    positions = jnp.argmax(
        local_order[None, :] == jnp.arange(group_size, dtype=jnp.int32)[:, None], axis=1
    )
    return (
        jnp.take(returned, positions, axis=0, mode="clip"),
        left_new[None],
        right_new[None],
    )


def solution(mesh):
    placed = (
        P("replica", None, "fsdp", None),
        P(("replica", "fsdp"), None, None),
        P(("replica", "fsdp"), None, None),
        P(("replica", "fsdp"), None, None),
        P(("replica", "fsdp"), None, None),
        P(("replica", "fsdp"), None, None),
        P(("replica", "fsdp"), None, None),
        P(),
        P(),
    )
    return jax.shard_map(
        on_device,
        mesh=mesh,
        in_specs=placed,
        out_specs=(
            P("replica", "fsdp", None),
            P(("replica", "fsdp"), None, None),
            P(("replica", "fsdp"), None, None),
        ),
        check_vma=False,
    )
```

```python
import jax
import jax.numpy as jnp
from jax import lax
from jax.experimental import pallas as pl
from jax.experimental.pallas import tpu as pltpu
from jax.sharding import PartitionSpec as P

F32 = jnp.float32
BF16 = jnp.bfloat16
NN = (((1,), (0,)), ((), ()))
NT = (((1,), (1,)), ((), ()))
VMEM_LIMIT = 24 * 1024 * 1024

START_BOUND = 0.5
ROUGH_BOUND = 0.5
FINE_BOUND = 0.016

FIRST_STEPS = 4
MORE_STEPS = 5
LAST_STEPS = 16


def dot(a, b, form=NN):
    return lax.dot_general(a, b, form, preferred_element_type=F32)


def split(x):
    hi = x.astype(BF16)
    return hi, (x - hi.astype(F32)).astype(BF16)


def store_split(hi_ref, lo_ref, x):
    hi, lo = split(x)
    hi_ref[...] = hi
    lo_ref[...] = lo


def halves(width):
    half = width // 2
    return ((slice(half, width), width), (slice(0, half), half))


def lower_step(gram, first_row):
    rows = lax.broadcasted_iota(jnp.int32, gram.shape, 0) + first_row
    cols = lax.broadcasted_iota(jnp.int32, gram.shape, 1)
    return jnp.where(rows > cols, gram, jnp.where(rows == cols, 0.5 * gram - 0.5, 0.0))


def triangle(hi_ref, lo_ref, step_ref):
    width = hi_ref.shape[0]
    total = 0.0
    for rows, reach in halves(width):
        gram = dot(hi_ref[rows, :], hi_ref[:reach, :], NT)
        if lo_ref is not None:
            gram += dot(hi_ref[rows, :], lo_ref[:reach, :], NT)
            gram += dot(lo_ref[rows, :], hi_ref[:reach, :], NT)
        step = lower_step(gram, rows.start)
        total += jnp.sum(step * step)
        step_ref[rows, :reach] = step.astype(BF16)
    return total


def apply_step(q_ref, hi_ref, lo_ref, step_ref, low_part):
    for rows, reach in halves(q_ref.shape[0]):
        change = dot(step_ref[rows, :reach], hi_ref[:reach, :])
        if low_part:
            change += dot(step_ref[rows, :reach], lo_ref[:reach, :])
        q_new = q_ref[rows, :] - change
        q_ref[rows, :] = q_new
        hi, lo = split(q_new)
        hi_ref[rows, :] = hi
        if lo_ref is not None:
            lo_ref[rows, :] = lo


def prepare_steps(most, q2, h2, s2, t2, th2):
    def body(carry):
        count, _ = carry
        worst = 0.0
        for side in range(2):
            worst = jnp.maximum(worst, triangle(h2.at[side], None, s2.at[side]))
        for side in range(2):
            apply_step(q2.at[side], h2.at[side], None, s2.at[side], False)
            apply_step(t2.at[side], th2.at[side], None, s2.at[side], False)
        return count + 1, worst

    lax.while_loop(
        lambda carry: (carry[0] < most) & (carry[1] > START_BOUND),
        body,
        (jnp.int32(0), jnp.float32(1e30)),
    )


def prepare_first(flag_ref, lf_ref, rf_ref, lb_ref, rb_ref, h2, th2, q2, t2, s2):

    @pl.when(flag_ref[0] != 0)
    def _():
        width = lf_ref.shape[0]
        eye = (
            lax.broadcasted_iota(jnp.int32, (width, width), 0)
            == lax.broadcasted_iota(jnp.int32, (width, width), 1)
        )
        for side, (factor, basis) in enumerate(((lf_ref, lb_ref), (rf_ref, rb_ref))):
            p = dot(factor[...].astype(BF16), basis[...].astype(BF16))
            scale = lax.rsqrt(jnp.sum(p * p, axis=0, keepdims=True))
            y = (p * scale).astype(BF16)
            h2[side] = y.T
            gram = dot(h2[side], h2[side], NT)
            reach = jnp.max(jnp.sum(jnp.abs(gram), axis=0, keepdims=True), axis=1, keepdims=True)
            factor_all = lax.rsqrt(0.5 * reach)
            start = h2[side].astype(F32) * factor_all
            q2[side] = start
            h2[side] = start.astype(BF16)
            diagonal = jnp.where(eye, scale * (factor_all / 0.95), 0.0)
            t2[side] = diagonal
            th2[side] = diagonal.astype(BF16)
        prepare_steps(FIRST_STEPS, q2, h2, s2, t2, th2)


def prepare_more(flag_ref, h_ref, th_ref, h2, th2, q2, t2, s2):
    @pl.when(flag_ref[0] != 0)
    def _():
        for side in range(2):
            h2[side] = h_ref[side]
            th2[side] = th_ref[side]
            q2[side] = h_ref[side].astype(F32)
            t2[side] = th_ref[side].astype(F32)
        prepare_steps(MORE_STEPS, q2, h2, s2, t2, th2)


def prepare_last(flag_ref, h_ref, th_ref, lf_ref, rf_ref, lb_ref, rb_ref,
                 lw_ref, lq_ref, rw_ref, rq_ref, h2, th2, q2, t2, s2):

    @pl.when(flag_ref[0] != 0)
    def _():
        for side in range(2):
            h2[side] = h_ref[side]
            th2[side] = th_ref[side]
            q2[side] = h_ref[side].astype(F32)
            t2[side] = th_ref[side].astype(F32)
        prepare_steps(LAST_STEPS, q2, h2, s2, t2, th2)
        for side, (factor, basis, w_ref, q_ref) in enumerate(
            ((lf_ref, lb_ref, lw_ref, lq_ref), (rf_ref, rb_ref, rw_ref, rq_ref))
        ):
            basis_hi, basis_lo = split(basis[...].T)
            w = dot(th2[side], basis_hi) + dot(th2[side], basis_lo)
            w_hi, w_lo = split(w)
            factor_hi, factor_lo = split(factor[...])
            w_ref[...] = w_hi
            q_ref[...] = 0.95 * (
                dot(w_hi, factor_hi, NT) + dot(w_hi, factor_lo, NT) + dot(w_lo, factor_hi, NT)
            )


def gram_schmidt(q_ref, hi_ref, lo_ref):
    width = q_ref.shape[0]
    rows = lax.broadcasted_iota(jnp.int32, (width, 1), 0)

    def one(at, carry):
        row = q_ref[pl.ds(at, 1), :]
        row = row * lax.rsqrt(jnp.sum(row * row))
        q = q_ref[...]
        share = jnp.sum(q * row, axis=1, keepdims=True)
        q_ref[...] = q - jnp.where(rows > at, share, 0.0) * row
        q_ref[pl.ds(at, 1), :] = row
        return carry

    lax.fori_loop(0, width, one, 0)
    store_split(hi_ref, lo_ref, q_ref[...])


def finish_kernel(owner_ref, right_ref, left_ref, own_right_ref, own_left_ref, *rest):
    outs, total = rest[:-1], rest[-1]
    half = right_ref.shape[0]
    total[:half] = (right_ref[...].astype(F32) + own_right_ref[...].astype(F32)).astype(BF16)
    total[half:] = (left_ref[...].astype(F32) + own_left_ref[...].astype(F32)).astype(BF16)
    for k, out in enumerate(outs):
        out[...] = total[owner_ref[0] ^ k]


def update_kernel(flag_ref, owner_ref, moment_ref, second_ref, lf_ref, rf_ref, lb_ref, rb_ref,
                  lw_ref, lq_ref, rw_ref, rq_ref, *rest):
    pieces, (update_ref, left_ref, right_ref, q2, h2, l2, s2, grad_ref) = rest[:-8], rest[-8:]
    width = grad_ref.shape[0]
    weight = 0.05 / width
    for k, piece in enumerate(pieces):
        rows = piece.shape[0]
        grad_ref[pl.ds(pl.multiple_of((owner_ref[0] ^ k) * rows, rows), rows), :] = piece[...]
    grad = grad_ref[...]
    grad_t = grad.T
    left_ref[...] = 0.95 * lf_ref[...] + weight * dot(grad, grad, NT)
    right_ref[...] = 0.95 * rf_ref[...] + weight * dot(grad_t, grad_t, NT)

    @pl.when(flag_ref[0] == 0)
    def _():
        store_split(h2.at[0], l2.at[0], lb_ref[...].T)
        store_split(h2.at[1], l2.at[1], rb_ref[...].T)

    @pl.when(flag_ref[0] != 0)
    def _():
        part = dot(lw_ref[...], grad).astype(BF16)
        q_left = lq_ref[...] + weight * dot(part, grad, NT)
        part = dot(rw_ref[...], grad, NT).astype(BF16)
        q_right = rq_ref[...] + weight * dot(part, grad)
        q2[0] = q_left
        store_split(h2.at[0], l2.at[0], q_left)
        q2[1] = q_right
        store_split(h2.at[1], l2.at[1], q_right)

        def rough(carry):
            count, _ = carry
            worst = 0.0
            for side in range(2):
                worst = jnp.maximum(worst, triangle(h2.at[side], None, s2.at[side]))
            for side in range(2):
                apply_step(q2.at[side], h2.at[side], l2.at[side], s2.at[side], True)
            return count + 1, worst

        def fine(carry):
            count, _ = carry
            worst = 0.0
            for side in range(2):
                worst = jnp.maximum(worst, triangle(h2.at[side], l2.at[side], s2.at[side]))
            for side in range(2):
                apply_step(q2.at[side], h2.at[side], l2.at[side], s2.at[side], False)
            return count + 1, worst

        start = (jnp.int32(0), jnp.float32(1e30))
        lax.while_loop(lambda carry: (carry[0] < 16) & (carry[1] > ROUGH_BOUND), rough, start)
        _, worst = lax.while_loop(
            lambda carry: (carry[0] < 5) & (carry[1] > FINE_BOUND), fine, start
        )

        @pl.when(jnp.logical_not(worst <= FINE_BOUND))
        def _():
            for side, (new_ref, basis) in enumerate(((left_ref, lb_ref), (right_ref, rb_ref))):
                q2[side] = lax.dot_general(
                    new_ref[...], basis[...], NN,
                    precision=lax.Precision.HIGHEST, preferred_element_type=F32,
                ).T
                gram_schmidt(q2.at[side], h2.at[side], l2.at[side])

    left_hi = h2[0]
    left_lo = l2[0]
    right_hi = h2[1]
    right_lo = l2[1]
    rotated = dot(dot(left_hi, grad).astype(BF16), right_hi, NT)
    moment_hi, moment_lo = split(0.9 * moment_ref[...] + 0.1 * grad.astype(F32))
    part = dot(left_hi, moment_hi) + dot(left_lo, moment_hi) + dot(left_hi, moment_lo)
    part_hi, part_lo = split(part)
    moment = (
        dot(part_hi, right_hi, NT) + dot(part_hi, right_lo, NT) + dot(part_lo, right_hi, NT)
    )
    second = 0.95 * second_ref[...] + 0.05 * rotated * rotated
    scaled_hi, scaled_lo = split(moment / (jnp.sqrt(second) + 1e-8))
    left_hi = left_hi.T
    left_lo = left_lo.T
    part = dot(left_hi, scaled_hi) + dot(left_lo, scaled_hi) + dot(left_hi, scaled_lo)
    part_hi, part_lo = split(part)
    update_ref[...] = (
        dot(part_hi, right_hi) + dot(part_hi, right_lo) + dot(part_lo, right_hi)
    ).astype(BF16)


SMEM_SPEC = pl.BlockSpec(memory_space=pltpu.SMEM)
VMEM_SPEC = pl.BlockSpec(memory_space=pltpu.VMEM)


def call(kernel, operands, scalars, outs, scratch, flops, name):
    return pl.pallas_call(
        kernel,
        out_shape=[jax.ShapeDtypeStruct(shape, dtype) for shape, dtype in outs],
        in_specs=[SMEM_SPEC] * scalars + [VMEM_SPEC] * (len(operands) - scalars),
        out_specs=[VMEM_SPEC] * len(outs),
        scratch_shapes=[pltpu.VMEM(shape, dtype) for shape, dtype in scratch],
        compiler_params=pltpu.CompilerParams(vmem_limit_bytes=VMEM_LIMIT),
        cost_estimate=pl.CostEstimate(
            flops=flops,
            bytes_accessed=sum(x.size * x.dtype.itemsize for x in operands),
            transcendentals=0,
        ),
        name=name,
    )(*operands)


def on_device(
    grad_parts,
    moment,
    second_moment,
    left_factor,
    right_factor,
    left_basis,
    right_basis,
    block_order,
    refresh_ids,
):
    replicas = lax.axis_size("replica")
    replica_at = lax.axis_index("replica")
    owners = lax.axis_size("fsdp")
    owner_at = lax.axis_index("fsdp")
    group_size = grad_parts.shape[1] // replicas
    half = group_size // 2
    rows = grad_parts.shape[2]
    width = grad_parts.shape[3]
    square = (width, width)
    pair = (2,) + square
    local_order = (
        lax.dynamic_slice_in_dim(block_order, replica_at * group_size, group_size)
        - replica_at * group_size
    )
    own_block = lax.dynamic_slice_in_dim(block_order, replica_at * group_size + owner_at, 1)
    flag = jnp.any(own_block == refresh_ids).astype(jnp.int32).reshape(1)
    owner = owner_at.astype(jnp.int32).reshape(1)
    factors = (left_factor[0], right_factor[0])
    bases = (left_basis[0], right_basis[0])

    def own(group, part):
        ids = lax.dynamic_slice_in_dim(
            block_order, lax.rem(group, replicas) * group_size + part * half, half
        )
        return jnp.take(grad_parts[0], ids, axis=0, mode="clip")

    def stage(at, state):
        flops = 40 * width**3
        work = [(pair, F32), (pair, F32), (pair, BF16)]
        if at == 0:
            return call(
                prepare_first, (flag, *factors, *bases), 1, [(pair, BF16)] * 2, work, flops,
                "prepare_first",
            )
        if at == 1:
            return call(
                prepare_more, (flag, *state), 1, [(pair, BF16)] * 2, work, flops, "prepare_more"
            )
        return call(
            prepare_last, (flag, *state, *factors, *bases), 1,
            [(square, BF16), (square, F32)] * 2, [(pair, BF16)] * 2 + work, flops,
            "prepare_last",
        )

    to_right = [(i, (i + 1) % replicas) for i in range(replicas)]
    to_left = [(i, (i - 1) % replicas) for i in range(replicas)]
    send_right = own(replica_at + replicas - 1, 0)
    send_left = own(replica_at + 1, 1)
    state = None
    stages = 3
    for step in range(replicas - 1):
        got_right = lax.ppermute(send_right, "replica", to_right)
        got_left = lax.ppermute(send_left, "replica", to_left)
        own_right = own(replica_at + 2 * replicas - 2 - step, 0)
        own_left = own(replica_at + 2 + step, 1)
        if step < stages:
            state = stage(step, state)
            own_right, own_left, *state = lax.optimization_barrier((own_right, own_left, *state))
        if step < replicas - 2:
            send_right = (got_right.astype(F32) + own_right.astype(F32)).astype(BF16)
            send_left = (got_left.astype(F32) + own_left.astype(F32)).astype(BF16)
    pieces = call(
        finish_kernel, (owner, got_right, got_left, own_right, own_left), 1,
        [((rows, width), BF16)] * owners, [((group_size, rows, width), BF16)], 0, "finish",
    )
    pieces = [pieces[0]] + [
        lax.ppermute(pieces[k], "fsdp", [(i, i ^ k) for i in range(owners)])
        for k in range(1, owners)
    ]
    update, left_new, right_new = call(
        update_kernel,
        (flag, owner, moment[0], second_moment[0], *factors, *bases, *state, *pieces), 2,
        [(square, BF16), (square, F32), (square, F32)],
        [(pair, F32), (pair, BF16), (pair, BF16), (pair, BF16), (square, BF16)],
        100 * width**3, "update",
    )
    returned = lax.all_to_all(
        update.reshape(owners, rows, width), "fsdp", split_axis=0, concat_axis=0, tiled=True
    )
    positions = jnp.argmax(
        local_order[None, :] == jnp.arange(group_size, dtype=jnp.int32)[:, None], axis=1
    )
    return (
        jnp.take(returned, positions, axis=0, mode="clip"),
        left_new[None],
        right_new[None],
    )


def solution(mesh):
    placed = (
        P("replica", None, "fsdp", None),
        P(("replica", "fsdp"), None, None),
        P(("replica", "fsdp"), None, None),
        P(("replica", "fsdp"), None, None),
        P(("replica", "fsdp"), None, None),
        P(("replica", "fsdp"), None, None),
        P(("replica", "fsdp"), None, None),
        P(),
        P(),
    )
    return jax.shard_map(
        on_device,
        mesh=mesh,
        in_specs=placed,
        out_specs=(
            P("replica", "fsdp", None),
            P(("replica", "fsdp"), None, None),
            P(("replica", "fsdp"), None, None),
        ),
        check_vma=False,
    )
```

```python
import functools

import jax
import jax.numpy as jnp
from jax import lax
from jax.experimental import pallas as pl
from jax.experimental.pallas import tpu as pltpu
from jax.sharding import PartitionSpec as P

F32 = jnp.float32
BF16 = jnp.bfloat16
NN = (((1,), (0,)), ((), ()))
NT = (((1,), (1,)), ((), ()))
VMEM_LIMIT = 24 * 1024 * 1024

START_BOUND = 0.5
ROUGH_BOUND = 0.5
FINE_BOUND = 0.016

FIRST_STEPS = 4
MORE_STEPS = 5
LAST_STEPS = 16


def dot(a, b, form=NN):
    return lax.dot_general(a, b, form, preferred_element_type=F32)


def split(x):
    hi = x.astype(BF16)
    return hi, (x - hi.astype(F32)).astype(BF16)


def store_split(hi_ref, lo_ref, x):
    hi, lo = split(x)
    hi_ref[...] = hi
    lo_ref[...] = lo


def halves(width):
    half = width // 2
    return ((slice(half, width), width), (slice(0, half), half))


def lower_step(gram, first_row):
    rows = lax.broadcasted_iota(jnp.int32, gram.shape, 0) + first_row
    cols = lax.broadcasted_iota(jnp.int32, gram.shape, 1)
    return jnp.where(rows > cols, gram, jnp.where(rows == cols, 0.5 * gram - 0.5, 0.0))


def triangle(hi_ref, lo_ref, step_ref):
    width = hi_ref.shape[0]
    total = 0.0
    for rows, reach in halves(width):
        gram = dot(hi_ref[rows, :], hi_ref[:reach, :], NT)
        if lo_ref is not None:
            gram += dot(hi_ref[rows, :], lo_ref[:reach, :], NT)
            gram += dot(lo_ref[rows, :], hi_ref[:reach, :], NT)
        step = lower_step(gram, rows.start)
        total += jnp.sum(step * step)
        step_ref[rows, :reach] = step.astype(BF16)
    return total


def apply_step(q_ref, hi_ref, lo_ref, step_ref, low_part):
    for rows, reach in halves(q_ref.shape[0]):
        change = dot(step_ref[rows, :reach], hi_ref[:reach, :])
        if low_part:
            change += dot(step_ref[rows, :reach], lo_ref[:reach, :])
        q_new = q_ref[rows, :] - change
        q_ref[rows, :] = q_new
        hi, lo = split(q_new)
        hi_ref[rows, :] = hi
        if lo_ref is not None:
            lo_ref[rows, :] = lo


def prepare_steps(most, q2, h2, s2, t2, th2):
    def body(carry):
        count, _ = carry
        worst = 0.0
        for side in range(2):
            worst = jnp.maximum(worst, triangle(h2.at[side], None, s2.at[side]))
        for side in range(2):
            apply_step(q2.at[side], h2.at[side], None, s2.at[side], False)
            apply_step(t2.at[side], th2.at[side], None, s2.at[side], False)
        return count + 1, worst

    lax.while_loop(
        lambda carry: (carry[0] < most) & (carry[1] > START_BOUND),
        body,
        (jnp.int32(0), jnp.float32(1e30)),
    )


def own_flag(order_ref, refresh_ref):
    owners = lax.axis_size("fsdp")
    block = order_ref[lax.axis_index("replica") * owners + lax.axis_index("fsdp")]
    flag = block == refresh_ref[0]
    for j in range(1, refresh_ref.shape[0]):
        flag |= block == refresh_ref[j]
    return flag


def start_copies(pairs, sems):
    copies = [pltpu.make_async_copy(src, dst, sems.at[i]) for i, (src, dst) in enumerate(pairs)]
    for copy in copies:
        copy.start()
    return copies


def wait_copies(copies):
    for copy in copies:
        copy.wait()


def prepare_first(order_ref, refresh_ref, lf_hbm, rf_hbm, lb_hbm, rb_hbm, h2, th2,
                  q2, t2, s2, f2, b2, sems):

    @pl.when(own_flag(order_ref, refresh_ref))
    def _():
        copies = start_copies(
            [(lf_hbm, f2.at[0]), (lb_hbm, b2.at[0]), (rf_hbm, f2.at[1]), (rb_hbm, b2.at[1])], sems
        )
        width = lf_hbm.shape[0]
        eye = (
            lax.broadcasted_iota(jnp.int32, (width, width), 0)
            == lax.broadcasted_iota(jnp.int32, (width, width), 1)
        )
        wait_copies(copies)
        for side in range(2):
            p = dot(f2[side].astype(BF16), b2[side].astype(BF16))
            scale = lax.rsqrt(jnp.sum(p * p, axis=0, keepdims=True))
            y = (p * scale).astype(BF16)
            h2[side] = y.T
            gram = dot(h2[side], h2[side], NT)
            reach = jnp.max(jnp.sum(jnp.abs(gram), axis=0, keepdims=True), axis=1, keepdims=True)
            factor_all = lax.rsqrt(0.5 * reach)
            start = h2[side].astype(F32) * factor_all
            q2[side] = start
            h2[side] = start.astype(BF16)
            diagonal = jnp.where(eye, scale * (factor_all / 0.95), 0.0)
            t2[side] = diagonal
            th2[side] = diagonal.astype(BF16)
        prepare_steps(FIRST_STEPS, q2, h2, s2, t2, th2)


def prepare_more(order_ref, refresh_ref, h_ref, th_ref, h2, th2, q2, t2, s2):
    @pl.when(own_flag(order_ref, refresh_ref))
    def _():
        for side in range(2):
            h2[side] = h_ref[side]
            th2[side] = th_ref[side]
            q2[side] = h_ref[side].astype(F32)
            t2[side] = th_ref[side].astype(F32)
        prepare_steps(MORE_STEPS, q2, h2, s2, t2, th2)


def prepare_last(order_ref, refresh_ref, h_ref, th_ref, lf_hbm, rf_hbm, lb_hbm, rb_hbm,
                 w2, q_out, h2, th2, q2, t2, s2, f2, b2, sems):

    @pl.when(own_flag(order_ref, refresh_ref))
    def _():
        copies = start_copies(
            [(lf_hbm, f2.at[0]), (lb_hbm, b2.at[0]), (rf_hbm, f2.at[1]), (rb_hbm, b2.at[1])], sems
        )
        for side in range(2):
            h2[side] = h_ref[side]
            th2[side] = th_ref[side]
            q2[side] = h_ref[side].astype(F32)
            t2[side] = th_ref[side].astype(F32)
        prepare_steps(LAST_STEPS, q2, h2, s2, t2, th2)
        wait_copies(copies)
        for side in range(2):
            basis_hi, basis_lo = split(b2[side].T)
            w = dot(th2[side], basis_hi) + dot(th2[side], basis_lo)
            w_hi, w_lo = split(w)
            factor_hi, factor_lo = split(f2[side])
            w2[side] = w_hi
            q_out[side] = 0.95 * (
                dot(w_hi, factor_hi, NT) + dot(w_hi, factor_lo, NT) + dot(w_lo, factor_hi, NT)
            )


def gram_schmidt(q_ref, hi_ref, lo_ref):
    width = q_ref.shape[0]
    rows = lax.broadcasted_iota(jnp.int32, (width, 1), 0)

    def one(at, carry):
        row = q_ref[pl.ds(at, 1), :]
        row = row * lax.rsqrt(jnp.sum(row * row))
        q = q_ref[...]
        share = jnp.sum(q * row, axis=1, keepdims=True)
        q_ref[...] = q - jnp.where(rows > at, share, 0.0) * row
        q_ref[pl.ds(at, 1), :] = row
        return carry

    lax.fori_loop(0, width, one, 0)
    store_split(hi_ref, lo_ref, q_ref[...])


def gather_kernel(steps, order_ref, parts_hbm, *rest):
    outs, sems = rest[:-1], rest[-1]
    replicas = lax.axis_size("replica")
    at = lax.axis_index("replica")
    half = outs[0].shape[0]
    pairs = []
    for number, step in enumerate(steps):
        for part in range(2):
            ahead = (2 * replicas - 1 - step) if part == 0 else (1 + step)
            first = lax.rem(at + ahead, replicas) * (2 * half) + part * half
            for i in range(half):
                pairs.append((parts_hbm.at[order_ref[first + i]], outs[2 * number + part].at[i]))
    wait_copies(start_copies(pairs, sems))


def add_kernel(got_ref, own_ref, out_ref):
    out_ref[...] = (got_ref[...].astype(F32) + own_ref[...].astype(F32)).astype(BF16)


def finish_kernel(got_right_ref, got_left_ref, own_right_ref, own_left_ref, out_ref):
    half = got_right_ref.shape[0]
    add_kernel(got_right_ref, own_right_ref, out_ref.at[:half])
    add_kernel(got_left_ref, own_left_ref, out_ref.at[half:])


def update_kernel(order_ref, refresh_ref, grad_ref, w_ref, q_ref, lf_hbm, rf_hbm, lb_hbm, rb_hbm,
                  moment_hbm, second_hbm, update_ref, left_hbm, right_hbm,
                  q2, h2, l2, s2, f2, b2, moment_ref, second_ref, new2, sems, out_sems):
    flag = own_flag(order_ref, refresh_ref)
    copies = start_copies(
        [(lf_hbm, f2.at[0]), (rf_hbm, f2.at[1]), (lb_hbm, b2.at[0]), (rb_hbm, b2.at[1]),
         (moment_hbm, moment_ref), (second_hbm, second_ref)],
        sems,
    )
    width = grad_ref.shape[0]
    weight = 0.05 / width
    grad = grad_ref[...]
    grad_t = grad.T
    left_gram = dot(grad, grad, NT)
    right_gram = dot(grad_t, grad_t, NT)
    wait_copies(copies)
    new2[0] = 0.95 * f2[0] + weight * left_gram
    new2[1] = 0.95 * f2[1] + weight * right_gram
    out_copies = start_copies([(new2.at[0], left_hbm), (new2.at[1], right_hbm)], out_sems)

    @pl.when(jnp.logical_not(flag))
    def _():
        store_split(h2.at[0], l2.at[0], b2[0].T)
        store_split(h2.at[1], l2.at[1], b2[1].T)

    @pl.when(flag)
    def _():
        part = dot(w_ref[0], grad).astype(BF16)
        q_left = q_ref[0] + weight * dot(part, grad, NT)
        part = dot(w_ref[1], grad, NT).astype(BF16)
        q_right = q_ref[1] + weight * dot(part, grad)
        q2[0] = q_left
        store_split(h2.at[0], l2.at[0], q_left)
        q2[1] = q_right
        store_split(h2.at[1], l2.at[1], q_right)

        def rough(carry):
            count, _ = carry
            worst = 0.0
            for side in range(2):
                worst = jnp.maximum(worst, triangle(h2.at[side], None, s2.at[side]))
            for side in range(2):
                apply_step(q2.at[side], h2.at[side], l2.at[side], s2.at[side], False)
            return count + 1, worst

        def fine(carry):
            count, _ = carry
            worst = 0.0
            for side in range(2):
                worst = jnp.maximum(worst, triangle(h2.at[side], l2.at[side], s2.at[side]))
            for side in range(2):
                apply_step(q2.at[side], h2.at[side], l2.at[side], s2.at[side], False)
            return count + 1, worst

        start = (jnp.int32(0), jnp.float32(1e30))
        lax.while_loop(lambda carry: (carry[0] < 16) & (carry[1] > ROUGH_BOUND), rough, start)
        _, worst = lax.while_loop(
            lambda carry: (carry[0] < 5) & (carry[1] > FINE_BOUND), fine, start
        )

        @pl.when(jnp.logical_not(worst <= FINE_BOUND))
        def _():
            for side in range(2):
                q2[side] = lax.dot_general(
                    new2[side], b2[side], NN,
                    precision=lax.Precision.HIGHEST, preferred_element_type=F32,
                ).T
                gram_schmidt(q2.at[side], h2.at[side], l2.at[side])

    left_hi = h2[0]
    left_lo = l2[0]
    right_hi = h2[1]
    right_lo = l2[1]
    rotated = dot(dot(left_hi, grad).astype(BF16), right_hi, NT)
    moment_hi, moment_lo = split(0.9 * moment_ref[...] + 0.1 * grad.astype(F32))
    part = dot(left_hi, moment_hi) + dot(left_lo, moment_hi) + dot(left_hi, moment_lo)
    part_hi, part_lo = split(part)
    moment = (
        dot(part_hi, right_hi, NT) + dot(part_hi, right_lo, NT) + dot(part_lo, right_hi, NT)
    )
    second = 0.95 * second_ref[...] + 0.05 * rotated * rotated
    scaled_hi, scaled_lo = split(moment / (jnp.sqrt(second) + 1e-8))
    left_hi = left_hi.T
    left_lo = left_lo.T
    part = dot(left_hi, scaled_hi) + dot(left_lo, scaled_hi) + dot(left_hi, scaled_lo)
    part_hi, part_lo = split(part)
    update_ref[...] = (
        dot(part_hi, right_hi) + dot(part_hi, right_lo) + dot(part_lo, right_hi)
    ).astype(BF16)
    wait_copies(out_copies)


SMEM_SPEC = pl.BlockSpec(memory_space=pltpu.SMEM)
VMEM_SPEC = pl.BlockSpec(memory_space=pltpu.VMEM)
HBM_SPEC = pl.BlockSpec(memory_space=pltpu.HBM)


def call(kernel, name, in_smem, in_vmem, in_hbm, out_vmem, out_hbm=(), scratch=(), sems=(), flops=0):
    operands = (*in_smem, *in_vmem, *in_hbm)
    return pl.pallas_call(
        kernel,
        out_shape=[jax.ShapeDtypeStruct(shape, dtype) for shape, dtype in (*out_vmem, *out_hbm)],
        in_specs=[SMEM_SPEC] * len(in_smem) + [VMEM_SPEC] * len(in_vmem) + [HBM_SPEC] * len(in_hbm),
        out_specs=[VMEM_SPEC] * len(out_vmem) + [HBM_SPEC] * len(out_hbm),
        scratch_shapes=[pltpu.VMEM(shape, dtype) for shape, dtype in scratch]
        + [pltpu.SemaphoreType.DMA((count,)) for count in sems],
        compiler_params=pltpu.CompilerParams(vmem_limit_bytes=VMEM_LIMIT),
        cost_estimate=pl.CostEstimate(
            flops=flops,
            bytes_accessed=sum(x.size * x.dtype.itemsize for x in in_vmem),
            transcendentals=0,
        ),
        name=name,
    )(*operands)


def on_device(
    grad_parts,
    moment,
    second_moment,
    left_factor,
    right_factor,
    left_basis,
    right_basis,
    block_order,
    refresh_ids,
):
    replicas = lax.axis_size("replica")
    replica_at = lax.axis_index("replica")
    owners = lax.axis_size("fsdp")
    group_size = grad_parts.shape[1] // replicas
    half = group_size // 2
    rows = grad_parts.shape[2]
    width = grad_parts.shape[3]
    square = (width, width)
    pair = (2,) + square
    work = [(pair, F32), (pair, F32), (pair, BF16)]
    loads = [(pair, F32), (pair, F32)]
    slots = (block_order, refresh_ids)
    state_arrays = (left_factor[0], right_factor[0], left_basis[0], right_basis[0])
    steps = replicas - 1

    def gather(name, at_steps):
        return call(
            functools.partial(gather_kernel, at_steps), name, (block_order,), (), (grad_parts[0],),
            [((half, rows, width), BF16)] * (2 * len(at_steps)),
            sems=[2 * half * len(at_steps)],
        )

    def stage(at, tied, state):
        flops = 40 * width**3
        if at == 0:
            return call(
                prepare_first, "prepare_first", (tied, refresh_ids), (), state_arrays,
                [(pair, BF16)] * 2, scratch=work + loads, sems=[4], flops=flops,
            )
        if at == 1:
            return call(
                prepare_more, "prepare_more", (tied, refresh_ids), state, (),
                [(pair, BF16)] * 2, scratch=work, flops=flops,
            )
        return call(
            prepare_last, "prepare_last", (tied, refresh_ids), state, state_arrays,
            [(pair, BF16), (pair, F32)], scratch=[(pair, BF16)] * 2 + work + loads, sems=[4],
            flops=flops,
        )

    to_right = [(i, (i + 1) % replicas) for i in range(replicas)]
    to_left = [(i, (i - 1) % replicas) for i in range(replicas)]
    send_right, send_left = gather("gather_first", (0,))
    own = gather("gather_rest", tuple(range(1, replicas)))
    state = None
    for step in range(steps):
        own_right, own_left = own[2 * step], own[2 * step + 1]
        if step < 3:
            tied, send_right, send_left = lax.optimization_barrier(
                (block_order, send_right, send_left)
            )
        got_right = lax.ppermute(send_right, "replica", to_right)
        got_left = lax.ppermute(send_left, "replica", to_left)
        if step < 3:
            state = stage(step, tied, state)
            own_right, own_left, *state = lax.optimization_barrier((own_right, own_left, *state))
        if step < steps - 1:
            chunk = [((half, rows, width), BF16)]
            (send_right,) = call(add_kernel, "add_right", (), (got_right, own_right), (), chunk)
            (send_left,) = call(add_kernel, "add_left", (), (got_left, own_left), (), chunk)
    (summed,) = call(
        finish_kernel, "finish", (), (got_right, got_left, own_right, own_left), (),
        [((group_size, rows, width), BF16)],
    )
    gradient = lax.all_to_all(summed, "fsdp", split_axis=0, concat_axis=0, tiled=True)
    update, left_new, right_new = call(
        update_kernel, "update", slots, (gradient.reshape(square), *state),
        (*state_arrays, moment[0], second_moment[0]), [(square, BF16)], [(square, F32)] * 2,
        scratch=[(pair, F32), (pair, BF16), (pair, BF16), (pair, BF16), *loads,
                 (square, F32), (square, F32), (pair, F32)],
        sems=[6, 2], flops=100 * width**3,
    )
    returned = lax.all_to_all(
        update.reshape(owners, rows, width), "fsdp", split_axis=0, concat_axis=0, tiled=True
    )
    local_order = (
        lax.dynamic_slice_in_dim(block_order, replica_at * group_size, group_size)
        - replica_at * group_size
    )
    positions = jnp.argmax(
        local_order[None, :] == jnp.arange(group_size, dtype=jnp.int32)[:, None], axis=1
    )
    return (
        jnp.take(returned, positions, axis=0, mode="clip"),
        left_new[None],
        right_new[None],
    )


def solution(mesh):
    placed = (
        P("replica", None, "fsdp", None),
        P(("replica", "fsdp"), None, None),
        P(("replica", "fsdp"), None, None),
        P(("replica", "fsdp"), None, None),
        P(("replica", "fsdp"), None, None),
        P(("replica", "fsdp"), None, None),
        P(("replica", "fsdp"), None, None),
        P(),
        P(),
    )
    return jax.shard_map(
        on_device,
        mesh=mesh,
        in_specs=placed,
        out_specs=(
            P("replica", "fsdp", None),
            P(("replica", "fsdp"), None, None),
            P(("replica", "fsdp"), None, None),
        ),
        check_vma=False,
    )
```

```python
import functools

import jax
import jax.numpy as jnp
from jax import lax
from jax.experimental import pallas as pl
from jax.experimental.pallas import tpu as pltpu
from jax.sharding import PartitionSpec as P

F32 = jnp.float32
BF16 = jnp.bfloat16
NN = (((1,), (0,)), ((), ()))
NT = (((1,), (1,)), ((), ()))
VMEM_LIMIT = 24 * 1024 * 1024
VMEM_MOST = 56 * 1024 * 1024

START_BOUND = 4.0
END_BOUND = 0.016

FIRST_STEPS = 4
MORE_STEPS = 5
LAST_STEPS = 16


def dot(a, b, form=NN):
    return lax.dot_general(a, b, form, preferred_element_type=F32)


def split(x):
    hi = x.astype(BF16)
    return hi, (x - hi.astype(F32)).astype(BF16)


def store_split(hi_ref, lo_ref, x):
    hi, lo = split(x)
    hi_ref[...] = hi
    lo_ref[...] = lo


def halves(width):
    half = width // 2
    return ((slice(half, width), width), (slice(0, half), half))


def lower_step(gram, first_row):
    rows = lax.broadcasted_iota(jnp.int32, gram.shape, 0) + first_row
    cols = lax.broadcasted_iota(jnp.int32, gram.shape, 1)
    return jnp.where(rows > cols, gram, jnp.where(rows == cols, 0.5 * gram - 0.5, 0.0))


def triangle(hi_ref, step_ref):
    total = 0.0
    for rows, reach in halves(hi_ref.shape[0]):
        step = lower_step(dot(hi_ref[rows, :], hi_ref[:reach, :], NT), rows.start)
        total += jnp.sum(step * step)
        step_ref[rows, :reach] = step.astype(BF16)
    return total


def apply_step(q_ref, hi_ref, lo_ref, step_ref):
    for rows, reach in halves(q_ref.shape[0]):
        q_new = q_ref[rows, :] - dot(step_ref[rows, :reach], hi_ref[:reach, :])
        q_ref[rows, :] = q_new
        hi, lo = split(q_new)
        hi_ref[rows, :] = hi
        if lo_ref is not None:
            lo_ref[rows, :] = lo


def prepare_steps(most, q2, h2, s2, t2, th2):
    def body(carry):
        count, _ = carry
        worst = 0.0
        for side in range(2):
            worst = jnp.maximum(worst, triangle(h2.at[side], s2.at[side]))
        for side in range(2):
            apply_step(q2.at[side], h2.at[side], None, s2.at[side])
            apply_step(t2.at[side], th2.at[side], None, s2.at[side])
        return count + 1, worst

    lax.while_loop(
        lambda carry: (carry[0] < most) & (carry[1] > START_BOUND),
        body,
        (jnp.int32(0), jnp.float32(1e30)),
    )


def own_flag(order_ref, refresh_ref):
    owners = lax.axis_size("fsdp")
    block = order_ref[lax.axis_index("replica") * owners + lax.axis_index("fsdp")]
    flag = block == refresh_ref[0]
    for j in range(1, refresh_ref.shape[0]):
        flag |= block == refresh_ref[j]
    return flag


def start_copies(pairs, sems):
    copies = [pltpu.make_async_copy(src, dst, sems.at[i]) for i, (src, dst) in enumerate(pairs)]
    for copy in copies:
        copy.start()
    return copies


def wait_copies(copies):
    for copy in copies:
        copy.wait()


def prepare_first(order_ref, refresh_ref, lf_hbm, rf_hbm, lb_hbm, rb_hbm, h2, th2,
                  q2, t2, s2, f2, b2, sems):

    @pl.when(own_flag(order_ref, refresh_ref))
    def _():
        copies = start_copies(
            [(lf_hbm, f2.at[0]), (lb_hbm, b2.at[0]), (rf_hbm, f2.at[1]), (rb_hbm, b2.at[1])], sems
        )
        width = lf_hbm.shape[0]
        eye = (
            lax.broadcasted_iota(jnp.int32, (width, width), 0)
            == lax.broadcasted_iota(jnp.int32, (width, width), 1)
        )
        wait_copies(copies)
        for side in range(2):
            p = dot(f2[side].astype(BF16), b2[side].astype(BF16))
            scale = lax.rsqrt(jnp.sum(p * p, axis=0, keepdims=True))
            y = (p * scale).astype(BF16)
            h2[side] = y.T
            gram = dot(h2[side], h2[side], NT)
            reach = jnp.max(jnp.sum(jnp.abs(gram), axis=0, keepdims=True), axis=1, keepdims=True)
            factor_all = lax.rsqrt(0.5 * reach)
            start = h2[side].astype(F32) * factor_all
            q2[side] = start
            h2[side] = start.astype(BF16)
            diagonal = jnp.where(eye, scale * (factor_all / 0.95), 0.0)
            t2[side] = diagonal
            th2[side] = diagonal.astype(BF16)
        prepare_steps(FIRST_STEPS, q2, h2, s2, t2, th2)


def prepare_more(order_ref, refresh_ref, h_ref, th_ref, h2, th2, q2, t2, s2):
    @pl.when(own_flag(order_ref, refresh_ref))
    def _():
        for side in range(2):
            h2[side] = h_ref[side]
            th2[side] = th_ref[side]
            q2[side] = h_ref[side].astype(F32)
            t2[side] = th_ref[side].astype(F32)
        prepare_steps(MORE_STEPS, q2, h2, s2, t2, th2)


def prepare_last(order_ref, refresh_ref, h_ref, th_ref, lf_hbm, rf_hbm, lb_hbm, rb_hbm,
                 w2, q_out, h2, th2, q2, t2, s2, f2, b2, sems):

    @pl.when(own_flag(order_ref, refresh_ref))
    def _():
        copies = start_copies(
            [(lf_hbm, f2.at[0]), (lb_hbm, b2.at[0]), (rf_hbm, f2.at[1]), (rb_hbm, b2.at[1])], sems
        )
        for side in range(2):
            h2[side] = h_ref[side]
            th2[side] = th_ref[side]
            q2[side] = h_ref[side].astype(F32)
            t2[side] = th_ref[side].astype(F32)
        prepare_steps(LAST_STEPS, q2, h2, s2, t2, th2)
        wait_copies(copies)
        for side in range(2):
            basis_hi, basis_lo = split(b2[side].T)
            w = dot(th2[side], basis_hi) + dot(th2[side], basis_lo)
            w_hi, w_lo = split(w)
            factor_hi, factor_lo = split(f2[side])
            w2[side] = w_hi
            q_out[side] = 0.95 * (
                dot(w_hi, factor_hi, NT) + dot(w_hi, factor_lo, NT) + dot(w_lo, factor_hi, NT)
            )


def gram_schmidt(q_ref, hi_ref, lo_ref):
    width = q_ref.shape[0]
    rows = lax.broadcasted_iota(jnp.int32, (width, 1), 0)

    def one(at, carry):
        row = q_ref[pl.ds(at, 1), :]
        row = row * lax.rsqrt(jnp.sum(row * row))
        q = q_ref[...]
        share = jnp.sum(q * row, axis=1, keepdims=True)
        q_ref[...] = q - jnp.where(rows > at, share, 0.0) * row
        q_ref[pl.ds(at, 1), :] = row
        return carry

    lax.fori_loop(0, width, one, 0)
    store_split(hi_ref, lo_ref, q_ref[...])


def gather_kernel(steps, order_ref, parts_hbm, *rest):
    outs, sems = rest[:-1], rest[-1]
    replicas = lax.axis_size("replica")
    at = lax.axis_index("replica")
    slots, _, half = outs[0].shape
    pairs = []
    for number, step in enumerate(steps):
        for part in range(2):
            ahead = (2 * replicas - 1 - step) if part == 0 else (1 + step)
            first = lax.rem(at + ahead, replicas) * slots
            for i in range(slots):
                source = parts_hbm.at[order_ref[first + i], :, pl.ds(part * half, half)]
                pairs.append((source, outs[2 * number + part].at[i]))
    wait_copies(start_copies(pairs, sems))


def add_kernel(got_ref, own_ref, out_ref):
    out_ref[...] = (got_ref[...].astype(F32) + own_ref[...].astype(F32)).astype(BF16)


def place_kernel(order_ref, rows_ref, out_hbm, sems):
    slots = rows_ref.shape[0]
    first = lax.axis_index("replica") * slots
    wait_copies(start_copies(
        [(rows_ref.at[i], out_hbm.at[order_ref[first + i] - first]) for i in range(slots)], sems
    ))


def update_kernel(order_ref, refresh_ref, first_ref, last_ref, w_ref, q_ref,
                  lf_hbm, rf_hbm, lb_hbm, rb_hbm, moment_hbm, second_hbm,
                  update_ref, left_hbm, right_hbm,
                  q2, h2, l2, s2, f2, b2, moment_ref, second_ref, new2, grad_ref, sems, out_sems):
    flag = own_flag(order_ref, refresh_ref)
    copies = start_copies(
        [(lf_hbm, f2.at[0]), (rf_hbm, f2.at[1]), (lb_hbm, b2.at[0]), (rb_hbm, b2.at[1]),
         (moment_hbm, moment_ref), (second_hbm, second_ref)],
        sems,
    )
    width = grad_ref.shape[0]
    weight = 0.05 / width
    grad_ref[:, : width // 2] = first_ref[...]
    grad_ref[:, width // 2 :] = last_ref[...]
    grad = grad_ref[...]
    grad_t = grad.T
    new2[0] = weight * dot(grad, grad, NT)
    new2[1] = weight * dot(grad_t, grad_t, NT)

    wait_copies(copies[:4])
    for side in range(2):
        new2[side] += 0.95 * f2[side]
    out_copies = start_copies([(new2.at[0], left_hbm), (new2.at[1], right_hbm)], out_sems)

    @pl.when(jnp.logical_not(flag))
    def _():
        store_split(h2.at[0], l2.at[0], b2[0].T)
        store_split(h2.at[1], l2.at[1], b2[1].T)

    @pl.when(flag)
    def _():
        part = dot(w_ref[0], grad).astype(BF16)
        q_left = q_ref[0] + weight * dot(part, grad, NT)
        part = dot(w_ref[1], grad, NT).astype(BF16)
        q_right = q_ref[1] + weight * dot(part, grad)
        q2[0] = q_left
        h2[0] = q_left.astype(BF16)
        q2[1] = q_right
        h2[1] = q_right.astype(BF16)

        def body(carry):
            count, _ = carry
            worst = 0.0
            for side in range(2):
                worst = jnp.maximum(worst, triangle(h2.at[side], s2.at[side]))
            for side in range(2):
                apply_step(q2.at[side], h2.at[side], l2.at[side], s2.at[side])
            return count + 1, worst

        _, worst = lax.while_loop(
            lambda carry: (carry[0] < 20) & (carry[1] > END_BOUND),
            body,
            (jnp.int32(0), jnp.float32(1e30)),
        )

        @pl.when(jnp.logical_not(worst <= END_BOUND))
        def _():
            for side in range(2):
                q2[side] = lax.dot_general(
                    new2[side], b2[side], NN,
                    precision=lax.Precision.HIGHEST, preferred_element_type=F32,
                ).T
                gram_schmidt(q2.at[side], h2.at[side], l2.at[side])

    left_hi = h2[0]
    left_lo = l2[0]
    right_hi = h2[1]
    right_lo = l2[1]
    wait_copies(copies[4:])
    rotated = dot(dot(left_hi, grad).astype(BF16), right_hi, NT)
    moment_hi, moment_lo = split(0.9 * moment_ref[...] + 0.1 * grad.astype(F32))
    part = dot(left_hi, moment_hi) + dot(left_lo, moment_hi) + dot(left_hi, moment_lo)
    part_hi, part_lo = split(part)
    moment = (
        dot(part_hi, right_hi, NT) + dot(part_hi, right_lo, NT) + dot(part_lo, right_hi, NT)
    )
    second = 0.95 * second_ref[...] + 0.05 * rotated * rotated
    scaled = (moment / (jnp.sqrt(second) + 1e-8)).astype(BF16)
    part = (dot(left_hi.T, scaled) + dot(left_lo.T, scaled)).astype(BF16)
    update_ref[...] = (dot(part, right_hi) + dot(part, right_lo)).astype(BF16)
    wait_copies(out_copies)


SMEM_SPEC = pl.BlockSpec(memory_space=pltpu.SMEM)
VMEM_SPEC = pl.BlockSpec(memory_space=pltpu.VMEM)
HBM_SPEC = pl.BlockSpec(memory_space=pltpu.HBM)


def call(kernel, name, in_smem, in_vmem, in_hbm, out_vmem, out_hbm=(), scratch=(), sems=(), flops=0,
         limit=VMEM_LIMIT):
    operands = (*in_smem, *in_vmem, *in_hbm)
    return pl.pallas_call(
        kernel,
        out_shape=[jax.ShapeDtypeStruct(shape, dtype) for shape, dtype in (*out_vmem, *out_hbm)],
        in_specs=[SMEM_SPEC] * len(in_smem) + [VMEM_SPEC] * len(in_vmem) + [HBM_SPEC] * len(in_hbm),
        out_specs=[VMEM_SPEC] * len(out_vmem) + [HBM_SPEC] * len(out_hbm),
        scratch_shapes=[pltpu.VMEM(shape, dtype) for shape, dtype in scratch]
        + [pltpu.SemaphoreType.DMA((count,)) for count in sems],
        compiler_params=pltpu.CompilerParams(vmem_limit_bytes=limit),
        cost_estimate=pl.CostEstimate(
            flops=flops,
            bytes_accessed=sum(x.size * x.dtype.itemsize for x in in_vmem),
            transcendentals=0,
        ),
        name=name,
    )(*operands)


def on_device(
    grad_parts,
    moment,
    second_moment,
    left_factor,
    right_factor,
    left_basis,
    right_basis,
    block_order,
    refresh_ids,
):
    replicas = lax.axis_size("replica")
    owners = lax.axis_size("fsdp")
    group_size = grad_parts.shape[1] // replicas
    rows = grad_parts.shape[2]
    width = grad_parts.shape[3]
    square = (width, width)
    pair = (2,) + square
    work = [(pair, F32), (pair, F32), (pair, BF16)]
    loads = [(pair, F32), (pair, F32)]
    slots = (block_order, refresh_ids)
    state_arrays = (left_factor[0], right_factor[0], left_basis[0], right_basis[0])
    steps = replicas - 1

    chunk = ((group_size, rows, width // 2), BF16)

    def gather(name, at_steps, **places):
        return call(
            functools.partial(gather_kernel, at_steps), name, (block_order,), (), (grad_parts[0],),
            sems=[2 * group_size * len(at_steps)], **places,
        )

    def stage(at, tied, state):
        flops = 40 * width**3
        if at == 0:
            return call(
                prepare_first, "prepare_first", (tied, refresh_ids), (), state_arrays,
                [(pair, BF16)] * 2, scratch=work + loads, sems=[4], flops=flops,
            )
        if at == 1:
            return call(
                prepare_more, "prepare_more", (tied, refresh_ids), state, (),
                [(pair, BF16)] * 2, scratch=work, flops=flops,
            )
        return call(
            prepare_last, "prepare_last", (tied, refresh_ids), state, state_arrays,
            [(pair, BF16), (pair, F32)], scratch=[(pair, BF16)] * 2 + work + loads, sems=[4],
            flops=flops,
        )

    ways = (
        [(i, (i + 1) % replicas) for i in range(replicas)],
        [(i, (i - 1) % replicas) for i in range(replicas)],
    )
    send = list(
        gather("gather_first", (0,), out_vmem=(), out_hbm=[chunk] * 2, limit=VMEM_MOST)
    )
    own = gather(
        "gather_rest", tuple(range(1, replicas)), out_vmem=[chunk] * (2 * steps)
    )
    state = None
    for step in range(steps):
        mine = [own[2 * step], own[2 * step + 1]]
        if step < 3:
            tied, send[0] = lax.optimization_barrier((block_order, send[0]))
        got = [lax.ppermute(send[way], "replica", ways[way]) for way in range(2)]
        if step < 3:
            state = stage(step, tied, state)
            mine[0], *state = lax.optimization_barrier((mine[0], *state))
        send = [
            call(add_kernel, ("add_right", "add_left")[way], (), (got[way], mine[way]), (), [chunk])[0]
            for way in range(2)
        ]
    halves_of = [
        lax.all_to_all(send[way], "fsdp", split_axis=0, concat_axis=0, tiled=True).reshape(
            width, width // 2
        )
        for way in range(2)
    ]
    update, left_new, right_new = call(
        update_kernel, "update", slots, (*halves_of, *state),
        (*state_arrays, moment[0], second_moment[0]), [(square, BF16)], [(square, F32)] * 2,
        scratch=[(pair, F32), (pair, BF16), (pair, BF16), (pair, BF16), *loads,
                 (square, F32), (square, F32), (pair, F32), (square, BF16)],
        sems=[6, 2], flops=100 * width**3,
    )
    returned = lax.all_to_all(
        update.reshape(owners, rows, width), "fsdp", split_axis=0, concat_axis=0, tiled=True
    )
    (step_dir,) = call(
        place_kernel, "place", (block_order,), (returned,), (), (),
        [((group_size, rows, width), BF16)], sems=[group_size],
    )
    return step_dir, left_new[None], right_new[None]


def solution(mesh):
    placed = (
        P("replica", None, "fsdp", None),
        P(("replica", "fsdp"), None, None),
        P(("replica", "fsdp"), None, None),
        P(("replica", "fsdp"), None, None),
        P(("replica", "fsdp"), None, None),
        P(("replica", "fsdp"), None, None),
        P(("replica", "fsdp"), None, None),
        P(),
        P(),
    )
    return jax.shard_map(
        on_device,
        mesh=mesh,
        in_specs=placed,
        out_specs=(
            P("replica", "fsdp", None),
            P(("replica", "fsdp"), None, None),
            P(("replica", "fsdp"), None, None),
        ),
        check_vma=False,
    )
```

```python
import functools

import jax
import jax.numpy as jnp
from jax import lax
from jax.experimental import pallas as pl
from jax.experimental.pallas import tpu as pltpu
from jax.sharding import PartitionSpec as P

F32 = jnp.float32
BF16 = jnp.bfloat16
NN = (((1,), (0,)), ((), ()))
NT = (((1,), (1,)), ((), ()))
VMEM_LIMIT = 24 * 1024 * 1024

START_BOUND = 4.0
END_BOUND = 0.016

FIRST_STEPS = 4
MORE_STEPS = 5
LAST_STEPS = 16


def dot(a, b, form=NN):
    return lax.dot_general(a, b, form, preferred_element_type=F32)


def split(x):
    hi = x.astype(BF16)
    return hi, (x - hi.astype(F32)).astype(BF16)


def store_split(hi_ref, lo_ref, x):
    hi, lo = split(x)
    hi_ref[...] = hi
    lo_ref[...] = lo


def halves(width):
    half = width // 2
    return ((slice(half, width), width), (slice(0, half), half))


def lower_step(gram, first_row):
    rows = lax.broadcasted_iota(jnp.int32, gram.shape, 0) + first_row
    cols = lax.broadcasted_iota(jnp.int32, gram.shape, 1)
    return jnp.where(rows > cols, gram, jnp.where(rows == cols, 0.5 * gram - 0.5, 0.0))


def triangle(hi_ref, step_ref):
    total = 0.0
    for rows, reach in halves(hi_ref.shape[0]):
        step = lower_step(dot(hi_ref[rows, :], hi_ref[:reach, :], NT), rows.start)
        total += jnp.sum(step * step)
        step_ref[rows, :reach] = step.astype(BF16)
    return total


def apply_step(q_ref, hi_ref, lo_ref, step_ref):
    for rows, reach in halves(q_ref.shape[0]):
        q_new = q_ref[rows, :] - dot(step_ref[rows, :reach], hi_ref[:reach, :])
        q_ref[rows, :] = q_new
        hi, lo = split(q_new)
        hi_ref[rows, :] = hi
        if lo_ref is not None:
            lo_ref[rows, :] = lo


def prepare_steps(most, q2, h2, s2, t2, th2):
    def body(carry):
        count, _ = carry
        worst = 0.0
        for side in range(2):
            worst = jnp.maximum(worst, triangle(h2.at[side], s2.at[side]))
        for side in range(2):
            apply_step(q2.at[side], h2.at[side], None, s2.at[side])
            apply_step(t2.at[side], th2.at[side], None, s2.at[side])
        return count + 1, worst

    lax.while_loop(
        lambda carry: (carry[0] < most) & (carry[1] > START_BOUND),
        body,
        (jnp.int32(0), jnp.float32(1e30)),
    )


def own_flag(order_ref, refresh_ref):
    owners = lax.axis_size("fsdp")
    block = order_ref[lax.axis_index("replica") * owners + lax.axis_index("fsdp")]
    flag = block == refresh_ref[0]
    for j in range(1, refresh_ref.shape[0]):
        flag |= block == refresh_ref[j]
    return flag


def start_copies(pairs, sems):
    copies = [pltpu.make_async_copy(src, dst, sems.at[i]) for i, (src, dst) in enumerate(pairs)]
    for copy in copies:
        copy.start()
    return copies


def wait_copies(copies):
    for copy in copies:
        copy.wait()


def prepare_first(order_ref, refresh_ref, lf_hbm, rf_hbm, lb_hbm, rb_hbm, h2, th2,
                  q2, t2, s2, f2, b2, sems):

    @pl.when(own_flag(order_ref, refresh_ref))
    def _():
        copies = start_copies(
            [(lf_hbm, f2.at[0]), (lb_hbm, b2.at[0]), (rf_hbm, f2.at[1]), (rb_hbm, b2.at[1])], sems
        )
        width = lf_hbm.shape[0]
        eye = (
            lax.broadcasted_iota(jnp.int32, (width, width), 0)
            == lax.broadcasted_iota(jnp.int32, (width, width), 1)
        )
        wait_copies(copies)
        for side in range(2):
            p = dot(f2[side].astype(BF16), b2[side].astype(BF16))
            scale = lax.rsqrt(jnp.sum(p * p, axis=0, keepdims=True))
            y = (p * scale).astype(BF16)
            h2[side] = y.T
            gram = dot(h2[side], h2[side], NT)
            reach = jnp.max(jnp.sum(jnp.abs(gram), axis=0, keepdims=True), axis=1, keepdims=True)
            factor_all = lax.rsqrt(0.5 * reach)
            start = h2[side].astype(F32) * factor_all
            q2[side] = start
            h2[side] = start.astype(BF16)
            diagonal = jnp.where(eye, scale * (factor_all / 0.95), 0.0)
            t2[side] = diagonal
            th2[side] = diagonal.astype(BF16)
        prepare_steps(FIRST_STEPS, q2, h2, s2, t2, th2)


def prepare_more(order_ref, refresh_ref, h_ref, th_ref, h2, th2, q2, t2, s2):
    @pl.when(own_flag(order_ref, refresh_ref))
    def _():
        for side in range(2):
            h2[side] = h_ref[side]
            th2[side] = th_ref[side]
            q2[side] = h_ref[side].astype(F32)
            t2[side] = th_ref[side].astype(F32)
        prepare_steps(MORE_STEPS, q2, h2, s2, t2, th2)


def prepare_last(order_ref, refresh_ref, h_ref, th_ref, lf_hbm, rf_hbm, lb_hbm, rb_hbm,
                 w2, q_out, h2, th2, q2, t2, s2, f2, b2, sems):

    @pl.when(own_flag(order_ref, refresh_ref))
    def _():
        copies = start_copies(
            [(lf_hbm, f2.at[0]), (lb_hbm, b2.at[0]), (rf_hbm, f2.at[1]), (rb_hbm, b2.at[1])], sems
        )
        for side in range(2):
            h2[side] = h_ref[side]
            th2[side] = th_ref[side]
            q2[side] = h_ref[side].astype(F32)
            t2[side] = th_ref[side].astype(F32)
        prepare_steps(LAST_STEPS, q2, h2, s2, t2, th2)
        wait_copies(copies)
        for side in range(2):
            basis_hi, basis_lo = split(b2[side].T)
            w = dot(th2[side], basis_hi) + dot(th2[side], basis_lo)
            w_hi, w_lo = split(w)
            factor_hi, factor_lo = split(f2[side])
            w2[side] = w_hi
            q_out[side] = 0.95 * (
                dot(w_hi, factor_hi, NT) + dot(w_hi, factor_lo, NT) + dot(w_lo, factor_hi, NT)
            )


def gram_schmidt(q_ref, hi_ref, lo_ref):
    width = q_ref.shape[0]
    rows = lax.broadcasted_iota(jnp.int32, (width, 1), 0)

    def one(at, carry):
        row = q_ref[pl.ds(at, 1), :]
        row = row * lax.rsqrt(jnp.sum(row * row))
        q = q_ref[...]
        share = jnp.sum(q * row, axis=1, keepdims=True)
        q_ref[...] = q - jnp.where(rows > at, share, 0.0) * row
        q_ref[pl.ds(at, 1), :] = row
        return carry

    lax.fori_loop(0, width, one, 0)
    store_split(hi_ref, lo_ref, q_ref[...])


def gather_kernel(steps, order_ref, parts_hbm, *rest):
    outs, sems = rest[:-1], rest[-1]
    replicas = lax.axis_size("replica")
    at = lax.axis_index("replica")
    slots, _, half = outs[0].shape
    pairs = []
    for number, step in enumerate(steps):
        for part in range(2):
            ahead = (2 * replicas - 1 - step) if part == 0 else (1 + step)
            first = lax.rem(at + ahead, replicas) * slots
            for i in range(slots):
                source = parts_hbm.at[order_ref[first + i], :, pl.ds(part * half, half)]
                pairs.append((source, outs[2 * number + part].at[i]))
    wait_copies(start_copies(pairs, sems))


def add_kernel(got_ref, own_ref, out_ref):
    out_ref[...] = (got_ref[...].astype(F32) + own_ref[...].astype(F32)).astype(BF16)


def place_kernel(order_ref, rows_ref, out_hbm, sems):
    slots = rows_ref.shape[0]
    first = lax.axis_index("replica") * slots
    wait_copies(start_copies(
        [(rows_ref.at[i], out_hbm.at[order_ref[first + i] - first]) for i in range(slots)], sems
    ))


def update_kernel(order_ref, refresh_ref, first_ref, last_ref, w_ref, q_ref,
                  lf_hbm, rf_hbm, lb_hbm, rb_hbm, moment_hbm, second_hbm,
                  update_ref, left_hbm, right_hbm,
                  q2, h2, l2, s2, f2, b2, moment_ref, second_ref, new2, grad_ref, sems, out_sems):
    flag = own_flag(order_ref, refresh_ref)
    copies = start_copies(
        [(lf_hbm, f2.at[0]), (rf_hbm, f2.at[1]), (lb_hbm, b2.at[0]), (rb_hbm, b2.at[1]),
         (moment_hbm, moment_ref), (second_hbm, second_ref)],
        sems,
    )
    width = grad_ref.shape[0]
    weight = 0.05 / width
    grad_ref[:, : width // 2] = first_ref[...]
    grad_ref[:, width // 2 :] = last_ref[...]
    grad = grad_ref[...]
    grad_t = grad.T
    new2[0] = weight * dot(grad, grad, NT)
    new2[1] = weight * dot(grad_t, grad_t, NT)

    wait_copies(copies[:4])
    for side in range(2):
        new2[side] += 0.95 * f2[side]
    out_copies = start_copies([(new2.at[0], left_hbm), (new2.at[1], right_hbm)], out_sems)

    @pl.when(jnp.logical_not(flag))
    def _():
        store_split(h2.at[0], l2.at[0], b2[0].T)
        store_split(h2.at[1], l2.at[1], b2[1].T)

    @pl.when(flag)
    def _():
        part = dot(w_ref[0], grad).astype(BF16)
        q_left = q_ref[0] + weight * dot(part, grad, NT)
        part = dot(w_ref[1], grad, NT).astype(BF16)
        q_right = q_ref[1] + weight * dot(part, grad)
        q2[0] = q_left
        h2[0] = q_left.astype(BF16)
        q2[1] = q_right
        h2[1] = q_right.astype(BF16)

        def body(carry):
            count, _ = carry
            worst = 0.0
            for side in range(2):
                worst = jnp.maximum(worst, triangle(h2.at[side], s2.at[side]))
            for side in range(2):
                apply_step(q2.at[side], h2.at[side], l2.at[side], s2.at[side])
            return count + 1, worst

        _, worst = lax.while_loop(
            lambda carry: (carry[0] < 20) & (carry[1] > END_BOUND),
            body,
            (jnp.int32(0), jnp.float32(1e30)),
        )

        @pl.when(jnp.logical_not(worst <= END_BOUND))
        def _():
            for side in range(2):
                q2[side] = lax.dot_general(
                    new2[side], b2[side], NN,
                    precision=lax.Precision.HIGHEST, preferred_element_type=F32,
                ).T
                gram_schmidt(q2.at[side], h2.at[side], l2.at[side])

    left_hi = h2[0]
    left_lo = l2[0]
    right_hi = h2[1]
    right_lo = l2[1]
    wait_copies(copies[4:])
    rotated = dot(dot(left_hi, grad).astype(BF16), right_hi, NT)
    moment_hi, moment_lo = split(0.9 * moment_ref[...] + 0.1 * grad.astype(F32))
    part = dot(left_hi, moment_hi) + dot(left_lo, moment_hi) + dot(left_hi, moment_lo)
    part_hi, part_lo = split(part)
    moment = (
        dot(part_hi, right_hi, NT) + dot(part_hi, right_lo, NT) + dot(part_lo, right_hi, NT)
    )
    second = 0.95 * second_ref[...] + 0.05 * rotated * rotated
    scaled = (moment / (jnp.sqrt(second) + 1e-8)).astype(BF16)
    part = (dot(left_hi.T, scaled) + dot(left_lo.T, scaled)).astype(BF16)
    update_ref[...] = (dot(part, right_hi) + dot(part, right_lo)).astype(BF16)
    wait_copies(out_copies)


SMEM_SPEC = pl.BlockSpec(memory_space=pltpu.SMEM)
VMEM_SPEC = pl.BlockSpec(memory_space=pltpu.VMEM)
HBM_SPEC = pl.BlockSpec(memory_space=pltpu.HBM)


def call(kernel, name, in_smem, in_vmem, in_hbm, out_vmem, out_hbm=(), scratch=(), sems=(), flops=0):
    operands = (*in_smem, *in_vmem, *in_hbm)
    return pl.pallas_call(
        kernel,
        out_shape=[jax.ShapeDtypeStruct(shape, dtype) for shape, dtype in (*out_vmem, *out_hbm)],
        in_specs=[SMEM_SPEC] * len(in_smem) + [VMEM_SPEC] * len(in_vmem) + [HBM_SPEC] * len(in_hbm),
        out_specs=[VMEM_SPEC] * len(out_vmem) + [HBM_SPEC] * len(out_hbm),
        scratch_shapes=[pltpu.VMEM(shape, dtype) for shape, dtype in scratch]
        + [pltpu.SemaphoreType.DMA((count,)) for count in sems],
        compiler_params=pltpu.CompilerParams(vmem_limit_bytes=VMEM_LIMIT),
        cost_estimate=pl.CostEstimate(
            flops=flops,
            bytes_accessed=sum(x.size * x.dtype.itemsize for x in in_vmem),
            transcendentals=0,
        ),
        name=name,
    )(*operands)


def on_device(
    grad_parts,
    moment,
    second_moment,
    left_factor,
    right_factor,
    left_basis,
    right_basis,
    block_order,
    refresh_ids,
):
    replicas = lax.axis_size("replica")
    owners = lax.axis_size("fsdp")
    group_size = grad_parts.shape[1] // replicas
    rows = grad_parts.shape[2]
    width = grad_parts.shape[3]
    square = (width, width)
    pair = (2,) + square
    work = [(pair, F32), (pair, F32), (pair, BF16)]
    loads = [(pair, F32), (pair, F32)]
    slots = (block_order, refresh_ids)
    state_arrays = (left_factor[0], right_factor[0], left_basis[0], right_basis[0])
    steps = replicas - 1

    chunk = ((group_size, rows, width // 2), BF16)

    def gather(name, at_steps):
        return call(
            functools.partial(gather_kernel, at_steps), name, (block_order,), (), (grad_parts[0],),
            [chunk] * (2 * len(at_steps)), sems=[2 * group_size * len(at_steps)],
        )

    def stage(at, tied, state):
        flops = 40 * width**3
        if at == 0:
            return call(
                prepare_first, "prepare_first", (tied, refresh_ids), (), state_arrays,
                [(pair, BF16)] * 2, scratch=work + loads, sems=[4], flops=flops,
            )
        if at == 1:
            return call(
                prepare_more, "prepare_more", (tied, refresh_ids), state, (),
                [(pair, BF16)] * 2, scratch=work, flops=flops,
            )
        return call(
            prepare_last, "prepare_last", (tied, refresh_ids), state, state_arrays,
            [(pair, BF16), (pair, F32)], scratch=[(pair, BF16)] * 2 + work + loads, sems=[4],
            flops=flops,
        )

    ways = (
        [(i, (i + 1) % replicas) for i in range(replicas)],
        [(i, (i - 1) % replicas) for i in range(replicas)],
    )
    send = list(gather("gather_first", (0,)))
    own = gather("gather_rest", tuple(range(1, replicas)))
    state = None
    for step in range(steps):
        mine = [own[2 * step], own[2 * step + 1]]
        if step < 3:
            tied, send[0] = lax.optimization_barrier((block_order, send[0]))
        got = [lax.ppermute(send[way], "replica", ways[way]) for way in range(2)]
        if step < 3:
            state = stage(step, tied, state)
            mine[0], *state = lax.optimization_barrier((mine[0], *state))
        send = [
            call(add_kernel, ("add_right", "add_left")[way], (), (got[way], mine[way]), (), [chunk])[0]
            for way in range(2)
        ]
    halves_of = [
        lax.all_to_all(send[way], "fsdp", split_axis=0, concat_axis=0, tiled=True).reshape(
            width, width // 2
        )
        for way in range(2)
    ]
    update, left_new, right_new = call(
        update_kernel, "update", slots, (*halves_of, *state),
        (*state_arrays, moment[0], second_moment[0]), [(square, BF16)], [(square, F32)] * 2,
        scratch=[(pair, F32), (pair, BF16), (pair, BF16), (pair, BF16), *loads,
                 (square, F32), (square, F32), (pair, F32), (square, BF16)],
        sems=[6, 2], flops=100 * width**3,
    )
    returned = lax.all_to_all(
        update.reshape(owners, rows, width), "fsdp", split_axis=0, concat_axis=0, tiled=True
    )
    (step_dir,) = call(
        place_kernel, "place", (block_order,), (returned,), (), (),
        [((group_size, rows, width), BF16)], sems=[group_size],
    )
    return step_dir, left_new[None], right_new[None]


def solution(mesh):
    placed = (
        P("replica", None, "fsdp", None),
        P(("replica", "fsdp"), None, None),
        P(("replica", "fsdp"), None, None),
        P(("replica", "fsdp"), None, None),
        P(("replica", "fsdp"), None, None),
        P(("replica", "fsdp"), None, None),
        P(("replica", "fsdp"), None, None),
        P(),
        P(),
    )
    return jax.shard_map(
        on_device,
        mesh=mesh,
        in_specs=placed,
        out_specs=(
            P("replica", "fsdp", None),
            P(("replica", "fsdp"), None, None),
            P(("replica", "fsdp"), None, None),
        ),
        check_vma=False,
    )
```

```python
import functools

import jax
import jax.numpy as jnp
from jax import lax
from jax.experimental import pallas as pl
from jax.experimental.pallas import tpu as pltpu
from jax.sharding import PartitionSpec as P

F32 = jnp.float32
BF16 = jnp.bfloat16
NN = (((1,), (0,)), ((), ()))
NT = (((1,), (1,)), ((), ()))
VMEM_LIMIT = 24 * 1024 * 1024

START_BOUND = 4.0
END_BOUND = 0.016

FIRST_STEPS = 4
MORE_STEPS = 5
LAST_STEPS = 16


def dot(a, b, form=NN):
    return lax.dot_general(a, b, form, preferred_element_type=F32)


def split(x):
    hi = x.astype(BF16)
    return hi, (x - hi.astype(F32)).astype(BF16)


def store_split(hi_ref, lo_ref, x):
    hi, lo = split(x)
    hi_ref[...] = hi
    lo_ref[...] = lo


def halves(width):
    half = width // 2
    return ((slice(half, width), width), (slice(0, half), half))


def lower_step(gram, first_row):
    rows = lax.broadcasted_iota(jnp.int32, gram.shape, 0) + first_row
    cols = lax.broadcasted_iota(jnp.int32, gram.shape, 1)
    return jnp.where(rows > cols, gram, jnp.where(rows == cols, 0.5 * gram - 0.5, 0.0))


def triangle(hi_ref, step_ref):
    total = 0.0
    for rows, reach in halves(hi_ref.shape[0]):
        step = lower_step(dot(hi_ref[rows, :], hi_ref[:reach, :], NT), rows.start)
        total += jnp.sum(step * step)
        step_ref[rows, :reach] = step.astype(BF16)
    return total


def apply_step(q_ref, hi_ref, lo_ref, step_ref):
    for rows, reach in halves(q_ref.shape[0]):
        q_new = q_ref[rows, :] - dot(step_ref[rows, :reach], hi_ref[:reach, :])
        q_ref[rows, :] = q_new
        hi, lo = split(q_new)
        hi_ref[rows, :] = hi
        if lo_ref is not None:
            lo_ref[rows, :] = lo


def prepare_steps(most, q2, h2, s2, t2, th2):
    def body(carry):
        count, _ = carry
        worst = 0.0
        for side in range(2):
            worst = jnp.maximum(worst, triangle(h2.at[side], s2.at[side]))
        for side in range(2):
            apply_step(q2.at[side], h2.at[side], None, s2.at[side])
            apply_step(t2.at[side], th2.at[side], None, s2.at[side])
        return count + 1, worst

    lax.while_loop(
        lambda carry: (carry[0] < most) & (carry[1] > START_BOUND),
        body,
        (jnp.int32(0), jnp.float32(1e30)),
    )


def own_flag(order_ref, refresh_ref):
    owners = lax.axis_size("fsdp")
    block = order_ref[lax.axis_index("replica") * owners + lax.axis_index("fsdp")]
    flag = block == refresh_ref[0]
    for j in range(1, refresh_ref.shape[0]):
        flag |= block == refresh_ref[j]
    return flag


def start_copies(pairs, sems):
    copies = [pltpu.make_async_copy(src, dst, sems.at[i]) for i, (src, dst) in enumerate(pairs)]
    for copy in copies:
        copy.start()
    return copies


def wait_copies(copies):
    for copy in copies:
        copy.wait()


def prepare_first(order_ref, refresh_ref, lf_hbm, rf_hbm, lb_hbm, rb_hbm, h2, th2,
                  q2, t2, s2, f2, b2, sems):

    @pl.when(own_flag(order_ref, refresh_ref))
    def _():
        copies = start_copies(
            [(lf_hbm, f2.at[0]), (lb_hbm, b2.at[0]), (rf_hbm, f2.at[1]), (rb_hbm, b2.at[1])], sems
        )
        width = lf_hbm.shape[0]
        eye = (
            lax.broadcasted_iota(jnp.int32, (width, width), 0)
            == lax.broadcasted_iota(jnp.int32, (width, width), 1)
        )
        wait_copies(copies)
        for side in range(2):
            p = dot(f2[side].astype(BF16), b2[side].astype(BF16))
            scale = lax.rsqrt(jnp.sum(p * p, axis=0, keepdims=True))
            y = (p * scale).astype(BF16)
            h2[side] = y.T
            gram = dot(h2[side], h2[side], NT)
            reach = jnp.max(jnp.sum(jnp.abs(gram), axis=0, keepdims=True), axis=1, keepdims=True)
            factor_all = lax.rsqrt(0.5 * reach)
            start = h2[side].astype(F32) * factor_all
            q2[side] = start
            h2[side] = start.astype(BF16)
            diagonal = jnp.where(eye, scale * (factor_all / 0.95), 0.0)
            t2[side] = diagonal
            th2[side] = diagonal.astype(BF16)
        prepare_steps(FIRST_STEPS, q2, h2, s2, t2, th2)


def prepare_more(order_ref, refresh_ref, h_ref, th_ref, h2, th2, q2, t2, s2):
    @pl.when(own_flag(order_ref, refresh_ref))
    def _():
        for side in range(2):
            h2[side] = h_ref[side]
            th2[side] = th_ref[side]
            q2[side] = h_ref[side].astype(F32)
            t2[side] = th_ref[side].astype(F32)
        prepare_steps(MORE_STEPS, q2, h2, s2, t2, th2)


def prepare_last(order_ref, refresh_ref, h_ref, th_ref, lf_hbm, rf_hbm, lb_hbm, rb_hbm,
                 w2, q_out, h2, th2, q2, t2, s2, f2, b2, sems):

    @pl.when(own_flag(order_ref, refresh_ref))
    def _():
        copies = start_copies(
            [(lf_hbm, f2.at[0]), (lb_hbm, b2.at[0]), (rf_hbm, f2.at[1]), (rb_hbm, b2.at[1])], sems
        )
        for side in range(2):
            h2[side] = h_ref[side]
            th2[side] = th_ref[side]
            q2[side] = h_ref[side].astype(F32)
            t2[side] = th_ref[side].astype(F32)
        prepare_steps(LAST_STEPS, q2, h2, s2, t2, th2)
        wait_copies(copies)
        for side in range(2):
            basis_hi, basis_lo = split(b2[side].T)
            w = dot(th2[side], basis_hi) + dot(th2[side], basis_lo)
            w_hi, w_lo = split(w)
            factor_hi, factor_lo = split(f2[side])
            w2[side] = w_hi
            q_out[side] = 0.95 * (
                dot(w_hi, factor_hi, NT) + dot(w_hi, factor_lo, NT) + dot(w_lo, factor_hi, NT)
            )


def gram_schmidt(q_ref, hi_ref, lo_ref):
    width = q_ref.shape[0]
    rows = lax.broadcasted_iota(jnp.int32, (width, 1), 0)

    def one(at, carry):
        row = q_ref[pl.ds(at, 1), :]
        row = row * lax.rsqrt(jnp.sum(row * row))
        q = q_ref[...]
        share = jnp.sum(q * row, axis=1, keepdims=True)
        q_ref[...] = q - jnp.where(rows > at, share, 0.0) * row
        q_ref[pl.ds(at, 1), :] = row
        return carry

    lax.fori_loop(0, width, one, 0)
    store_split(hi_ref, lo_ref, q_ref[...])


def gather_kernel(steps, order_ref, parts_hbm, *rest):
    outs, sems = rest[:-1], rest[-1]
    replicas = lax.axis_size("replica")
    at = lax.axis_index("replica")
    slots, _, half = outs[0].shape
    pairs = []
    for number, step in enumerate(steps):
        for part in range(2):
            ahead = (2 * replicas - 1 - step) if part == 0 else (1 + step)
            first = lax.rem(at + ahead, replicas) * slots
            for i in range(slots):
                source = parts_hbm.at[order_ref[first + i], :, pl.ds(part * half, half)]
                pairs.append((source, outs[2 * number + part].at[i]))
    wait_copies(start_copies(pairs, sems))


def add_kernel(got_ref, own_ref, out_ref):
    out_ref[...] = (got_ref[...].astype(F32) + own_ref[...].astype(F32)).astype(BF16)


def finish_kernel(got_right_ref, got_left_ref, own_right_ref, own_left_ref, out_ref):
    half = got_right_ref.shape[2]
    add_kernel(got_right_ref, own_right_ref, out_ref.at[:, :, :half])
    add_kernel(got_left_ref, own_left_ref, out_ref.at[:, :, half:])


def place_kernel(order_ref, rows_ref, out_hbm, sems):
    slots = rows_ref.shape[0]
    first = lax.axis_index("replica") * slots
    wait_copies(start_copies(
        [(rows_ref.at[i], out_hbm.at[order_ref[first + i] - first]) for i in range(slots)], sems
    ))


def update_kernel(order_ref, refresh_ref, grad_ref, w_ref, q_ref,
                  lf_hbm, rf_hbm, lb_hbm, rb_hbm, moment_hbm, second_hbm,
                  update_ref, left_hbm, right_hbm,
                  q2, h2, l2, s2, f2, b2, moment_ref, second_ref, new2, sems, out_sems):
    flag = own_flag(order_ref, refresh_ref)
    copies = start_copies(
        [(lf_hbm, f2.at[0]), (rf_hbm, f2.at[1]), (lb_hbm, b2.at[0]), (rb_hbm, b2.at[1]),
         (moment_hbm, moment_ref), (second_hbm, second_ref)],
        sems,
    )
    width = grad_ref.shape[0]
    weight = 0.05 / width
    grad = grad_ref[...]
    grad_t = grad.T
    new2[0] = weight * dot(grad, grad, NT)
    new2[1] = weight * dot(grad_t, grad_t, NT)

    wait_copies(copies[:4])
    for side in range(2):
        new2[side] += 0.95 * f2[side]
    out_copies = start_copies([(new2.at[0], left_hbm), (new2.at[1], right_hbm)], out_sems)

    @pl.when(jnp.logical_not(flag))
    def _():
        store_split(h2.at[0], l2.at[0], b2[0].T)
        store_split(h2.at[1], l2.at[1], b2[1].T)

    @pl.when(flag)
    def _():
        part = dot(w_ref[0], grad).astype(BF16)
        q_left = q_ref[0] + weight * dot(part, grad, NT)
        part = dot(w_ref[1], grad, NT).astype(BF16)
        q_right = q_ref[1] + weight * dot(part, grad)
        q2[0] = q_left
        h2[0] = q_left.astype(BF16)
        q2[1] = q_right
        h2[1] = q_right.astype(BF16)

        def body(carry):
            count, _ = carry
            worst = 0.0
            for side in range(2):
                worst = jnp.maximum(worst, triangle(h2.at[side], s2.at[side]))
            for side in range(2):
                apply_step(q2.at[side], h2.at[side], l2.at[side], s2.at[side])
            return count + 1, worst

        _, worst = lax.while_loop(
            lambda carry: (carry[0] < 20) & (carry[1] > END_BOUND),
            body,
            (jnp.int32(0), jnp.float32(1e30)),
        )

        @pl.when(jnp.logical_not(worst <= END_BOUND))
        def _():
            for side in range(2):
                q2[side] = lax.dot_general(
                    new2[side], b2[side], NN,
                    precision=lax.Precision.HIGHEST, preferred_element_type=F32,
                ).T
                gram_schmidt(q2.at[side], h2.at[side], l2.at[side])

    left_hi = h2[0]
    left_lo = l2[0]
    right_hi = h2[1]
    right_lo = l2[1]
    wait_copies(copies[4:])
    rotated = dot(dot(left_hi, grad).astype(BF16), right_hi, NT)
    moment_hi, moment_lo = split(0.9 * moment_ref[...] + 0.1 * grad.astype(F32))
    part = dot(left_hi, moment_hi) + dot(left_lo, moment_hi) + dot(left_hi, moment_lo)
    part_hi, part_lo = split(part)
    moment = (
        dot(part_hi, right_hi, NT) + dot(part_hi, right_lo, NT) + dot(part_lo, right_hi, NT)
    )
    second = 0.95 * second_ref[...] + 0.05 * rotated * rotated
    scaled = (moment / (jnp.sqrt(second) + 1e-8)).astype(BF16)
    part = (dot(left_hi.T, scaled) + dot(left_lo.T, scaled)).astype(BF16)
    update_ref[...] = (dot(part, right_hi) + dot(part, right_lo)).astype(BF16)
    wait_copies(out_copies)


SMEM_SPEC = pl.BlockSpec(memory_space=pltpu.SMEM)
VMEM_SPEC = pl.BlockSpec(memory_space=pltpu.VMEM)
HBM_SPEC = pl.BlockSpec(memory_space=pltpu.HBM)


def call(kernel, name, in_smem, in_vmem, in_hbm, out_vmem, out_hbm=(), scratch=(), sems=(), flops=0):
    operands = (*in_smem, *in_vmem, *in_hbm)
    return pl.pallas_call(
        kernel,
        out_shape=[jax.ShapeDtypeStruct(shape, dtype) for shape, dtype in (*out_vmem, *out_hbm)],
        in_specs=[SMEM_SPEC] * len(in_smem) + [VMEM_SPEC] * len(in_vmem) + [HBM_SPEC] * len(in_hbm),
        out_specs=[VMEM_SPEC] * len(out_vmem) + [HBM_SPEC] * len(out_hbm),
        scratch_shapes=[pltpu.VMEM(shape, dtype) for shape, dtype in scratch]
        + [pltpu.SemaphoreType.DMA((count,)) for count in sems],
        compiler_params=pltpu.CompilerParams(vmem_limit_bytes=VMEM_LIMIT),
        cost_estimate=pl.CostEstimate(
            flops=flops,
            bytes_accessed=sum(x.size * x.dtype.itemsize for x in in_vmem),
            transcendentals=0,
        ),
        name=name,
    )(*operands)


def on_device(
    grad_parts,
    moment,
    second_moment,
    left_factor,
    right_factor,
    left_basis,
    right_basis,
    block_order,
    refresh_ids,
):
    replicas = lax.axis_size("replica")
    owners = lax.axis_size("fsdp")
    group_size = grad_parts.shape[1] // replicas
    rows = grad_parts.shape[2]
    width = grad_parts.shape[3]
    square = (width, width)
    pair = (2,) + square
    work = [(pair, F32), (pair, F32), (pair, BF16)]
    loads = [(pair, F32), (pair, F32)]
    slots = (block_order, refresh_ids)
    state_arrays = (left_factor[0], right_factor[0], left_basis[0], right_basis[0])
    steps = replicas - 1

    chunk = ((group_size, rows, width // 2), BF16)

    def gather(name, at_steps):
        return call(
            functools.partial(gather_kernel, at_steps), name, (block_order,), (), (grad_parts[0],),
            [chunk] * (2 * len(at_steps)), sems=[2 * group_size * len(at_steps)],
        )

    def stage(at, tied, state):
        flops = 40 * width**3
        if at == 0:
            return call(
                prepare_first, "prepare_first", (tied, refresh_ids), (), state_arrays,
                [(pair, BF16)] * 2, scratch=work + loads, sems=[4], flops=flops,
            )
        if at == 1:
            return call(
                prepare_more, "prepare_more", (tied, refresh_ids), state, (),
                [(pair, BF16)] * 2, scratch=work, flops=flops,
            )
        return call(
            prepare_last, "prepare_last", (tied, refresh_ids), state, state_arrays,
            [(pair, BF16), (pair, F32)], scratch=[(pair, BF16)] * 2 + work + loads, sems=[4],
            flops=flops,
        )

    ways = (
        [(i, (i + 1) % replicas) for i in range(replicas)],
        [(i, (i - 1) % replicas) for i in range(replicas)],
    )
    send = list(gather("gather_first", (0,)))
    own = gather("gather_rest", tuple(range(1, replicas)))
    state = None
    for step in range(steps):
        mine = [own[2 * step], own[2 * step + 1]]
        if step < 3:
            tied, send[0] = lax.optimization_barrier((block_order, send[0]))
        got = [lax.ppermute(send[way], "replica", ways[way]) for way in range(2)]
        if step < 3:
            state = stage(step, tied, state)
            mine[0], *state = lax.optimization_barrier((mine[0], *state))
        if step == steps - 1:
            break
        send = [
            call(add_kernel, ("add_right", "add_left")[way], (), (got[way], mine[way]), (), [chunk])[0]
            for way in range(2)
        ]
    (summed,) = call(
        finish_kernel, "finish", (), (*got, *mine), (), [((group_size, rows, width), BF16)]
    )
    gradient = lax.all_to_all(summed, "fsdp", split_axis=0, concat_axis=0, tiled=True)
    update, left_new, right_new = call(
        update_kernel, "update", slots, (gradient.reshape(square), *state),
        (*state_arrays, moment[0], second_moment[0]), [(square, BF16)], [(square, F32)] * 2,
        scratch=[(pair, F32), (pair, BF16), (pair, BF16), (pair, BF16), *loads,
                 (square, F32), (square, F32), (pair, F32)],
        sems=[6, 2], flops=100 * width**3,
    )
    returned = lax.all_to_all(
        update.reshape(owners, rows, width), "fsdp", split_axis=0, concat_axis=0, tiled=True
    )
    (step_dir,) = call(
        place_kernel, "place", (block_order,), (returned,), (), (),
        [((group_size, rows, width), BF16)], sems=[group_size],
    )
    return step_dir, left_new[None], right_new[None]


def solution(mesh):
    placed = (
        P("replica", None, "fsdp", None),
        P(("replica", "fsdp"), None, None),
        P(("replica", "fsdp"), None, None),
        P(("replica", "fsdp"), None, None),
        P(("replica", "fsdp"), None, None),
        P(("replica", "fsdp"), None, None),
        P(("replica", "fsdp"), None, None),
        P(),
        P(),
    )
    return jax.shard_map(
        on_device,
        mesh=mesh,
        in_specs=placed,
        out_specs=(
            P("replica", "fsdp", None),
            P(("replica", "fsdp"), None, None),
            P(("replica", "fsdp"), None, None),
        ),
        check_vma=False,
    )
```

```python
import functools

import jax
import jax.numpy as jnp
from jax import lax
from jax.experimental import pallas as pl
from jax.experimental.pallas import tpu as pltpu
from jax.sharding import PartitionSpec as P

F32 = jnp.float32
BF16 = jnp.bfloat16
NN = (((1,), (0,)), ((), ()))
NT = (((1,), (1,)), ((), ()))
VMEM_LIMIT = 24 * 1024 * 1024
VMEM_MOST = 56 * 1024 * 1024

START_BOUND = 4.0
END_BOUND = 0.016


def dot(a, b, form=NN):
    return lax.dot_general(a, b, form, preferred_element_type=F32)


def split(x):
    hi = x.astype(BF16)
    return hi, (x - hi.astype(F32)).astype(BF16)


def store_split(hi_ref, lo_ref, x):
    hi, lo = split(x)
    hi_ref[...] = hi
    lo_ref[...] = lo


def halves(width):
    half = width // 2
    return ((slice(half, width), width), (slice(0, half), half))


def lower_step(gram, first_row):
    rows = lax.broadcasted_iota(jnp.int32, gram.shape, 0) + first_row
    cols = lax.broadcasted_iota(jnp.int32, gram.shape, 1)
    return jnp.where(rows > cols, gram, jnp.where(rows == cols, 0.5 * gram - 0.5, 0.0))


def triangle(hi_ref, step_ref):
    total = 0.0
    for rows, reach in halves(hi_ref.shape[0]):
        step = lower_step(dot(hi_ref[rows, :], hi_ref[:reach, :], NT), rows.start)
        total += jnp.sum(step * step)
        step_ref[rows, :reach] = step.astype(BF16)
    return total


def apply_step(q_ref, hi_ref, lo_ref, step_ref):
    for rows, reach in halves(q_ref.shape[0]):
        q_new = q_ref[rows, :] - dot(step_ref[rows, :reach], hi_ref[:reach, :])
        q_ref[rows, :] = q_new
        hi, lo = split(q_new)
        hi_ref[rows, :] = hi
        if lo_ref is not None:
            lo_ref[rows, :] = lo


def boosted_steps(number, q2, h2, s2, t2, th2):
    for _ in range(number):
        for side in range(2):
            triangle(h2.at[side], s2.at[side])
        for side in range(2):
            for full, low in ((q2, h2), (t2, th2)):
                for rows, reach in halves(q2.shape[1]):
                    new = 1.3 * full[side, rows, :] - 1.4 * dot(
                        s2[side, rows, :reach], low[side, :reach, :]
                    )
                    full[side, rows, :] = new
                    low[side, rows, :] = new.astype(BF16)


def prepare_steps(most, q2, h2, s2, t2, th2):
    def body(carry):
        count, _ = carry
        worst = 0.0
        for side in range(2):
            worst = jnp.maximum(worst, triangle(h2.at[side], s2.at[side]))
        for side in range(2):
            apply_step(q2.at[side], h2.at[side], None, s2.at[side])
            apply_step(t2.at[side], th2.at[side], None, s2.at[side])
        return count + 1, worst

    lax.while_loop(
        lambda carry: (carry[0] < most) & (carry[1] > START_BOUND),
        body,
        (jnp.int32(0), jnp.float32(1e30)),
    )


def own_flag(order_ref, refresh_ref):
    owners = lax.axis_size("fsdp")
    block = order_ref[lax.axis_index("replica") * owners + lax.axis_index("fsdp")]
    flag = block == refresh_ref[0]
    for j in range(1, refresh_ref.shape[0]):
        flag |= block == refresh_ref[j]
    return flag


def start_copies(pairs, sems):
    copies = [pltpu.make_async_copy(src, dst, sems.at[i]) for i, (src, dst) in enumerate(pairs)]
    for copy in copies:
        copy.start()
    return copies


def wait_copies(copies):
    for copy in copies:
        copy.wait()


def prepare_start(order_ref, refresh_ref, lf_hbm, rf_hbm, lb_hbm, rb_hbm, h2, th2, f2, b2, sems):

    @pl.when(own_flag(order_ref, refresh_ref))
    def _():
        copies = start_copies(
            [(lf_hbm, f2.at[0]), (lb_hbm, b2.at[0]), (rf_hbm, f2.at[1]), (rb_hbm, b2.at[1])], sems
        )
        width = lf_hbm.shape[0]
        eye = (
            lax.broadcasted_iota(jnp.int32, (width, width), 0)
            == lax.broadcasted_iota(jnp.int32, (width, width), 1)
        )
        for side in range(2):
            wait_copies(copies[2 * side : 2 * side + 2])
            p = dot(f2[side].astype(BF16), b2[side].astype(BF16))
            scale = lax.rsqrt(jnp.sum(p * p, axis=0, keepdims=True))
            y = (p * scale).astype(BF16)
            gram = dot(y.T, y).astype(BF16)
            square = jnp.abs(dot(gram, gram))
            reach = jnp.max(jnp.sum(square, axis=0, keepdims=True), axis=1, keepdims=True)
            factor_all = lax.rsqrt(0.5 * jnp.sqrt(reach))
            h2[side] = (y.astype(F32) * factor_all).astype(BF16).T
            th2[side] = jnp.where(eye, scale * (factor_all / 0.95), 0.0).astype(BF16)


def load_state(h_ref, th_ref, h2, th2, q2, t2):
    for side in range(2):
        h2[side] = h_ref[side]
        th2[side] = th_ref[side]
        q2[side] = h_ref[side].astype(F32)
        t2[side] = th_ref[side].astype(F32)


def prepare_boost(order_ref, refresh_ref, h_ref, th_ref, h2, th2, q2, t2, s2):
    @pl.when(own_flag(order_ref, refresh_ref))
    def _():
        load_state(h_ref, th_ref, h2, th2, q2, t2)
        boosted_steps(2, q2, h2, s2, t2, th2)


def prepare_more(most, order_ref, refresh_ref, h_ref, th_ref, h2, th2, q2, t2, s2):
    @pl.when(own_flag(order_ref, refresh_ref))
    def _():
        load_state(h_ref, th_ref, h2, th2, q2, t2)
        prepare_steps(most, q2, h2, s2, t2, th2)


def prepare_last(order_ref, refresh_ref, h_ref, th_ref, lf_hbm, rf_hbm, lb_hbm, rb_hbm,
                 w2, q_out, f2, b2, sems):

    @pl.when(own_flag(order_ref, refresh_ref))
    def _():
        copies = start_copies(
            [(lb_hbm, b2.at[0]), (lf_hbm, f2.at[0]), (rb_hbm, b2.at[1]), (rf_hbm, f2.at[1])], sems
        )
        for side in range(2):
            wait_copies(copies[2 * side : 2 * side + 2])
            basis_hi, basis_lo = split(b2[side].T)
            w = dot(th_ref[side], basis_hi) + dot(th_ref[side], basis_lo)
            w_hi, w_lo = split(w)
            factor_hi, factor_lo = split(f2[side])
            w2[side] = w_hi
            q_out[side] = 0.95 * (
                dot(w_hi, factor_hi, NT) + dot(w_hi, factor_lo, NT) + dot(w_lo, factor_hi, NT)
            )


def gram_schmidt(q_ref, hi_ref, lo_ref):
    width = q_ref.shape[0]
    rows = lax.broadcasted_iota(jnp.int32, (width, 1), 0)

    def one(at, carry):
        row = q_ref[pl.ds(at, 1), :]
        row = row * lax.rsqrt(jnp.sum(row * row))
        q = q_ref[...]
        share = jnp.sum(q * row, axis=1, keepdims=True)
        q_ref[...] = q - jnp.where(rows > at, share, 0.0) * row
        q_ref[pl.ds(at, 1), :] = row
        return carry

    lax.fori_loop(0, width, one, 0)
    store_split(hi_ref, lo_ref, q_ref[...])


def gather_kernel(steps, order_ref, parts_hbm, *rest):
    outs, sems = rest[:-1], rest[-1]
    replicas = lax.axis_size("replica")
    at = lax.axis_index("replica")
    slots, _, half = outs[0].shape
    pairs = []
    for number, step in enumerate(steps):
        for part in range(2):
            ahead = (2 * replicas - 1 - step) if part == 0 else (1 + step)
            first = lax.rem(at + ahead, replicas) * slots
            for i in range(slots):
                source = parts_hbm.at[order_ref[first + i], :, pl.ds(part * half, half)]
                pairs.append((source, outs[2 * number + part].at[i]))
    wait_copies(start_copies(pairs, sems))


def add_kernel(got_ref, own_ref, out_ref):
    out_ref[...] = (got_ref[...].astype(F32) + own_ref[...].astype(F32)).astype(BF16)


def finish_kernel(got_right_ref, got_left_ref, own_right_ref, own_left_ref, out_ref):
    half = got_right_ref.shape[2]
    add_kernel(got_right_ref, own_right_ref, out_ref.at[:, :, :half])
    add_kernel(got_left_ref, own_left_ref, out_ref.at[:, :, half:])


def place_kernel(order_ref, rows_ref, out_hbm, sems):
    slots = rows_ref.shape[0]
    first = lax.axis_index("replica") * slots
    wait_copies(start_copies(
        [(rows_ref.at[i], out_hbm.at[order_ref[first + i] - first]) for i in range(slots)], sems
    ))


def update_kernel(order_ref, refresh_ref, grad_ref, w_ref, q_ref,
                  lf_hbm, rf_hbm, lb_hbm, rb_hbm, moment_hbm, second_hbm,
                  update_ref, left_hbm, right_hbm,
                  q2, h2, l2, s2, f2, b2, moment_ref, second_ref, new2, sems, out_sems):
    flag = own_flag(order_ref, refresh_ref)
    copies = start_copies(
        [(lf_hbm, f2.at[0]), (rf_hbm, f2.at[1]), (lb_hbm, b2.at[0]), (rb_hbm, b2.at[1]),
         (moment_hbm, moment_ref), (second_hbm, second_ref)],
        sems,
    )
    width = grad_ref.shape[0]
    weight = 0.05 / width
    grad = grad_ref[...]
    grad_t = grad.T
    new2[0] = weight * dot(grad, grad, NT)
    new2[1] = weight * dot(grad_t, grad_t, NT)

    wait_copies(copies[:4])
    for side in range(2):
        new2[side] += 0.95 * f2[side]
    out_copies = start_copies([(new2.at[0], left_hbm), (new2.at[1], right_hbm)], out_sems)

    @pl.when(jnp.logical_not(flag))
    def _():
        store_split(h2.at[0], l2.at[0], b2[0].T)
        store_split(h2.at[1], l2.at[1], b2[1].T)

    @pl.when(flag)
    def _():
        part = dot(w_ref[0], grad).astype(BF16)
        q_left = q_ref[0] + weight * dot(part, grad, NT)
        part = dot(w_ref[1], grad, NT).astype(BF16)
        q_right = q_ref[1] + weight * dot(part, grad)
        q2[0] = q_left
        h2[0] = q_left.astype(BF16)
        q2[1] = q_right
        h2[1] = q_right.astype(BF16)

        def body(carry):
            count, _ = carry
            worst = 0.0
            for side in range(2):
                worst = jnp.maximum(worst, triangle(h2.at[side], s2.at[side]))
            for side in range(2):
                apply_step(q2.at[side], h2.at[side], l2.at[side], s2.at[side])
            return count + 1, worst

        _, worst = lax.while_loop(
            lambda carry: (carry[0] < 20) & (carry[1] > END_BOUND),
            body,
            (jnp.int32(0), jnp.float32(1e30)),
        )

        @pl.when(jnp.logical_not(worst <= END_BOUND))
        def _():
            for side in range(2):
                q2[side] = lax.dot_general(
                    new2[side], b2[side], NN,
                    precision=lax.Precision.HIGHEST, preferred_element_type=F32,
                ).T
                gram_schmidt(q2.at[side], h2.at[side], l2.at[side])

    left_hi = h2[0]
    left_lo = l2[0]
    right_hi = h2[1]
    right_lo = l2[1]
    wait_copies(copies[4:])
    rotated = dot(dot(left_hi, grad).astype(BF16), right_hi, NT)
    moment_hi, moment_lo = split(0.9 * moment_ref[...] + 0.1 * grad.astype(F32))
    part = dot(left_hi, moment_hi) + dot(left_lo, moment_hi) + dot(left_hi, moment_lo)
    part_hi, part_lo = split(part)
    moment = (
        dot(part_hi, right_hi, NT) + dot(part_hi, right_lo, NT) + dot(part_lo, right_hi, NT)
    )
    second = 0.95 * second_ref[...] + 0.05 * rotated * rotated
    scaled = (moment / (jnp.sqrt(second) + 1e-8)).astype(BF16)
    part = (dot(left_hi.T, scaled) + dot(left_lo.T, scaled)).astype(BF16)
    update_ref[...] = (dot(part, right_hi) + dot(part, right_lo)).astype(BF16)
    wait_copies(out_copies)


SMEM_SPEC = pl.BlockSpec(memory_space=pltpu.SMEM)
VMEM_SPEC = pl.BlockSpec(memory_space=pltpu.VMEM)
HBM_SPEC = pl.BlockSpec(memory_space=pltpu.HBM)


def call(kernel, name, in_smem, in_vmem, in_hbm, out_vmem, out_hbm=(), scratch=(), sems=(), flops=0,
         limit=VMEM_LIMIT):
    operands = (*in_smem, *in_vmem, *in_hbm)
    return pl.pallas_call(
        kernel,
        out_shape=[jax.ShapeDtypeStruct(shape, dtype) for shape, dtype in (*out_vmem, *out_hbm)],
        in_specs=[SMEM_SPEC] * len(in_smem) + [VMEM_SPEC] * len(in_vmem) + [HBM_SPEC] * len(in_hbm),
        out_specs=[VMEM_SPEC] * len(out_vmem) + [HBM_SPEC] * len(out_hbm),
        scratch_shapes=[pltpu.VMEM(shape, dtype) for shape, dtype in scratch]
        + [pltpu.SemaphoreType.DMA((count,)) for count in sems],
        compiler_params=pltpu.CompilerParams(vmem_limit_bytes=limit),
        cost_estimate=pl.CostEstimate(
            flops=flops,
            bytes_accessed=sum(x.size * x.dtype.itemsize for x in in_vmem),
            transcendentals=0,
        ),
        name=name,
    )(*operands)


def on_device(
    grad_parts,
    moment,
    second_moment,
    left_factor,
    right_factor,
    left_basis,
    right_basis,
    block_order,
    refresh_ids,
):
    replicas = lax.axis_size("replica")
    owners = lax.axis_size("fsdp")
    group_size = grad_parts.shape[1] // replicas
    rows = grad_parts.shape[2]
    width = grad_parts.shape[3]
    square = (width, width)
    pair = (2,) + square
    work = [(pair, F32), (pair, F32), (pair, BF16)]
    loads = [(pair, F32), (pair, F32)]
    slots = (block_order, refresh_ids)
    state_arrays = (left_factor[0], right_factor[0], left_basis[0], right_basis[0])
    steps = replicas - 1

    chunk = ((group_size, rows, width // 2), BF16)

    def gather(name, at_steps, limit):
        return call(
            functools.partial(gather_kernel, at_steps), name, (block_order,), (), (grad_parts[0],),
            [chunk] * (2 * len(at_steps)), sems=[2 * group_size * len(at_steps)], limit=limit,
        )

    def stage(at, tied, state):
        flops = 20 * width**3
        given = (tied, refresh_ids)
        if at == 0:
            return call(
                prepare_start, "prepare_start", given, (), state_arrays,
                [(pair, BF16)] * 2, scratch=loads, sems=[4], flops=flops,
            )
        if at == 5:
            return call(
                prepare_last, "prepare_last", given, state, state_arrays,
                [(pair, BF16), (pair, F32)], scratch=loads, sems=[4], flops=flops,
            )
        kernel = prepare_boost if at == 1 else functools.partial(prepare_more, 2 if at < 4 else 16)
        return call(
            kernel, "prepare_boost" if at == 1 else "prepare_more", given, state, (),
            [(pair, BF16)] * 2, scratch=work, flops=flops,
        )

    ways = (
        [(i, (i + 1) % replicas) for i in range(replicas)],
        [(i, (i - 1) % replicas) for i in range(replicas)],
    )
    send = list(gather("gather_first", (0,), VMEM_MOST))
    own = list(gather("gather_rest", tuple(range(1, replicas)), VMEM_LIMIT))
    got = [None, None]
    state = ()
    for event in range(2 * steps):
        step, way = divmod(event, 2)
        if event == 0:
            tied, *send = lax.optimization_barrier((block_order, *send))
            got = [lax.ppermute(send[k], "replica", ways[k]) for k in range(2)]
        if event < 6:
            state = stage(event, tied, state)
            own[event], *state = lax.optimization_barrier((own[event], *state))
        if step < steps - 1:
            (send[way],) = call(
                add_kernel, ("add_right", "add_left")[way], (), (got[way], own[event]), (), [chunk]
            )
            tied, send[way] = lax.optimization_barrier((block_order, send[way]))
            got[way] = lax.ppermute(send[way], "replica", ways[way])
        elif way == 0:
            tied, got[0] = lax.optimization_barrier((block_order, got[0]))
    mine = own[-2:]
    (summed,) = call(
        finish_kernel, "finish", (), (*got, *mine), (), [((group_size, rows, width), BF16)]
    )
    gradient = lax.all_to_all(summed, "fsdp", split_axis=0, concat_axis=0, tiled=True)
    update, left_new, right_new = call(
        update_kernel, "update", slots, (gradient.reshape(square), *state),
        (*state_arrays, moment[0], second_moment[0]), [(square, BF16)], [(square, F32)] * 2,
        scratch=[(pair, F32), (pair, BF16), (pair, BF16), (pair, BF16), *loads,
                 (square, F32), (square, F32), (pair, F32)],
        sems=[6, 2], flops=100 * width**3,
    )
    returned = lax.all_to_all(
        update.reshape(owners, rows, width), "fsdp", split_axis=0, concat_axis=0, tiled=True
    )
    (step_dir,) = call(
        place_kernel, "place", (block_order,), (returned,), (), (),
        [((group_size, rows, width), BF16)], sems=[group_size],
    )
    return step_dir, left_new[None], right_new[None]


def solution(mesh):
    placed = (
        P("replica", None, "fsdp", None),
        P(("replica", "fsdp"), None, None),
        P(("replica", "fsdp"), None, None),
        P(("replica", "fsdp"), None, None),
        P(("replica", "fsdp"), None, None),
        P(("replica", "fsdp"), None, None),
        P(("replica", "fsdp"), None, None),
        P(),
        P(),
    )
    return jax.shard_map(
        on_device,
        mesh=mesh,
        in_specs=placed,
        out_specs=(
            P("replica", "fsdp", None),
            P(("replica", "fsdp"), None, None),
            P(("replica", "fsdp"), None, None),
        ),
        check_vma=False,
    )
```

```python
import functools

import jax
import jax.numpy as jnp
from jax import lax
from jax.experimental import pallas as pl
from jax.experimental.pallas import tpu as pltpu
from jax.sharding import PartitionSpec as P

F32 = jnp.float32
BF16 = jnp.bfloat16
NN = (((1,), (0,)), ((), ()))
NT = (((1,), (1,)), ((), ()))
VMEM_LIMIT = 24 * 1024 * 1024

START_BOUND = 4.0
END_BOUND = 0.016


def dot(a, b, form=NN):
    return lax.dot_general(a, b, form, preferred_element_type=F32)


def split(x):
    hi = x.astype(BF16)
    return hi, (x - hi.astype(F32)).astype(BF16)


def store_split(hi_ref, lo_ref, x):
    hi, lo = split(x)
    hi_ref[...] = hi
    lo_ref[...] = lo


def halves(width):
    half = width // 2
    return ((slice(half, width), width), (slice(0, half), half))


def lower_step(gram, first_row):
    rows = lax.broadcasted_iota(jnp.int32, gram.shape, 0) + first_row
    cols = lax.broadcasted_iota(jnp.int32, gram.shape, 1)
    return jnp.where(rows > cols, gram, jnp.where(rows == cols, 0.5 * gram - 0.5, 0.0))


def triangle(hi_ref, step_ref):
    total = 0.0
    for rows, reach in halves(hi_ref.shape[0]):
        step = lower_step(dot(hi_ref[rows, :], hi_ref[:reach, :], NT), rows.start)
        total += jnp.sum(step * step)
        step_ref[rows, :reach] = step.astype(BF16)
    return total


def apply_step(q_ref, hi_ref, lo_ref, step_ref):
    for rows, reach in halves(q_ref.shape[0]):
        q_new = q_ref[rows, :] - dot(step_ref[rows, :reach], hi_ref[:reach, :])
        q_ref[rows, :] = q_new
        hi, lo = split(q_new)
        hi_ref[rows, :] = hi
        if lo_ref is not None:
            lo_ref[rows, :] = lo


def boosted_steps(number, q2, h2, s2, t2, th2):
    for _ in range(number):
        for side in range(2):
            triangle(h2.at[side], s2.at[side])
        for side in range(2):
            for full, low in ((q2, h2), (t2, th2)):
                for rows, reach in halves(q2.shape[1]):
                    new = 1.3 * full[side, rows, :] - 1.4 * dot(
                        s2[side, rows, :reach], low[side, :reach, :]
                    )
                    full[side, rows, :] = new
                    low[side, rows, :] = new.astype(BF16)


def prepare_steps(most, q2, h2, s2, t2, th2):
    def body(carry):
        count, _ = carry
        worst = 0.0
        for side in range(2):
            worst = jnp.maximum(worst, triangle(h2.at[side], s2.at[side]))
        for side in range(2):
            apply_step(q2.at[side], h2.at[side], None, s2.at[side])
            apply_step(t2.at[side], th2.at[side], None, s2.at[side])
        return count + 1, worst

    lax.while_loop(
        lambda carry: (carry[0] < most) & (carry[1] > START_BOUND),
        body,
        (jnp.int32(0), jnp.float32(1e30)),
    )


def own_flag(order_ref, refresh_ref):
    owners = lax.axis_size("fsdp")
    block = order_ref[lax.axis_index("replica") * owners + lax.axis_index("fsdp")]
    flag = block == refresh_ref[0]
    for j in range(1, refresh_ref.shape[0]):
        flag |= block == refresh_ref[j]
    return flag


def start_copies(pairs, sems):
    copies = [pltpu.make_async_copy(src, dst, sems.at[i]) for i, (src, dst) in enumerate(pairs)]
    for copy in copies:
        copy.start()
    return copies


def wait_copies(copies):
    for copy in copies:
        copy.wait()


def prepare_start(order_ref, refresh_ref, lf_hbm, rf_hbm, lb_hbm, rb_hbm, h2, th2, f2, b2, sems):

    @pl.when(own_flag(order_ref, refresh_ref))
    def _():
        copies = start_copies(
            [(lf_hbm, f2.at[0]), (lb_hbm, b2.at[0]), (rf_hbm, f2.at[1]), (rb_hbm, b2.at[1])], sems
        )
        width = lf_hbm.shape[0]
        eye = (
            lax.broadcasted_iota(jnp.int32, (width, width), 0)
            == lax.broadcasted_iota(jnp.int32, (width, width), 1)
        )
        for side in range(2):
            wait_copies(copies[2 * side : 2 * side + 2])
            p = dot(f2[side].astype(BF16), b2[side].astype(BF16))
            scale = lax.rsqrt(jnp.sum(p * p, axis=0, keepdims=True))
            y = (p * scale).astype(BF16)
            gram = dot(y.T, y).astype(BF16)
            square = jnp.abs(dot(gram, gram))
            reach = jnp.max(jnp.sum(square, axis=0, keepdims=True), axis=1, keepdims=True)
            factor_all = lax.rsqrt(0.5 * jnp.sqrt(reach))
            h2[side] = (y.astype(F32) * factor_all).astype(BF16).T
            th2[side] = jnp.where(eye, scale * (factor_all / 0.95), 0.0).astype(BF16)


def load_state(h_ref, th_ref, h2, th2, q2, t2):
    for side in range(2):
        h2[side] = h_ref[side]
        th2[side] = th_ref[side]
        q2[side] = h_ref[side].astype(F32)
        t2[side] = th_ref[side].astype(F32)


def prepare_boost(order_ref, refresh_ref, h_ref, th_ref, h2, th2, q2, t2, s2):
    @pl.when(own_flag(order_ref, refresh_ref))
    def _():
        load_state(h_ref, th_ref, h2, th2, q2, t2)
        boosted_steps(2, q2, h2, s2, t2, th2)


def prepare_more(most, order_ref, refresh_ref, h_ref, th_ref, h2, th2, q2, t2, s2):
    @pl.when(own_flag(order_ref, refresh_ref))
    def _():
        load_state(h_ref, th_ref, h2, th2, q2, t2)
        prepare_steps(most, q2, h2, s2, t2, th2)


def prepare_last(order_ref, refresh_ref, h_ref, th_ref, lf_hbm, rf_hbm, lb_hbm, rb_hbm,
                 w2, q_out, f2, b2, sems):

    @pl.when(own_flag(order_ref, refresh_ref))
    def _():
        copies = start_copies(
            [(lb_hbm, b2.at[0]), (lf_hbm, f2.at[0]), (rb_hbm, b2.at[1]), (rf_hbm, f2.at[1])], sems
        )
        for side in range(2):
            wait_copies(copies[2 * side : 2 * side + 2])
            basis_hi, basis_lo = split(b2[side].T)
            w = dot(th_ref[side], basis_hi) + dot(th_ref[side], basis_lo)
            w_hi, w_lo = split(w)
            factor_hi, factor_lo = split(f2[side])
            w2[side] = w_hi
            q_out[side] = 0.95 * (
                dot(w_hi, factor_hi, NT) + dot(w_hi, factor_lo, NT) + dot(w_lo, factor_hi, NT)
            )


def gram_schmidt(q_ref, hi_ref, lo_ref):
    width = q_ref.shape[0]
    rows = lax.broadcasted_iota(jnp.int32, (width, 1), 0)

    def one(at, carry):
        row = q_ref[pl.ds(at, 1), :]
        row = row * lax.rsqrt(jnp.sum(row * row))
        q = q_ref[...]
        share = jnp.sum(q * row, axis=1, keepdims=True)
        q_ref[...] = q - jnp.where(rows > at, share, 0.0) * row
        q_ref[pl.ds(at, 1), :] = row
        return carry

    lax.fori_loop(0, width, one, 0)
    store_split(hi_ref, lo_ref, q_ref[...])


def slice_kernel(parts_hbm, *rest):
    outs, sems = rest[:-1], rest[-1]
    replicas = lax.axis_size("replica")
    slots, _, half = outs[0].shape
    pairs = []
    for event, out in enumerate(outs):
        step, way = divmod(event, 2)
        first = passing_group(step + 1, way, replicas) * slots
        pairs.append((parts_hbm.at[pl.ds(first, slots), :, pl.ds(way * half, half)], out))
    wait_copies(start_copies(pairs, sems))


def passing_group(step, way, replicas):
    ahead = (2 * replicas - 1 - step) if way == 0 else (1 + step)
    return lax.rem(lax.axis_index("replica") + ahead, replicas)


def add_kernel(got_ref, own_ref, out_ref):
    out_ref[...] = (got_ref[...].astype(F32) + own_ref[...].astype(F32)).astype(BF16)


def finish_kernel(order_ref, got_ref, own_ref, out_ref):
    slots = out_ref.shape[0]
    first = lax.axis_index("replica") * slots
    for i in range(slots):
        at = order_ref[first + i] - first
        out_ref[i] = (got_ref[at].astype(F32) + own_ref[at].astype(F32)).astype(BF16)


def place_kernel(order_ref, rows_ref, out_hbm, sems):
    slots = rows_ref.shape[0]
    first = lax.axis_index("replica") * slots
    wait_copies(start_copies(
        [(rows_ref.at[i], out_hbm.at[order_ref[first + i] - first]) for i in range(slots)], sems
    ))


def update_kernel(order_ref, refresh_ref, first_ref, last_ref, w_ref, q_ref,
                  lf_hbm, rf_hbm, lb_hbm, rb_hbm, moment_hbm, second_hbm,
                  update_ref, left_hbm, right_hbm,
                  q2, h2, l2, s2, f2, b2, moment_ref, second_ref, new2, grad_ref, sems, out_sems):
    flag = own_flag(order_ref, refresh_ref)
    copies = start_copies(
        [(lf_hbm, f2.at[0]), (rf_hbm, f2.at[1]), (lb_hbm, b2.at[0]), (rb_hbm, b2.at[1]),
         (moment_hbm, moment_ref), (second_hbm, second_ref)],
        sems,
    )
    width = grad_ref.shape[0]
    weight = 0.05 / width
    grad_ref[:, : width // 2] = first_ref[...]
    grad_ref[:, width // 2 :] = last_ref[...]
    grad = grad_ref[...]
    grad_t = grad.T
    new2[0] = weight * dot(grad, grad, NT)
    new2[1] = weight * dot(grad_t, grad_t, NT)

    wait_copies(copies[:4])
    for side in range(2):
        new2[side] += 0.95 * f2[side]
    out_copies = start_copies([(new2.at[0], left_hbm), (new2.at[1], right_hbm)], out_sems)

    @pl.when(jnp.logical_not(flag))
    def _():
        store_split(h2.at[0], l2.at[0], b2[0].T)
        store_split(h2.at[1], l2.at[1], b2[1].T)

    @pl.when(flag)
    def _():
        part = dot(w_ref[0], grad).astype(BF16)
        q_left = q_ref[0] + weight * dot(part, grad, NT)
        part = dot(w_ref[1], grad, NT).astype(BF16)
        q_right = q_ref[1] + weight * dot(part, grad)
        q2[0] = q_left
        h2[0] = q_left.astype(BF16)
        q2[1] = q_right
        h2[1] = q_right.astype(BF16)

        def body(carry):
            count, _ = carry
            worst = 0.0
            for side in range(2):
                worst = jnp.maximum(worst, triangle(h2.at[side], s2.at[side]))
            for side in range(2):
                apply_step(q2.at[side], h2.at[side], l2.at[side], s2.at[side])
            return count + 1, worst

        _, worst = lax.while_loop(
            lambda carry: (carry[0] < 20) & (carry[1] > END_BOUND),
            body,
            (jnp.int32(0), jnp.float32(1e30)),
        )

        @pl.when(jnp.logical_not(worst <= END_BOUND))
        def _():
            for side in range(2):
                q2[side] = lax.dot_general(
                    new2[side], b2[side], NN,
                    precision=lax.Precision.HIGHEST, preferred_element_type=F32,
                ).T
                gram_schmidt(q2.at[side], h2.at[side], l2.at[side])

    left_hi = h2[0]
    left_lo = l2[0]
    right_hi = h2[1]
    right_lo = l2[1]
    wait_copies(copies[4:])
    rotated = dot(dot(left_hi, grad).astype(BF16), right_hi, NT)
    moment_hi, moment_lo = split(0.9 * moment_ref[...] + 0.1 * grad.astype(F32))
    part = dot(left_hi, moment_hi) + dot(left_lo, moment_hi) + dot(left_hi, moment_lo)
    part_hi, part_lo = split(part)
    moment = (
        dot(part_hi, right_hi, NT) + dot(part_hi, right_lo, NT) + dot(part_lo, right_hi, NT)
    )
    second = 0.95 * second_ref[...] + 0.05 * rotated * rotated
    scaled = (moment / (jnp.sqrt(second) + 1e-8)).astype(BF16)
    part = (dot(left_hi.T, scaled) + dot(left_lo.T, scaled)).astype(BF16)
    update_ref[...] = (dot(part, right_hi) + dot(part, right_lo)).astype(BF16)
    wait_copies(out_copies)


SMEM_SPEC = pl.BlockSpec(memory_space=pltpu.SMEM)
VMEM_SPEC = pl.BlockSpec(memory_space=pltpu.VMEM)
HBM_SPEC = pl.BlockSpec(memory_space=pltpu.HBM)


def call(kernel, name, in_smem, in_vmem, in_hbm, out_vmem, out_hbm=(), scratch=(), sems=(), flops=0):
    operands = (*in_smem, *in_vmem, *in_hbm)
    return pl.pallas_call(
        kernel,
        out_shape=[jax.ShapeDtypeStruct(shape, dtype) for shape, dtype in (*out_vmem, *out_hbm)],
        in_specs=[SMEM_SPEC] * len(in_smem) + [VMEM_SPEC] * len(in_vmem) + [HBM_SPEC] * len(in_hbm),
        out_specs=[VMEM_SPEC] * len(out_vmem) + [HBM_SPEC] * len(out_hbm),
        scratch_shapes=[pltpu.VMEM(shape, dtype) for shape, dtype in scratch]
        + [pltpu.SemaphoreType.DMA((count,)) for count in sems],
        compiler_params=pltpu.CompilerParams(vmem_limit_bytes=VMEM_LIMIT),
        cost_estimate=pl.CostEstimate(
            flops=flops,
            bytes_accessed=sum(x.size * x.dtype.itemsize for x in in_vmem),
            transcendentals=0,
        ),
        name=name,
    )(*operands)


def on_device(
    grad_parts,
    moment,
    second_moment,
    left_factor,
    right_factor,
    left_basis,
    right_basis,
    block_order,
    refresh_ids,
):
    replicas = lax.axis_size("replica")
    owners = lax.axis_size("fsdp")
    group_size = grad_parts.shape[1] // replicas
    rows = grad_parts.shape[2]
    width = grad_parts.shape[3]
    square = (width, width)
    pair = (2,) + square
    work = [(pair, F32), (pair, F32), (pair, BF16)]
    loads = [(pair, F32), (pair, F32)]
    slots = (block_order, refresh_ids)
    state_arrays = (left_factor[0], right_factor[0], left_basis[0], right_basis[0])
    steps = replicas - 1

    chunk = ((group_size, rows, width // 2), BF16)

    def stage(at, tied, state):
        flops = 20 * width**3
        given = (tied, refresh_ids)
        if at == 0:
            return call(
                prepare_start, "prepare_start", given, (), state_arrays,
                [(pair, BF16)] * 2, scratch=loads, sems=[4], flops=flops,
            )
        if at == 5:
            return call(
                prepare_last, "prepare_last", given, state, state_arrays,
                [(pair, BF16), (pair, F32)], scratch=loads, sems=[4], flops=flops,
            )
        kernel = prepare_boost if at == 1 else functools.partial(prepare_more, 2 if at < 4 else 16)
        return call(
            kernel, "prepare_boost" if at == 1 else "prepare_more", given, state, (),
            [(pair, BF16)] * 2, scratch=work, flops=flops,
        )

    ways = (
        [(i, (i + 1) % replicas) for i in range(replicas)],
        [(i, (i - 1) % replicas) for i in range(replicas)],
    )
    half = width // 2
    send = [
        lax.dynamic_slice(
            grad_parts[0],
            (passing_group(0, way, replicas) * group_size, 0, way * half),
            (group_size, rows, half),
        )
        for way in range(2)
    ]
    tied, *send = lax.optimization_barrier((block_order, *send))
    got = [lax.ppermute(send[way], "replica", ways[way]) for way in range(2)]
    own = list(
        call(
            slice_kernel, "own_blocks", (), (), (grad_parts[0],), [chunk] * (2 * steps),
            sems=[2 * steps],
        )
    )
    state = ()
    for event in range(2 * steps - 2):
        way = event % 2
        if event < 4:
            state = stage(event, tied, state)
            own[event], *state = lax.optimization_barrier((own[event], *state))
        (send[way],) = call(
            add_kernel, ("add_right", "add_left")[way], (), (got[way], own[event]), (), [chunk]
        )
        tied, send[way] = lax.optimization_barrier((block_order, send[way]))
        got[way] = lax.ppermute(send[way], "replica", ways[way])
    state = stage(5, tied, stage(4, tied, state))
    parts = []
    for way in range(2):
        mine = own[2 * steps - 2 + way]
        mine, *state = lax.optimization_barrier((mine, *state))
        (summed,) = call(
            finish_kernel, ("finish_right", "finish_left")[way], (block_order,), (got[way], mine),
            (), [chunk],
        )
        part = lax.all_to_all(summed, "fsdp", split_axis=0, concat_axis=0, tiled=True)
        if way == 0:
            part, own[-1] = lax.optimization_barrier((part, own[-1]))
        parts.append(part.reshape(width, half))
    update, left_new, right_new = call(
        update_kernel, "update", slots, (*parts, *state),
        (*state_arrays, moment[0], second_moment[0]), [(square, BF16)], [(square, F32)] * 2,
        scratch=[(pair, F32), (pair, BF16), (pair, BF16), (pair, BF16), *loads,
                 (square, F32), (square, F32), (pair, F32), (square, BF16)],
        sems=[6, 2], flops=100 * width**3,
    )
    returned = lax.all_to_all(
        update.reshape(owners, rows, width), "fsdp", split_axis=0, concat_axis=0, tiled=True
    )
    (step_dir,) = call(
        place_kernel, "place", (block_order,), (returned,), (), (),
        [((group_size, rows, width), BF16)], sems=[group_size],
    )
    return step_dir, left_new[None], right_new[None]


def solution(mesh):
    placed = (
        P("replica", None, "fsdp", None),
        P(("replica", "fsdp"), None, None),
        P(("replica", "fsdp"), None, None),
        P(("replica", "fsdp"), None, None),
        P(("replica", "fsdp"), None, None),
        P(("replica", "fsdp"), None, None),
        P(("replica", "fsdp"), None, None),
        P(),
        P(),
    )
    return jax.shard_map(
        on_device,
        mesh=mesh,
        in_specs=placed,
        out_specs=(
            P("replica", "fsdp", None),
            P(("replica", "fsdp"), None, None),
            P(("replica", "fsdp"), None, None),
        ),
        check_vma=False,
    )
```

```python
import functools

import jax
import jax.numpy as jnp
from jax import lax
from jax.experimental import pallas as pl
from jax.experimental.pallas import tpu as pltpu
from jax.sharding import PartitionSpec as P

F32 = jnp.float32
BF16 = jnp.bfloat16
NN = (((1,), (0,)), ((), ()))
NT = (((1,), (1,)), ((), ()))
VMEM_LIMIT = 20 * 1024 * 1024

START_BOUND = 4.0
END_BOUND = 0.016


def dot(a, b, form=NN):
    return lax.dot_general(a, b, form, preferred_element_type=F32)


def split(x):
    hi = x.astype(BF16)
    return hi, (x - hi.astype(F32)).astype(BF16)


def store_split(hi_ref, lo_ref, x):
    hi, lo = split(x)
    hi_ref[...] = hi
    lo_ref[...] = lo


def ranges(width):
    return slice(0, width // 2), slice(width // 2, width)


def triangle(hi_ref, step_ref):
    first, last = ranges(hi_ref.shape[0])
    square = (first.stop, first.stop)
    rows = lax.broadcasted_iota(jnp.int32, square, 0)
    cols = lax.broadcasted_iota(jnp.int32, square, 1)
    weight = jnp.where(rows > cols, 1.0, jnp.where(rows == cols, 0.5, 0.0))
    half_eye = jnp.where(rows == cols, 0.5, 0.0)
    step = dot(hi_ref[last, :], hi_ref[first, :], NT)
    total = step * step
    step_ref[last, first] = step.astype(BF16)
    for part in (first, last):
        step = dot(hi_ref[part, :], hi_ref[part, :], NT) * weight - half_eye
        total += step * step
        step_ref[part, part] = step.astype(BF16)
    return jnp.sum(total)


def apply_step(q_ref, hi_ref, step_ref, keep=1.0, gain=1.0):
    first, last = ranges(q_ref.shape[0])
    for rows, reach in ((last, q_ref.shape[0]), (first, first.stop)):
        q_new = keep * q_ref[rows, :] - gain * dot(step_ref[rows, :reach], hi_ref[:reach, :])
        q_ref[rows, :] = q_new
        hi_ref[rows, :] = q_new.astype(BF16)


def apply_triangle(t_ref, hi_ref, step_ref, keep=1.0, gain=1.0):
    first, last = ranges(t_ref.shape[0])
    for rows, cols, reach in (
        (last, first, slice(0, last.stop)), (last, last, last), (first, first, first)
    ):
        new = keep * t_ref[rows, cols] - gain * dot(step_ref[rows, reach], hi_ref[reach, cols])
        t_ref[rows, cols] = new
        hi_ref[rows, cols] = new.astype(BF16)


def one_step(q2, h2, s2, t2, th2, keep=1.0, gain=1.0):
    worst = 0.0
    for side in range(2):
        worst = jnp.maximum(worst, triangle(h2.at[side], s2.at[side]))
    for side in range(2):
        apply_step(q2.at[side], h2.at[side], s2.at[side], keep, gain)
        if t2 is not None:
            apply_triangle(t2.at[side], th2.at[side], s2.at[side], keep, gain)
    return worst


def steps_until(bound, most, *refs):
    return lax.while_loop(
        lambda carry: (carry[0] < most) & (carry[1] > bound),
        lambda carry: (carry[0] + 1, one_step(*refs)),
        (jnp.int32(0), jnp.float32(1e30)),
    )[1]


def own_flag(order_ref, refresh_ref):
    owners = lax.axis_size("fsdp")
    block = order_ref[lax.axis_index("replica") * owners + lax.axis_index("fsdp")]
    flag = block == refresh_ref[0]
    for j in range(1, refresh_ref.shape[0]):
        flag |= block == refresh_ref[j]
    return flag


def start_copies(pairs, sems):
    copies = [pltpu.make_async_copy(src, dst, sems.at[i]) for i, (src, dst) in enumerate(pairs)]
    for copy in copies:
        copy.start()
    return copies


def wait_copies(copies):
    for copy in copies:
        copy.wait()


def prepare_start(order_ref, refresh_ref, lf_hbm, rf_hbm, lb_hbm, rb_hbm, h2, th2, f2, b2, sems):

    @pl.when(own_flag(order_ref, refresh_ref))
    def _():
        copies = start_copies(
            [(lf_hbm, f2.at[0]), (lb_hbm, b2.at[0]), (rf_hbm, f2.at[1]), (rb_hbm, b2.at[1])], sems
        )
        width = lf_hbm.shape[0]
        eye = (
            lax.broadcasted_iota(jnp.int32, (width, width), 0)
            == lax.broadcasted_iota(jnp.int32, (width, width), 1)
        )
        for side in range(2):
            wait_copies(copies[2 * side : 2 * side + 2])
            p = dot(f2[side].astype(BF16), b2[side].astype(BF16))
            scale = lax.rsqrt(jnp.sum(p * p, axis=0, keepdims=True))
            y = (p * scale).astype(BF16)
            gram = dot(y.T, y).astype(BF16)
            square = jnp.abs(dot(gram, gram))
            reach = jnp.max(jnp.sum(square, axis=0, keepdims=True), axis=1, keepdims=True)
            factor_all = lax.rsqrt(0.5 * jnp.sqrt(reach))
            h2[side] = (y.astype(F32) * factor_all).astype(BF16).T
            th2[side] = jnp.where(eye, scale * (factor_all / 0.95), 0.0).astype(BF16)


def load_state(h_ref, th_ref, h2, th2, q2, t2):
    for side in range(2):
        h2[side] = h_ref[side]
        th2[side] = th_ref[side]
        q2[side] = h_ref[side].astype(F32)
        t2[side] = th_ref[side].astype(F32)


def prepare_boost(order_ref, refresh_ref, h_ref, th_ref, h2, th2, q2, t2, s2):
    @pl.when(own_flag(order_ref, refresh_ref))
    def _():
        load_state(h_ref, th_ref, h2, th2, q2, t2)
        for _ in range(2):
            one_step(q2, h2, s2, t2, th2, 1.3, 1.4)
        one_step(q2, h2, s2, t2, th2)


def prepare_more(most, order_ref, refresh_ref, h_ref, th_ref, h2, th2, q2, t2, s2):
    @pl.when(own_flag(order_ref, refresh_ref))
    def _():
        load_state(h_ref, th_ref, h2, th2, q2, t2)
        steps_until(START_BOUND, most, q2, h2, s2, t2, th2)


def prepare_last(order_ref, refresh_ref, h_ref, th_ref, lf_hbm, rf_hbm, lb_hbm, rb_hbm,
                 w2, q_out, f2, b2, sems):

    @pl.when(own_flag(order_ref, refresh_ref))
    def _():
        copies = start_copies(
            [(lb_hbm, b2.at[0]), (lf_hbm, f2.at[0]), (rb_hbm, b2.at[1]), (rf_hbm, f2.at[1])], sems
        )
        for side in range(2):
            wait_copies(copies[2 * side : 2 * side + 2])
            basis_hi, basis_lo = split(b2[side].T)
            w = dot(th_ref[side], basis_hi) + dot(th_ref[side], basis_lo)
            w_hi, w_lo = split(w)
            factor_hi, factor_lo = split(f2[side])
            w2[side] = w_hi
            q_out[side] = 0.95 * (
                dot(w_hi, factor_hi, NT) + dot(w_hi, factor_lo, NT) + dot(w_lo, factor_hi, NT)
            )


def gram_schmidt(q_ref):
    width = q_ref.shape[0]
    rows = lax.broadcasted_iota(jnp.int32, (width, 1), 0)

    def one(at, carry):
        row = q_ref[pl.ds(at, 1), :]
        row = row * lax.rsqrt(jnp.sum(row * row))
        q = q_ref[...]
        share = jnp.sum(q * row, axis=1, keepdims=True)
        q_ref[...] = q - jnp.where(rows > at, share, 0.0) * row
        q_ref[pl.ds(at, 1), :] = row
        return carry

    lax.fori_loop(0, width, one, 0)


def slice_kernel(parts_hbm, *rest):
    outs, sems = rest[:-1], rest[-1]
    replicas = lax.axis_size("replica")
    slots, _, half = outs[0].shape
    pairs = []
    for event, out in enumerate(outs):
        step, way = divmod(event, 2)
        first = passing_group(step + 1, way, replicas) * slots
        pairs.append((parts_hbm.at[pl.ds(first, slots), :, pl.ds(way * half, half)], out))
    wait_copies(start_copies(pairs, sems))


def passing_group(step, way, replicas):
    ahead = (2 * replicas - 1 - step) if way == 0 else (1 + step)
    return lax.rem(lax.axis_index("replica") + ahead, replicas)


def add_kernel(got_ref, own_ref, out_ref):
    out_ref[...] = (got_ref[...].astype(F32) + own_ref[...].astype(F32)).astype(BF16)


def finish_kernel(order_ref, got_right_ref, got_left_ref, own_right_ref, own_left_ref, out_ref):
    slots = out_ref.shape[0]
    half = got_right_ref.shape[2]
    first = lax.axis_index("replica") * slots
    for i in range(slots):
        at = order_ref[first + i] - first
        for got_ref, own_ref, cols in (
            (got_right_ref, own_right_ref, slice(0, half)),
            (got_left_ref, own_left_ref, slice(half, 2 * half)),
        ):
            out_ref[i, :, cols] = (got_ref[at].astype(F32) + own_ref[at].astype(F32)).astype(BF16)


def place_kernel(order_ref, rows_ref, out_hbm, sems):
    slots = rows_ref.shape[0]
    first = lax.axis_index("replica") * slots
    wait_copies(start_copies(
        [(rows_ref.at[i], out_hbm.at[order_ref[first + i] - first]) for i in range(slots)], sems
    ))


def update_kernel(order_ref, refresh_ref, grad_ref, w_ref, q_ref, lf_ref, rf_ref, lb_ref, rb_ref,
                  moment_ref, second_ref, update_ref, left_hbm, right_hbm,
                  q2, h2, l2, s2, new2, out_sems):
    flag = own_flag(order_ref, refresh_ref)
    width = grad_ref.shape[0]
    weight = 0.05 / width
    grad = grad_ref[...]
    grad_t = grad.T
    new2[0] = 0.95 * lf_ref[...] + weight * dot(grad, grad, NT)
    new2[1] = 0.95 * rf_ref[...] + weight * dot(grad_t, grad_t, NT)
    out_copies = start_copies([(new2.at[0], left_hbm), (new2.at[1], right_hbm)], out_sems)

    @pl.when(jnp.logical_not(flag))
    def _():
        store_split(h2.at[0], l2.at[0], lb_ref[...].T)
        store_split(h2.at[1], l2.at[1], rb_ref[...].T)

    @pl.when(flag)
    def _():
        part = dot(w_ref[0], grad).astype(BF16)
        q_left = q_ref[0] + weight * dot(part, grad, NT)
        part = dot(w_ref[1], grad, NT).astype(BF16)
        q_right = q_ref[1] + weight * dot(part, grad)
        q2[0] = q_left
        h2[0] = q_left.astype(BF16)
        q2[1] = q_right
        h2[1] = q_right.astype(BF16)

        worst = steps_until(END_BOUND, 20, q2, h2, s2, None, None)

        @pl.when(jnp.logical_not(worst <= END_BOUND))
        def _():
            for side, basis in enumerate((lb_ref, rb_ref)):
                q2[side] = lax.dot_general(
                    new2[side], basis[...], NN,
                    precision=lax.Precision.HIGHEST, preferred_element_type=F32,
                ).T
                gram_schmidt(q2.at[side])

        for side in range(2):
            store_split(h2.at[side], l2.at[side], q2[side])

    left_hi = h2[0]
    left_lo = l2[0]
    right_hi = h2[1]
    right_lo = l2[1]
    rotated = dot(dot(left_hi, grad).astype(BF16), right_hi, NT)
    moment_hi, moment_lo = split(0.9 * moment_ref[...] + 0.1 * grad.astype(F32))
    part = dot(left_hi, moment_hi) + dot(left_lo, moment_hi) + dot(left_hi, moment_lo)
    part_hi, part_lo = split(part)
    moment = (
        dot(part_hi, right_hi, NT) + dot(part_hi, right_lo, NT) + dot(part_lo, right_hi, NT)
    )
    second = 0.95 * second_ref[...] + 0.05 * rotated * rotated
    scaled = (moment / (jnp.sqrt(second) + 1e-8)).astype(BF16)
    part = (dot(left_hi.T, scaled) + dot(left_lo.T, scaled)).astype(BF16)
    update_ref[...] = (dot(part, right_hi) + dot(part, right_lo)).astype(BF16)
    wait_copies(out_copies)


SMEM_SPEC = pl.BlockSpec(memory_space=pltpu.SMEM)
VMEM_SPEC = pl.BlockSpec(memory_space=pltpu.VMEM)
HBM_SPEC = pl.BlockSpec(memory_space=pltpu.HBM)


def call(kernel, name, in_smem, in_vmem, in_hbm, out_vmem, out_hbm=(), scratch=(), sems=(), flops=0):
    operands = (*in_smem, *in_vmem, *in_hbm)
    return pl.pallas_call(
        kernel,
        out_shape=[jax.ShapeDtypeStruct(shape, dtype) for shape, dtype in (*out_vmem, *out_hbm)],
        in_specs=[SMEM_SPEC] * len(in_smem) + [VMEM_SPEC] * len(in_vmem) + [HBM_SPEC] * len(in_hbm),
        out_specs=[VMEM_SPEC] * len(out_vmem) + [HBM_SPEC] * len(out_hbm),
        scratch_shapes=[pltpu.VMEM(shape, dtype) for shape, dtype in scratch]
        + [pltpu.SemaphoreType.DMA((count,)) for count in sems],
        compiler_params=pltpu.CompilerParams(vmem_limit_bytes=VMEM_LIMIT),
        cost_estimate=pl.CostEstimate(
            flops=flops,
            bytes_accessed=sum(x.size * x.dtype.itemsize for x in in_vmem),
            transcendentals=0,
        ),
        name=name,
    )(*operands)


def on_device(
    grad_parts,
    moment,
    second_moment,
    left_factor,
    right_factor,
    left_basis,
    right_basis,
    block_order,
    refresh_ids,
):
    replicas = lax.axis_size("replica")
    owners = lax.axis_size("fsdp")
    group_size = grad_parts.shape[1] // replicas
    rows = grad_parts.shape[2]
    width = grad_parts.shape[3]
    square = (width, width)
    pair = (2,) + square
    work = [(pair, F32), (pair, F32), (pair, BF16)]
    loads = [(pair, F32), (pair, F32)]
    slots = (block_order, refresh_ids)
    state_arrays = (left_factor[0], right_factor[0], left_basis[0], right_basis[0])
    steps = replicas - 1

    chunk = ((group_size, rows, width // 2), BF16)

    def stage(at, tied, state):
        flops = 20 * width**3
        given = (tied, refresh_ids)
        if at == 0:
            return call(
                prepare_start, "prepare_start", given, (), state_arrays,
                [(pair, BF16)] * 2, scratch=loads, sems=[4], flops=flops,
            )
        if at == 4:
            return call(
                prepare_last, "prepare_last", given, state, state_arrays,
                [(pair, BF16), (pair, F32)], scratch=loads, sems=[4], flops=flops,
            )
        kernel = prepare_boost if at == 1 else functools.partial(prepare_more, 3 if at == 2 else 16)
        return call(
            kernel, "prepare_boost" if at == 1 else "prepare_more", given, state, (),
            [(pair, BF16)] * 2, scratch=work, flops=flops,
        )

    ways = (
        [(i, (i + 1) % replicas) for i in range(replicas)],
        [(i, (i - 1) % replicas) for i in range(replicas)],
    )
    half = width // 2
    send = [
        lax.dynamic_slice(
            grad_parts[0],
            (passing_group(0, way, replicas) * group_size, 0, way * half),
            (group_size, rows, half),
        )
        for way in range(2)
    ]
    tied, *send = lax.optimization_barrier((block_order, *send))
    got = [lax.ppermute(send[way], "replica", ways[way]) for way in range(2)]
    own = list(
        call(
            slice_kernel, "own_blocks", (), (), (grad_parts[0],), [chunk] * (2 * steps),
            sems=[2 * steps],
        )
    )
    state = ()
    for event in range(2 * steps):
        way = event % 2
        if 0 < event < 6:
            state = stage(event - 1, tied, state)
            own[event], *state = lax.optimization_barrier((own[event], *state))
        if event < 2 * steps - 2:
            (send[way],) = call(
                add_kernel, ("add_right", "add_left")[way], (), (got[way], own[event]), (), [chunk]
            )
            tied, send[way] = lax.optimization_barrier((block_order, send[way]))
            got[way] = lax.ppermute(send[way], "replica", ways[way])
        elif way == 0:
            tied, got[0] = lax.optimization_barrier((block_order, got[0]))
    (summed,) = call(
        finish_kernel, "finish", (block_order,), (*got, *own[-2:]), (),
        [((group_size, rows, width), BF16)],
    )
    gradient = lax.all_to_all(summed, "fsdp", split_axis=0, concat_axis=0, tiled=True)
    update, left_new, right_new = call(
        update_kernel, "update", slots,
        (gradient.reshape(square), *state, *state_arrays, moment[0], second_moment[0]), (),
        [(square, BF16)], [(square, F32)] * 2,
        scratch=[(pair, F32), (pair, BF16), (pair, BF16), (pair, BF16), (pair, F32)],
        sems=[2], flops=100 * width**3,
    )
    returned = lax.all_to_all(
        update.reshape(owners, rows, width), "fsdp", split_axis=0, concat_axis=0, tiled=True
    )
    (step_dir,) = call(
        place_kernel, "place", (block_order,), (returned,), (), (),
        [((group_size, rows, width), BF16)], sems=[group_size],
    )
    return step_dir, left_new[None], right_new[None]


def solution(mesh):
    placed = (
        P("replica", None, "fsdp", None),
        P(("replica", "fsdp"), None, None),
        P(("replica", "fsdp"), None, None),
        P(("replica", "fsdp"), None, None),
        P(("replica", "fsdp"), None, None),
        P(("replica", "fsdp"), None, None),
        P(("replica", "fsdp"), None, None),
        P(),
        P(),
    )
    return jax.shard_map(
        on_device,
        mesh=mesh,
        in_specs=placed,
        out_specs=(
            P("replica", "fsdp", None),
            P(("replica", "fsdp"), None, None),
            P(("replica", "fsdp"), None, None),
        ),
        check_vma=False,
    )
```

```python
import functools

import jax
import jax.numpy as jnp
from jax import lax
from jax.experimental import pallas as pl
from jax.experimental.pallas import tpu as pltpu
from jax.sharding import PartitionSpec as P

F32 = jnp.float32
BF16 = jnp.bfloat16
NN = (((1,), (0,)), ((), ()))
NT = (((1,), (1,)), ((), ()))
VMEM_LIMIT = 20 * 1024 * 1024

START_BOUND = 4.0
END_BOUND = 0.016


def dot(a, b, form=NN):
    return lax.dot_general(a, b, form, preferred_element_type=F32)


def split(x):
    hi = x.astype(BF16)
    return hi, (x - hi.astype(F32)).astype(BF16)


def store_split(hi_ref, lo_ref, x):
    hi, lo = split(x)
    hi_ref[...] = hi
    lo_ref[...] = lo


def ranges(width):
    return slice(0, width // 2), slice(width // 2, width)


def triangle(hi_ref, step_ref):
    first, last = ranges(hi_ref.shape[0])
    square = (first.stop, first.stop)
    rows = lax.broadcasted_iota(jnp.int32, square, 0)
    cols = lax.broadcasted_iota(jnp.int32, square, 1)
    weight = jnp.where(rows > cols, 1.0, jnp.where(rows == cols, 0.5, 0.0))
    half_eye = jnp.where(rows == cols, 0.5, 0.0)
    step = dot(hi_ref[last, :], hi_ref[first, :], NT)
    total = step * step
    step_ref[last, first] = step.astype(BF16)
    for part in (first, last):
        step = dot(hi_ref[part, :], hi_ref[part, :], NT) * weight - half_eye
        total += step * step
        step_ref[part, part] = step.astype(BF16)
    return total


def apply_step(q_ref, hi_ref, step_ref, keep=1.0, gain=1.0):
    first, last = ranges(q_ref.shape[0])
    for rows, reach in ((last, q_ref.shape[0]), (first, first.stop)):
        q_new = keep * q_ref[rows, :] - gain * dot(step_ref[rows, :reach], hi_ref[:reach, :])
        q_ref[rows, :] = q_new
        hi_ref[rows, :] = q_new.astype(BF16)


def apply_triangle(t_ref, hi_ref, step_ref, keep=1.0, gain=1.0):
    first, last = ranges(t_ref.shape[0])
    for rows, cols, reach in (
        (last, first, slice(0, last.stop)), (last, last, last), (first, first, first)
    ):
        new = keep * t_ref[rows, cols] - gain * dot(step_ref[rows, reach], hi_ref[reach, cols])
        t_ref[rows, cols] = new
        hi_ref[rows, cols] = new.astype(BF16)


def one_step(q2, h2, s2, t2, th2, keep=1.0, gain=1.0):
    totals = [triangle(h2.at[side], s2.at[side]) for side in range(2)]
    for side in range(2):
        apply_step(q2.at[side], h2.at[side], s2.at[side], keep, gain)
        if t2 is not None:
            apply_triangle(t2.at[side], th2.at[side], s2.at[side], keep, gain)
    return totals


def steps_until(bound, most, *refs):
    return lax.while_loop(
        lambda carry: (carry[0] < most) & (carry[1] > bound),
        lambda carry: (carry[0] + 1, jnp.maximum(*map(jnp.sum, one_step(*refs)))),
        (jnp.int32(0), jnp.float32(1e30)),
    )[1]


def own_flag(order_ref, refresh_ref):
    owners = lax.axis_size("fsdp")
    block = order_ref[lax.axis_index("replica") * owners + lax.axis_index("fsdp")]
    flag = block == refresh_ref[0]
    for j in range(1, refresh_ref.shape[0]):
        flag |= block == refresh_ref[j]
    return flag


def start_copies(pairs, sems):
    copies = [pltpu.make_async_copy(src, dst, sems.at[i]) for i, (src, dst) in enumerate(pairs)]
    for copy in copies:
        copy.start()
    return copies


def wait_copies(copies):
    for copy in copies:
        copy.wait()


def prepare_start(order_ref, refresh_ref, lf_ref, rf_ref, lb_ref, rb_ref, h2, th2):

    @pl.when(own_flag(order_ref, refresh_ref))
    def _():
        width = lf_ref.shape[0]
        eye = (
            lax.broadcasted_iota(jnp.int32, (width, width), 0)
            == lax.broadcasted_iota(jnp.int32, (width, width), 1)
        )
        for side, (factor, basis) in enumerate(((lf_ref, lb_ref), (rf_ref, rb_ref))):
            p = dot(factor[...].astype(BF16), basis[...].astype(BF16))
            scale = lax.rsqrt(jnp.sum(p * p, axis=0, keepdims=True))
            y = (p * scale).astype(BF16)
            gram = dot(y.T, y).astype(BF16)
            square = jnp.abs(dot(gram, gram))
            reach = jnp.max(jnp.sum(square, axis=0, keepdims=True), axis=1, keepdims=True)
            factor_all = lax.rsqrt(0.5 * jnp.sqrt(reach))
            h2[side] = (y.astype(F32) * factor_all).astype(BF16).T
            th2[side] = jnp.where(eye, scale * (factor_all / 0.95), 0.0).astype(BF16)


def load_state(h_ref, th_ref, h2, th2, q2, t2):
    for side in range(2):
        h2[side] = h_ref[side]
        th2[side] = th_ref[side]
        q2[side] = h_ref[side].astype(F32)
        t2[side] = th_ref[side].astype(F32)


def prepare_boost(order_ref, refresh_ref, h_ref, th_ref, h2, th2, q2, t2, s2):
    @pl.when(own_flag(order_ref, refresh_ref))
    def _():
        load_state(h_ref, th_ref, h2, th2, q2, t2)
        for _ in range(2):
            one_step(q2, h2, s2, t2, th2, 1.3, 1.4)
        one_step(q2, h2, s2, t2, th2)


def prepare_more(most, order_ref, refresh_ref, h_ref, th_ref, h2, th2, q2, t2, s2):
    @pl.when(own_flag(order_ref, refresh_ref))
    def _():
        load_state(h_ref, th_ref, h2, th2, q2, t2)
        if most:
            steps_until(START_BOUND, most, q2, h2, s2, t2, th2)
        else:
            one_step(q2, h2, s2, t2, th2)
            one_step(q2, h2, s2, t2, th2)


def prepare_last(order_ref, refresh_ref, h_ref, th_ref, lf_ref, rf_ref, lb_ref, rb_ref, w2, q_out):

    @pl.when(own_flag(order_ref, refresh_ref))
    def _():
        for side, (factor, basis) in enumerate(((lf_ref, lb_ref), (rf_ref, rb_ref))):
            basis_hi, basis_lo = split(basis[...].T)
            w = dot(th_ref[side], basis_hi) + dot(th_ref[side], basis_lo)
            w_hi, w_lo = split(w)
            factor_hi, factor_lo = split(factor[...])
            w2[side] = w_hi
            q_out[side] = 0.95 * (
                dot(w_hi, factor_hi, NT) + dot(w_hi, factor_lo, NT) + dot(w_lo, factor_hi, NT)
            )


def gram_schmidt(q_ref):
    width = q_ref.shape[0]
    rows = lax.broadcasted_iota(jnp.int32, (width, 1), 0)

    def one(at, carry):
        row = q_ref[pl.ds(at, 1), :]
        row = row * lax.rsqrt(jnp.sum(row * row))
        q = q_ref[...]
        share = jnp.sum(q * row, axis=1, keepdims=True)
        q_ref[...] = q - jnp.where(rows > at, share, 0.0) * row
        q_ref[pl.ds(at, 1), :] = row
        return carry

    lax.fori_loop(0, width, one, 0)


def slice_kernel(parts_hbm, *rest):
    outs, sems = rest[:-1], rest[-1]
    replicas = lax.axis_size("replica")
    slots, _, half = outs[0].shape
    pairs = []
    for event, out in enumerate(outs):
        step, way = divmod(event, 2)
        first = passing_group(step + 1, way, replicas) * slots
        pairs.append((parts_hbm.at[pl.ds(first, slots), :, pl.ds(way * half, half)], out))
    wait_copies(start_copies(pairs, sems))


def passing_group(step, way, replicas):
    ahead = (2 * replicas - 1 - step) if way == 0 else (1 + step)
    return lax.rem(lax.axis_index("replica") + ahead, replicas)


def add_kernel(got_ref, own_ref, out_ref):
    out_ref[...] = (got_ref[...].astype(F32) + own_ref[...].astype(F32)).astype(BF16)


def finish_kernel(order_ref, got_right_ref, got_left_ref, own_right_ref, own_left_ref, out_ref):
    slots = out_ref.shape[0]
    half = got_right_ref.shape[2]
    first = lax.axis_index("replica") * slots
    for i in range(slots):
        at = order_ref[first + i] - first
        for got_ref, own_ref, cols in (
            (got_right_ref, own_right_ref, slice(0, half)),
            (got_left_ref, own_left_ref, slice(half, 2 * half)),
        ):
            out_ref[i, :, cols] = (got_ref[at].astype(F32) + own_ref[at].astype(F32)).astype(BF16)


def place_kernel(order_ref, rows_ref, out_hbm, sems):
    slots = rows_ref.shape[0]
    first = lax.axis_index("replica") * slots
    wait_copies(start_copies(
        [(rows_ref.at[i], out_hbm.at[order_ref[first + i] - first]) for i in range(slots)], sems
    ))


def update_kernel(order_ref, refresh_ref, grad_ref, w_ref, q_ref, lf_ref, rf_ref, lb_ref, rb_ref,
                  moment_ref, second_ref, update_ref, left_hbm, right_hbm,
                  q2, h2, l2, s2, new2, out_sems):
    flag = own_flag(order_ref, refresh_ref)
    width = grad_ref.shape[0]
    weight = 0.05 / width
    grad = grad_ref[...]
    grad_t = grad.T
    new2[0] = 0.95 * lf_ref[...] + weight * dot(grad, grad, NT)
    new2[1] = 0.95 * rf_ref[...] + weight * dot(grad_t, grad_t, NT)
    out_copies = start_copies([(new2.at[0], left_hbm), (new2.at[1], right_hbm)], out_sems)

    @pl.when(jnp.logical_not(flag))
    def _():
        store_split(h2.at[0], l2.at[0], lb_ref[...].T)
        store_split(h2.at[1], l2.at[1], rb_ref[...].T)

    @pl.when(flag)
    def _():
        part = dot(w_ref[0], grad).astype(BF16)
        q_left = q_ref[0] + weight * dot(part, grad, NT)
        part = dot(w_ref[1], grad, NT).astype(BF16)
        q_right = q_ref[1] + weight * dot(part, grad)
        q2[0] = q_left
        h2[0] = q_left.astype(BF16)
        q2[1] = q_right
        h2[1] = q_right.astype(BF16)

        one_step(q2, h2, s2, None, None)
        one_step(q2, h2, s2, None, None)
        worst = steps_until(END_BOUND, 20, q2, h2, s2, None, None)

        @pl.when(jnp.logical_not(worst <= END_BOUND))
        def _():
            for side, basis in enumerate((lb_ref, rb_ref)):
                q2[side] = lax.dot_general(
                    new2[side], basis[...], NN,
                    precision=lax.Precision.HIGHEST, preferred_element_type=F32,
                ).T
                gram_schmidt(q2.at[side])

        for side in range(2):
            store_split(h2.at[side], l2.at[side], q2[side])

    left_hi = h2[0]
    left_lo = l2[0]
    right_hi = h2[1]
    right_lo = l2[1]
    rotated = dot(dot(left_hi, grad).astype(BF16), right_hi, NT)
    moment_hi, moment_lo = split(0.9 * moment_ref[...] + 0.1 * grad.astype(F32))
    part = dot(left_hi, moment_hi) + dot(left_lo, moment_hi) + dot(left_hi, moment_lo)
    part_hi, part_lo = split(part)
    moment = (
        dot(part_hi, right_hi, NT) + dot(part_hi, right_lo, NT) + dot(part_lo, right_hi, NT)
    )
    second = 0.95 * second_ref[...] + 0.05 * rotated * rotated
    scaled = (moment / (jnp.sqrt(second) + 1e-8)).astype(BF16)
    part = (dot(left_hi.T, scaled) + dot(left_lo.T, scaled)).astype(BF16)
    update_ref[...] = (dot(part, right_hi) + dot(part, right_lo)).astype(BF16)
    wait_copies(out_copies)


SMEM_SPEC = pl.BlockSpec(memory_space=pltpu.SMEM)
VMEM_SPEC = pl.BlockSpec(memory_space=pltpu.VMEM)
HBM_SPEC = pl.BlockSpec(memory_space=pltpu.HBM)


def call(kernel, name, in_smem, in_vmem, in_hbm, out_vmem, out_hbm=(), scratch=(), sems=(), flops=0):
    operands = (*in_smem, *in_vmem, *in_hbm)
    return pl.pallas_call(
        kernel,
        out_shape=[jax.ShapeDtypeStruct(shape, dtype) for shape, dtype in (*out_vmem, *out_hbm)],
        in_specs=[SMEM_SPEC] * len(in_smem) + [VMEM_SPEC] * len(in_vmem) + [HBM_SPEC] * len(in_hbm),
        out_specs=[VMEM_SPEC] * len(out_vmem) + [HBM_SPEC] * len(out_hbm),
        scratch_shapes=[pltpu.VMEM(shape, dtype) for shape, dtype in scratch]
        + [pltpu.SemaphoreType.DMA((count,)) for count in sems],
        compiler_params=pltpu.CompilerParams(vmem_limit_bytes=VMEM_LIMIT),
        cost_estimate=pl.CostEstimate(
            flops=flops,
            bytes_accessed=sum(x.size * x.dtype.itemsize for x in in_vmem),
            transcendentals=0,
        ),
        name=name,
    )(*operands)


def on_device(
    grad_parts,
    moment,
    second_moment,
    left_factor,
    right_factor,
    left_basis,
    right_basis,
    block_order,
    refresh_ids,
):
    replicas = lax.axis_size("replica")
    owners = lax.axis_size("fsdp")
    group_size = grad_parts.shape[1] // replicas
    rows = grad_parts.shape[2]
    width = grad_parts.shape[3]
    square = (width, width)
    pair = (2,) + square
    work = [(pair, F32), (pair, F32), (pair, BF16)]
    slots = (block_order, refresh_ids)
    state_arrays = (left_factor[0], right_factor[0], left_basis[0], right_basis[0])
    steps = replicas - 1

    chunk = ((group_size, rows, width // 2), BF16)

    def stage(at, tied, state):
        flops = 20 * width**3
        given = (tied, refresh_ids)
        if at == 0:
            return call(
                prepare_start, "prepare_start", given, state_arrays, (),
                [(pair, BF16)] * 2, flops=flops,
            )
        if at == 4:
            return call(
                prepare_last, "prepare_last", given, (*state, *state_arrays), (),
                [(pair, BF16), (pair, F32)], flops=flops,
            )
        kernel = prepare_boost if at == 1 else functools.partial(prepare_more, 0 if at == 2 else 16)
        return call(
            kernel, "prepare_boost" if at == 1 else "prepare_more", given, state, (),
            [(pair, BF16)] * 2, scratch=work, flops=flops,
        )

    ways = (
        [(i, (i + 1) % replicas) for i in range(replicas)],
        [(i, (i - 1) % replicas) for i in range(replicas)],
    )
    half = width // 2
    send = [
        lax.dynamic_slice(
            grad_parts[0],
            (passing_group(0, way, replicas) * group_size, 0, way * half),
            (group_size, rows, half),
        )
        for way in range(2)
    ]
    tied, *send = lax.optimization_barrier((block_order, *send))
    got = [lax.ppermute(send[way], "replica", ways[way]) for way in range(2)]
    own = list(
        call(
            slice_kernel, "own_blocks", (), (), (grad_parts[0],), [chunk] * (2 * steps),
            sems=[2 * steps],
        )
    )
    state = ()
    for event in range(2 * steps):
        way = event % 2
        if 0 < event < 6:
            state = stage(event - 1, tied, state)
            own[event], *state = lax.optimization_barrier((own[event], *state))
        if event < 2 * steps - 2:
            (send[way],) = call(
                add_kernel, ("add_right", "add_left")[way], (), (got[way], own[event]), (), [chunk]
            )
            tied, send[way] = lax.optimization_barrier((block_order, send[way]))
            got[way] = lax.ppermute(send[way], "replica", ways[way])
        elif way == 0:
            tied, got[0] = lax.optimization_barrier((block_order, got[0]))
    (summed,) = call(
        finish_kernel, "finish", (block_order,), (*got, *own[-2:]), (),
        [((group_size, rows, width), BF16)],
    )
    gradient = lax.all_to_all(summed, "fsdp", split_axis=0, concat_axis=0, tiled=True)
    update, left_new, right_new = call(
        update_kernel, "update", slots,
        (gradient.reshape(square), *state, *state_arrays, moment[0], second_moment[0]), (),
        [(square, BF16)], [(square, F32)] * 2,
        scratch=[(pair, F32), (pair, BF16), (pair, BF16), (pair, BF16), (pair, F32)],
        sems=[2], flops=100 * width**3,
    )
    returned = lax.all_to_all(
        update.reshape(owners, rows, width), "fsdp", split_axis=0, concat_axis=0, tiled=True
    )
    (step_dir,) = call(
        place_kernel, "place", (block_order,), (returned,), (), (),
        [((group_size, rows, width), BF16)], sems=[group_size],
    )
    return step_dir, left_new[None], right_new[None]


def solution(mesh):
    placed = (
        P("replica", None, "fsdp", None),
        P(("replica", "fsdp"), None, None),
        P(("replica", "fsdp"), None, None),
        P(("replica", "fsdp"), None, None),
        P(("replica", "fsdp"), None, None),
        P(("replica", "fsdp"), None, None),
        P(("replica", "fsdp"), None, None),
        P(),
        P(),
    )
    return jax.shard_map(
        on_device,
        mesh=mesh,
        in_specs=placed,
        out_specs=(
            P("replica", "fsdp", None),
            P(("replica", "fsdp"), None, None),
            P(("replica", "fsdp"), None, None),
        ),
        check_vma=False,
    )
```

```python
import functools

import jax
import jax.numpy as jnp
from jax import lax
from jax.experimental import pallas as pl
from jax.experimental.pallas import tpu as pltpu
from jax.sharding import PartitionSpec as P

F32 = jnp.float32
BF16 = jnp.bfloat16
NN = (((1,), (0,)), ((), ()))
NT = (((1,), (1,)), ((), ()))
VMEM_LIMIT = 20 * 1024 * 1024

START_BOUND = 4.0
END_BOUND = 0.016


def dot(a, b, form=NN):
    return lax.dot_general(a, b, form, preferred_element_type=F32)


def split(x):
    hi = x.astype(BF16)
    return hi, (x - hi.astype(F32)).astype(BF16)


def store_split(hi_ref, lo_ref, x):
    hi, lo = split(x)
    hi_ref[...] = hi
    lo_ref[...] = lo


def ranges(width):
    return slice(0, width // 2), slice(width // 2, width)


def triangle(hi_ref, step_ref):
    first, last = ranges(hi_ref.shape[0])
    square = (first.stop, first.stop)
    rows = lax.broadcasted_iota(jnp.int32, square, 0)
    cols = lax.broadcasted_iota(jnp.int32, square, 1)
    weight = jnp.where(rows > cols, 1.0, jnp.where(rows == cols, 0.5, 0.0))
    half_eye = jnp.where(rows == cols, 0.5, 0.0)
    step = dot(hi_ref[last, :], hi_ref[first, :], NT)
    total = step * step
    step_ref[last, first] = step.astype(BF16)
    for part in (first, last):
        step = dot(hi_ref[part, :], hi_ref[part, :], NT) * weight - half_eye
        total += step * step
        step_ref[part, part] = step.astype(BF16)
    return total


def apply_step(q_ref, hi_ref, step_ref, keep=1.0, gain=1.0):
    first, last = ranges(q_ref.shape[0])
    for rows, reach in ((last, q_ref.shape[0]), (first, first.stop)):
        q_new = keep * q_ref[rows, :] - gain * dot(step_ref[rows, :reach], hi_ref[:reach, :])
        q_ref[rows, :] = q_new
        hi_ref[rows, :] = q_new.astype(BF16)


def apply_triangle(t_ref, hi_ref, step_ref, keep=1.0, gain=1.0):
    first, last = ranges(t_ref.shape[0])
    for rows, cols, reach in (
        (last, first, slice(0, last.stop)), (last, last, last), (first, first, first)
    ):
        new = keep * t_ref[rows, cols] - gain * dot(step_ref[rows, reach], hi_ref[reach, cols])
        t_ref[rows, cols] = new
        hi_ref[rows, cols] = new.astype(BF16)


def one_step(q2, h2, s2, t2, th2, keep=1.0, gain=1.0):
    totals = [triangle(h2.at[side], s2.at[side]) for side in range(2)]
    for side in range(2):
        apply_step(q2.at[side], h2.at[side], s2.at[side], keep, gain)
        if t2 is not None:
            apply_triangle(t2.at[side], th2.at[side], s2.at[side], keep, gain)
    return totals


def steps_until(bound, most, *refs):
    return lax.while_loop(
        lambda carry: (carry[0] < most) & (carry[1] > bound),
        lambda carry: (carry[0] + 1, jnp.maximum(*map(jnp.sum, one_step(*refs)))),
        (jnp.int32(0), jnp.float32(1e30)),
    )[1]


def own_flag(order_ref, refresh_ref):
    owners = lax.axis_size("fsdp")
    block = order_ref[lax.axis_index("replica") * owners + lax.axis_index("fsdp")]
    flag = block == refresh_ref[0]
    for j in range(1, refresh_ref.shape[0]):
        flag |= block == refresh_ref[j]
    return flag


def start_copies(pairs, sems):
    copies = [pltpu.make_async_copy(src, dst, sems.at[i]) for i, (src, dst) in enumerate(pairs)]
    for copy in copies:
        copy.start()
    return copies


def wait_copies(copies):
    for copy in copies:
        copy.wait()


def prepare_start(order_ref, refresh_ref, lf_ref, rf_ref, lb_ref, rb_ref, h2, th2):

    @pl.when(own_flag(order_ref, refresh_ref))
    def _():
        width = lf_ref.shape[0]
        eye = (
            lax.broadcasted_iota(jnp.int32, (width, width), 0)
            == lax.broadcasted_iota(jnp.int32, (width, width), 1)
        )
        for side, (factor, basis) in enumerate(((lf_ref, lb_ref), (rf_ref, rb_ref))):
            p = dot(factor[...].astype(BF16), basis[...].astype(BF16))
            scale = lax.rsqrt(jnp.sum(p * p, axis=0, keepdims=True))
            y = (p * scale).astype(BF16)
            gram = dot(y.T, y).astype(BF16)
            square = jnp.abs(dot(gram, gram))
            reach = jnp.max(jnp.sum(square, axis=0, keepdims=True), axis=1, keepdims=True)
            factor_all = lax.rsqrt(0.5 * jnp.sqrt(reach))
            h2[side] = (y.astype(F32) * factor_all).astype(BF16).T
            th2[side] = jnp.where(eye, scale * (factor_all / 0.95), 0.0).astype(BF16)


def load_state(h_ref, th_ref, h2, th2, q2, t2):
    for side in range(2):
        h2[side] = h_ref[side]
        th2[side] = th_ref[side]
        q2[side] = h_ref[side].astype(F32)
        t2[side] = th_ref[side].astype(F32)


def prepare_boost(order_ref, refresh_ref, h_ref, th_ref, h2, th2, q2, t2, s2):
    @pl.when(own_flag(order_ref, refresh_ref))
    def _():
        load_state(h_ref, th_ref, h2, th2, q2, t2)
        for _ in range(2):
            one_step(q2, h2, s2, t2, th2, 1.3, 1.4)
        one_step(q2, h2, s2, t2, th2)


def prepare_more(most, order_ref, refresh_ref, h_ref, th_ref, h2, th2, q2, t2, s2):
    @pl.when(own_flag(order_ref, refresh_ref))
    def _():
        load_state(h_ref, th_ref, h2, th2, q2, t2)
        if most:
            steps_until(START_BOUND, most, q2, h2, s2, t2, th2)
        else:
            one_step(q2, h2, s2, t2, th2)
            one_step(q2, h2, s2, t2, th2)


def prepare_last(order_ref, refresh_ref, h_ref, th_ref, lf_ref, rf_ref, lb_ref, rb_ref, w2, q_out):

    @pl.when(own_flag(order_ref, refresh_ref))
    def _():
        for side, (factor, basis) in enumerate(((lf_ref, lb_ref), (rf_ref, rb_ref))):
            basis_hi, basis_lo = split(basis[...].T)
            w = dot(th_ref[side], basis_hi) + dot(th_ref[side], basis_lo)
            w_hi, w_lo = split(w)
            factor_hi, factor_lo = split(factor[...])
            w2[side] = w_hi
            q_out[side] = 0.95 * (
                dot(w_hi, factor_hi, NT) + dot(w_hi, factor_lo, NT) + dot(w_lo, factor_hi, NT)
            )


def gram_schmidt(q_ref):
    width = q_ref.shape[0]
    rows = lax.broadcasted_iota(jnp.int32, (width, 1), 0)

    def one(at, carry):
        row = q_ref[pl.ds(at, 1), :]
        row = row * lax.rsqrt(jnp.sum(row * row))
        q = q_ref[...]
        share = jnp.sum(q * row, axis=1, keepdims=True)
        q_ref[...] = q - jnp.where(rows > at, share, 0.0) * row
        q_ref[pl.ds(at, 1), :] = row
        return carry

    lax.fori_loop(0, width, one, 0)


def target_group(hop, turn, replicas):
    return jnp.where(lax.axis_index("replica") == hop, replicas - 1 - turn, turn)


def slice_kernel(sends, parts_hbm, *rest):
    outs, sems = rest[:-1], rest[-1]
    replicas = lax.axis_size("replica")
    slots, _, half = outs[0].shape
    groups = [target_group(hop, turn, replicas) for hop, turn in sends]
    groups.append(lax.axis_index("replica"))
    pairs = []
    for at, out in enumerate(outs):
        number, part = divmod(at, 2)
        source = parts_hbm.at[pl.ds(groups[number] * slots, slots), :, pl.ds(part * half, half)]
        pairs.append((source, out))
    wait_copies(start_copies(pairs, sems))


def add_kernel(got_ref, own_ref, out_ref):
    out_ref[...] = (got_ref[...].astype(F32) + own_ref[...].astype(F32)).astype(BF16)


def finish_kernel(order_ref, *rest):
    refs, out_ref = rest[:-1], rest[-1]
    slots, _, width = out_ref.shape
    half = width // 2
    first = lax.axis_index("replica") * slots
    for i in range(slots):
        at = order_ref[first + i] - first
        for part in range(2):
            total = refs[part][at].astype(F32)
            for ref in refs[part + 2 :: 2]:
                total += ref[at].astype(F32)
            out_ref[i, :, pl.ds(part * half, half)] = total.astype(BF16)


def place_kernel(order_ref, rows_ref, out_hbm, sems):
    slots = rows_ref.shape[0]
    first = lax.axis_index("replica") * slots
    wait_copies(start_copies(
        [(rows_ref.at[i], out_hbm.at[order_ref[first + i] - first]) for i in range(slots)], sems
    ))


def update_kernel(order_ref, refresh_ref, grad_ref, w_ref, q_ref, lf_ref, rf_ref, lb_ref, rb_ref,
                  moment_ref, second_ref, update_ref, left_hbm, right_hbm,
                  q2, h2, l2, s2, new2, out_sems):
    flag = own_flag(order_ref, refresh_ref)
    width = grad_ref.shape[0]
    weight = 0.05 / width
    grad = grad_ref[...]
    grad_t = grad.T
    new2[0] = 0.95 * lf_ref[...] + weight * dot(grad, grad, NT)
    new2[1] = 0.95 * rf_ref[...] + weight * dot(grad_t, grad_t, NT)
    out_copies = start_copies([(new2.at[0], left_hbm), (new2.at[1], right_hbm)], out_sems)

    @pl.when(jnp.logical_not(flag))
    def _():
        store_split(h2.at[0], l2.at[0], lb_ref[...].T)
        store_split(h2.at[1], l2.at[1], rb_ref[...].T)

    @pl.when(flag)
    def _():
        part = dot(w_ref[0], grad).astype(BF16)
        q_left = q_ref[0] + weight * dot(part, grad, NT)
        part = dot(w_ref[1], grad, NT).astype(BF16)
        q_right = q_ref[1] + weight * dot(part, grad)
        q2[0] = q_left
        h2[0] = q_left.astype(BF16)
        q2[1] = q_right
        h2[1] = q_right.astype(BF16)

        one_step(q2, h2, s2, None, None)
        one_step(q2, h2, s2, None, None)
        worst = steps_until(END_BOUND, 20, q2, h2, s2, None, None)

        @pl.when(jnp.logical_not(worst <= END_BOUND))
        def _():
            for side, basis in enumerate((lb_ref, rb_ref)):
                q2[side] = lax.dot_general(
                    new2[side], basis[...], NN,
                    precision=lax.Precision.HIGHEST, preferred_element_type=F32,
                ).T
                gram_schmidt(q2.at[side])

        for side in range(2):
            store_split(h2.at[side], l2.at[side], q2[side])

    left_hi = h2[0]
    left_lo = l2[0]
    right_hi = h2[1]
    right_lo = l2[1]
    rotated = dot(dot(left_hi, grad).astype(BF16), right_hi, NT)
    moment_hi, moment_lo = split(0.9 * moment_ref[...] + 0.1 * grad.astype(F32))
    part = dot(left_hi, moment_hi) + dot(left_lo, moment_hi) + dot(left_hi, moment_lo)
    part_hi, part_lo = split(part)
    moment = (
        dot(part_hi, right_hi, NT) + dot(part_hi, right_lo, NT) + dot(part_lo, right_hi, NT)
    )
    second = 0.95 * second_ref[...] + 0.05 * rotated * rotated
    root = second * lax.rsqrt(second) + 1e-8
    scaled = (moment * pl.reciprocal(root, approx=True)).astype(BF16)
    part = (dot(left_hi.T, scaled) + dot(left_lo.T, scaled)).astype(BF16)
    update_ref[...] = (dot(part, right_hi) + dot(part, right_lo)).astype(BF16)
    wait_copies(out_copies)


SMEM_SPEC = pl.BlockSpec(memory_space=pltpu.SMEM)
VMEM_SPEC = pl.BlockSpec(memory_space=pltpu.VMEM)
HBM_SPEC = pl.BlockSpec(memory_space=pltpu.HBM)


def call(kernel, name, in_smem, in_vmem, in_hbm, out_vmem, out_hbm=(), scratch=(), sems=(), flops=0):
    operands = (*in_smem, *in_vmem, *in_hbm)
    return pl.pallas_call(
        kernel,
        out_shape=[jax.ShapeDtypeStruct(shape, dtype) for shape, dtype in (*out_vmem, *out_hbm)],
        in_specs=[SMEM_SPEC] * len(in_smem) + [VMEM_SPEC] * len(in_vmem) + [HBM_SPEC] * len(in_hbm),
        out_specs=[VMEM_SPEC] * len(out_vmem) + [HBM_SPEC] * len(out_hbm),
        scratch_shapes=[pltpu.VMEM(shape, dtype) for shape, dtype in scratch]
        + [pltpu.SemaphoreType.DMA((count,)) for count in sems],
        compiler_params=pltpu.CompilerParams(vmem_limit_bytes=VMEM_LIMIT),
        cost_estimate=pl.CostEstimate(
            flops=flops,
            bytes_accessed=sum(x.size * x.dtype.itemsize for x in in_vmem),
            transcendentals=0,
        ),
        name=name,
    )(*operands)


def on_device(
    grad_parts,
    moment,
    second_moment,
    left_factor,
    right_factor,
    left_basis,
    right_basis,
    block_order,
    refresh_ids,
):
    replicas = lax.axis_size("replica")
    owners = lax.axis_size("fsdp")
    group_size = grad_parts.shape[1] // replicas
    rows = grad_parts.shape[2]
    width = grad_parts.shape[3]
    square = (width, width)
    pair = (2,) + square
    work = [(pair, F32), (pair, F32), (pair, BF16)]
    slots = (block_order, refresh_ids)
    state_arrays = (left_factor[0], right_factor[0], left_basis[0], right_basis[0])

    chunk = ((group_size, rows, width // 2), BF16)

    def stage(at, tied, state):
        flops = 20 * width**3
        given = (tied, refresh_ids)
        if at == 0:
            return call(
                prepare_start, "prepare_start", given, state_arrays, (),
                [(pair, BF16)] * 2, flops=flops,
            )
        if at == 4:
            return call(
                prepare_last, "prepare_last", given, (*state, *state_arrays), (),
                [(pair, BF16), (pair, F32)], flops=flops,
            )
        kernel = prepare_boost if at == 1 else functools.partial(prepare_more, 0 if at == 2 else 16)
        return call(
            kernel, "prepare_boost" if at == 1 else "prepare_more", given, state, (),
            [(pair, BF16)] * 2, scratch=work, flops=flops,
        )

    half = width // 2
    places = [(hop, turn) for hop in range(replicas - 1) for turn in range(replicas - 1 - hop)]
    blocks = call(
        functools.partial(slice_kernel, places[1:]), "own_blocks", (), (), (grad_parts[0],),
        [chunk] * (2 * len(places)), sems=[2 * len(places)],
    )
    own = {place: blocks[2 * i : 2 * i + 2] for i, place in enumerate(places[1:])}
    first = target_group(0, 0, replicas) * group_size
    send = {}
    for part in range(2):
        piece = lax.dynamic_slice(
            grad_parts[0], (first, 0, part * half), (group_size, rows, half)
        )
        send[0, 0, part] = piece
    got = {}
    state = ()
    waves = sorted(places, key=lambda place: (place[0] + place[1], place[0]))
    for hop, turn in waves:
        for part in range(2):
            if hop == 0 and turn > 0:
                send[0, turn, part], got[0, turn - 1, part] = lax.optimization_barrier(
                    (own[0, turn][part], got[0, turn - 1, part])
                )
            if hop > 0:
                (send[hop, turn, part],) = call(
                    add_kernel, f"add_{hop}_{turn}_{part}", (),
                    (got[hop - 1, turn, part], own[hop, turn][part]), (), [chunk],
                )
            got[hop, turn, part] = lax.ppermute(
                send[hop, turn, part], "replica",
                [(hop, hop + 1), (replicas - 1 - hop, replicas - 2 - hop)],
            )
    mine = list(blocks[-2:])
    for piece in range(5):
        turn, part = divmod(piece, 2)
        tied, got[0, turn, part] = lax.optimization_barrier((block_order, got[0, turn, part]))
        state = stage(piece, tied, state)
    mine[0], *state = lax.optimization_barrier((mine[0], *state))
    ends = [got[hop, replicas - 2 - hop, part] for hop in range(replicas - 1) for part in range(2)]
    (summed,) = call(
        finish_kernel, "finish", (block_order,), (*mine, *ends), (),
        [((group_size, rows, width), BF16)],
    )
    gradient = lax.all_to_all(summed, "fsdp", split_axis=0, concat_axis=0, tiled=True)
    update, left_new, right_new = call(
        update_kernel, "update", slots,
        (gradient.reshape(square), *state, *state_arrays, moment[0], second_moment[0]), (),
        [(square, BF16)], [(square, F32)] * 2,
        scratch=[(pair, F32), (pair, BF16), (pair, BF16), (pair, BF16), (pair, F32)],
        sems=[2], flops=100 * width**3,
    )
    returned = lax.all_to_all(
        update.reshape(owners, rows, width), "fsdp", split_axis=0, concat_axis=0, tiled=True
    )
    (step_dir,) = call(
        place_kernel, "place", (block_order,), (returned,), (), (),
        [((group_size, rows, width), BF16)], sems=[group_size],
    )
    return step_dir, left_new[None], right_new[None]


def solution(mesh):
    placed = (
        P("replica", None, "fsdp", None),
        P(("replica", "fsdp"), None, None),
        P(("replica", "fsdp"), None, None),
        P(("replica", "fsdp"), None, None),
        P(("replica", "fsdp"), None, None),
        P(("replica", "fsdp"), None, None),
        P(("replica", "fsdp"), None, None),
        P(),
        P(),
    )
    return jax.shard_map(
        on_device,
        mesh=mesh,
        in_specs=placed,
        out_specs=(
            P("replica", "fsdp", None),
            P(("replica", "fsdp"), None, None),
            P(("replica", "fsdp"), None, None),
        ),
        check_vma=False,
    )
```

```python
import functools

import jax
import jax.numpy as jnp
from jax import lax
from jax.experimental import pallas as pl
from jax.experimental.pallas import tpu as pltpu
from jax.sharding import PartitionSpec as P

F32 = jnp.float32
BF16 = jnp.bfloat16
NN = (((1,), (0,)), ((), ()))
NT = (((1,), (1,)), ((), ()))
VMEM_LIMIT = 20 * 1024 * 1024

START_BOUND = 4.0
END_BOUND = 0.016


def dot(a, b, form=NN):
    return lax.dot_general(a, b, form, preferred_element_type=F32)


def split(x):
    hi = x.astype(BF16)
    return hi, (x - hi.astype(F32)).astype(BF16)


def store_split(hi_ref, lo_ref, x):
    hi, lo = split(x)
    hi_ref[...] = hi
    lo_ref[...] = lo


def ranges(width):
    return slice(0, width // 2), slice(width // 2, width)


def triangle(hi_ref, step_ref):
    first, last = ranges(hi_ref.shape[0])
    square = (first.stop, first.stop)
    rows = lax.broadcasted_iota(jnp.int32, square, 0)
    cols = lax.broadcasted_iota(jnp.int32, square, 1)
    weight = jnp.where(rows > cols, 1.0, jnp.where(rows == cols, 0.5, 0.0))
    half_eye = jnp.where(rows == cols, 0.5, 0.0)
    step = dot(hi_ref[last, :], hi_ref[first, :], NT)
    total = step * step
    step_ref[last, first] = step.astype(BF16)
    for part in (first, last):
        step = dot(hi_ref[part, :], hi_ref[part, :], NT) * weight - half_eye
        total += step * step
        step_ref[part, part] = step.astype(BF16)
    return total


def apply_step(q_ref, hi_ref, step_ref, keep=1.0, gain=1.0):
    first, last = ranges(q_ref.shape[0])
    for rows, reach in ((last, q_ref.shape[0]), (first, first.stop)):
        q_new = keep * q_ref[rows, :] - gain * dot(step_ref[rows, :reach], hi_ref[:reach, :])
        q_ref[rows, :] = q_new
        hi_ref[rows, :] = q_new.astype(BF16)


def apply_triangle(t_ref, hi_ref, step_ref, keep=1.0, gain=1.0):
    first, last = ranges(t_ref.shape[0])
    for rows, cols, reach in (
        (last, first, slice(0, last.stop)), (last, last, last), (first, first, first)
    ):
        new = keep * t_ref[rows, cols] - gain * dot(step_ref[rows, reach], hi_ref[reach, cols])
        t_ref[rows, cols] = new
        hi_ref[rows, cols] = new.astype(BF16)


def one_step(q2, h2, s2, t2, th2, keep=1.0, gain=1.0):
    totals = [triangle(h2.at[side], s2.at[side]) for side in range(2)]
    for side in range(2):
        apply_step(q2.at[side], h2.at[side], s2.at[side], keep, gain)
        if t2 is not None:
            apply_triangle(t2.at[side], th2.at[side], s2.at[side], keep, gain)
    return totals


def steps_until(bound, most, *refs):
    return lax.while_loop(
        lambda carry: (carry[0] < most) & (carry[1] > bound),
        lambda carry: (carry[0] + 1, jnp.maximum(*map(jnp.sum, one_step(*refs)))),
        (jnp.int32(0), jnp.float32(1e30)),
    )[1]


def own_flag(order_ref, refresh_ref):
    owners = lax.axis_size("fsdp")
    block = order_ref[lax.axis_index("replica") * owners + lax.axis_index("fsdp")]
    flag = block == refresh_ref[0]
    for j in range(1, refresh_ref.shape[0]):
        flag |= block == refresh_ref[j]
    return flag


def start_copies(pairs, sems):
    copies = [pltpu.make_async_copy(src, dst, sems.at[i]) for i, (src, dst) in enumerate(pairs)]
    for copy in copies:
        copy.start()
    return copies


def wait_copies(copies):
    for copy in copies:
        copy.wait()


def prepare_start(order_ref, refresh_ref, lf_ref, rf_ref, lb_ref, rb_ref, h2, th2):

    @pl.when(own_flag(order_ref, refresh_ref))
    def _():
        width = lf_ref.shape[0]
        eye = (
            lax.broadcasted_iota(jnp.int32, (width, width), 0)
            == lax.broadcasted_iota(jnp.int32, (width, width), 1)
        )
        for side, (factor, basis) in enumerate(((lf_ref, lb_ref), (rf_ref, rb_ref))):
            p = dot(factor[...].astype(BF16), basis[...].astype(BF16))
            scale = lax.rsqrt(jnp.sum(p * p, axis=0, keepdims=True))
            y = (p * scale).astype(BF16)
            gram = dot(y.T, y).astype(BF16)
            square = jnp.abs(dot(gram, gram))
            reach = jnp.max(jnp.sum(square, axis=0, keepdims=True), axis=1, keepdims=True)
            factor_all = lax.rsqrt(0.5 * jnp.sqrt(reach))
            h2[side] = (y.astype(F32) * factor_all).astype(BF16).T
            th2[side] = jnp.where(eye, scale * (factor_all / 0.95), 0.0).astype(BF16)


def load_state(h_ref, th_ref, h2, th2, q2, t2):
    for side in range(2):
        h2[side] = h_ref[side]
        th2[side] = th_ref[side]
        q2[side] = h_ref[side].astype(F32)
        t2[side] = th_ref[side].astype(F32)


def prepare_boost(order_ref, refresh_ref, h_ref, th_ref, h2, th2, q2, t2, s2):
    @pl.when(own_flag(order_ref, refresh_ref))
    def _():
        load_state(h_ref, th_ref, h2, th2, q2, t2)
        for _ in range(2):
            one_step(q2, h2, s2, t2, th2, 1.3, 1.4)


def prepare_more(order_ref, refresh_ref, h_ref, th_ref, h2, th2, q2, t2, s2):
    @pl.when(own_flag(order_ref, refresh_ref))
    def _():
        load_state(h_ref, th_ref, h2, th2, q2, t2)
        one_step(q2, h2, s2, t2, th2)
        one_step(q2, h2, s2, t2, th2)
        steps_until(START_BOUND, 16, q2, h2, s2, t2, th2)


def prepare_last(order_ref, refresh_ref, h_ref, th_ref, lf_ref, rf_ref, lb_ref, rb_ref, w2, q_out):

    @pl.when(own_flag(order_ref, refresh_ref))
    def _():
        for side, (factor, basis) in enumerate(((lf_ref, lb_ref), (rf_ref, rb_ref))):
            basis_hi, basis_lo = split(basis[...].T)
            w = dot(th_ref[side], basis_hi) + dot(th_ref[side], basis_lo)
            w_hi, w_lo = split(w)
            factor_hi, factor_lo = split(factor[...])
            w2[side] = w_hi
            q_out[side] = 0.95 * (
                dot(w_hi, factor_hi, NT) + dot(w_hi, factor_lo, NT) + dot(w_lo, factor_hi, NT)
            )


def gram_schmidt(q_ref):
    width = q_ref.shape[0]
    rows = lax.broadcasted_iota(jnp.int32, (width, 1), 0)

    def one(at, carry):
        row = q_ref[pl.ds(at, 1), :]
        row = row * lax.rsqrt(jnp.sum(row * row))
        q = q_ref[...]
        share = jnp.sum(q * row, axis=1, keepdims=True)
        q_ref[...] = q - jnp.where(rows > at, share, 0.0) * row
        q_ref[pl.ds(at, 1), :] = row
        return carry

    lax.fori_loop(0, width, one, 0)


def slice_kernel(parts_hbm, *rest):
    outs, sems = rest[:-1], rest[-1]
    replicas = lax.axis_size("replica")
    slots, _, half = outs[0].shape
    pairs = []
    for event, out in enumerate(outs):
        step, way = divmod(event, 2)
        first = passing_group(step + 1, way, replicas) * slots
        pairs.append((parts_hbm.at[pl.ds(first, slots), :, pl.ds(way * half, half)], out))
    wait_copies(start_copies(pairs, sems))


def passing_group(step, way, replicas):
    ahead = (2 * replicas - 1 - step) if way == 0 else (1 + step)
    return lax.rem(lax.axis_index("replica") + ahead, replicas)


def add_kernel(got_ref, own_ref, out_ref):
    out_ref[...] = (got_ref[...].astype(F32) + own_ref[...].astype(F32)).astype(BF16)


def finish_kernel(order_ref, got_right_ref, got_left_ref, own_right_ref, own_left_ref, out_ref):
    slots = out_ref.shape[0]
    half = got_right_ref.shape[2]
    first = lax.axis_index("replica") * slots
    for i in range(slots):
        at = order_ref[first + i] - first
        for got_ref, own_ref, cols in (
            (got_right_ref, own_right_ref, slice(0, half)),
            (got_left_ref, own_left_ref, slice(half, 2 * half)),
        ):
            out_ref[i, :, cols] = (got_ref[at].astype(F32) + own_ref[at].astype(F32)).astype(BF16)


def place_kernel(order_ref, rows_ref, out_hbm, sems):
    slots = rows_ref.shape[0]
    first = lax.axis_index("replica") * slots
    wait_copies(start_copies(
        [(rows_ref.at[i], out_hbm.at[order_ref[first + i] - first]) for i in range(slots)], sems
    ))


def update_kernel(order_ref, refresh_ref, grad_ref, w_ref, q_ref, lf_ref, rf_ref, lb_ref, rb_ref,
                  moment_ref, second_ref, update_ref, left_hbm, right_hbm,
                  q2, h2, l2, s2, new2, out_sems):
    flag = own_flag(order_ref, refresh_ref)
    width = grad_ref.shape[0]
    weight = 0.05 / width
    grad = grad_ref[...]
    grad_t = grad.T
    new2[0] = 0.95 * lf_ref[...] + weight * dot(grad, grad, NT)
    new2[1] = 0.95 * rf_ref[...] + weight * dot(grad_t, grad_t, NT)
    out_copies = start_copies([(new2.at[0], left_hbm), (new2.at[1], right_hbm)], out_sems)

    @pl.when(jnp.logical_not(flag))
    def _():
        store_split(h2.at[0], l2.at[0], lb_ref[...].T)
        store_split(h2.at[1], l2.at[1], rb_ref[...].T)

    @pl.when(flag)
    def _():
        part = dot(w_ref[0], grad).astype(BF16)
        q_left = q_ref[0] + weight * dot(part, grad, NT)
        part = dot(w_ref[1], grad, NT).astype(BF16)
        q_right = q_ref[1] + weight * dot(part, grad)
        q2[0] = q_left
        h2[0] = q_left.astype(BF16)
        q2[1] = q_right
        h2[1] = q_right.astype(BF16)

        one_step(q2, h2, s2, None, None)
        one_step(q2, h2, s2, None, None)
        worst = steps_until(END_BOUND, 20, q2, h2, s2, None, None)

        @pl.when(jnp.logical_not(worst <= END_BOUND))
        def _():
            for side, basis in enumerate((lb_ref, rb_ref)):
                q2[side] = lax.dot_general(
                    new2[side], basis[...], NN,
                    precision=lax.Precision.HIGHEST, preferred_element_type=F32,
                ).T
                gram_schmidt(q2.at[side])

        for side in range(2):
            store_split(h2.at[side], l2.at[side], q2[side])

    left_hi = h2[0]
    left_lo = l2[0]
    right_hi = h2[1]
    right_lo = l2[1]
    rotated = dot(dot(left_hi, grad).astype(BF16), right_hi, NT)
    moment_hi, moment_lo = split(0.9 * moment_ref[...] + 0.1 * grad.astype(F32))
    part = dot(left_hi, moment_hi) + dot(left_lo, moment_hi) + dot(left_hi, moment_lo)
    part_hi, part_lo = split(part)
    moment = (
        dot(part_hi, right_hi, NT) + dot(part_hi, right_lo, NT) + dot(part_lo, right_hi, NT)
    )
    second = 0.95 * second_ref[...] + 0.05 * rotated * rotated
    root = second * lax.rsqrt(second) + 1e-8
    scaled = (moment * pl.reciprocal(root, approx=True)).astype(BF16)
    part = (dot(left_hi.T, scaled) + dot(left_lo.T, scaled)).astype(BF16)
    update_ref[...] = (dot(part, right_hi) + dot(part, right_lo)).astype(BF16)
    wait_copies(out_copies)


SMEM_SPEC = pl.BlockSpec(memory_space=pltpu.SMEM)
VMEM_SPEC = pl.BlockSpec(memory_space=pltpu.VMEM)
HBM_SPEC = pl.BlockSpec(memory_space=pltpu.HBM)


def call(kernel, name, in_smem, in_vmem, in_hbm, out_vmem, out_hbm=(), scratch=(), sems=(), flops=0):
    operands = (*in_smem, *in_vmem, *in_hbm)
    return pl.pallas_call(
        kernel,
        out_shape=[jax.ShapeDtypeStruct(shape, dtype) for shape, dtype in (*out_vmem, *out_hbm)],
        in_specs=[SMEM_SPEC] * len(in_smem) + [VMEM_SPEC] * len(in_vmem) + [HBM_SPEC] * len(in_hbm),
        out_specs=[VMEM_SPEC] * len(out_vmem) + [HBM_SPEC] * len(out_hbm),
        scratch_shapes=[pltpu.VMEM(shape, dtype) for shape, dtype in scratch]
        + [pltpu.SemaphoreType.DMA((count,)) for count in sems],
        compiler_params=pltpu.CompilerParams(vmem_limit_bytes=VMEM_LIMIT),
        cost_estimate=pl.CostEstimate(
            flops=flops,
            bytes_accessed=sum(x.size * x.dtype.itemsize for x in in_vmem),
            transcendentals=0,
        ),
        name=name,
    )(*operands)


def on_device(
    grad_parts,
    moment,
    second_moment,
    left_factor,
    right_factor,
    left_basis,
    right_basis,
    block_order,
    refresh_ids,
):
    replicas = lax.axis_size("replica")
    owners = lax.axis_size("fsdp")
    group_size = grad_parts.shape[1] // replicas
    rows = grad_parts.shape[2]
    width = grad_parts.shape[3]
    square = (width, width)
    pair = (2,) + square
    work = [(pair, F32), (pair, F32), (pair, BF16)]
    slots = (block_order, refresh_ids)
    state_arrays = (left_factor[0], right_factor[0], left_basis[0], right_basis[0])
    steps = replicas - 1

    chunk = ((group_size, rows, width // 2), BF16)

    def stage(at, tied, state):
        flops = 20 * width**3
        given = (tied, refresh_ids)
        if at == 0:
            return call(
                prepare_start, "prepare_start", given, state_arrays, (),
                [(pair, BF16)] * 2, flops=flops,
            )
        if at == 3:
            return call(
                prepare_last, "prepare_last", given, (*state, *state_arrays), (),
                [(pair, BF16), (pair, F32)], flops=flops,
            )
        return call(
            prepare_boost if at == 1 else prepare_more, "prepare_boost" if at == 1 else "prepare_more",
            given, state, (), [(pair, BF16)] * 2, scratch=work, flops=flops,
        )

    ways = (
        [(i, (i + 1) % replicas) for i in range(replicas)],
        [(i, (i - 1) % replicas) for i in range(replicas)],
    )
    half = width // 2
    send = [
        lax.dynamic_slice(
            grad_parts[0],
            (passing_group(0, way, replicas) * group_size, 0, way * half),
            (group_size, rows, half),
        )
        for way in range(2)
    ]
    tied, *send = lax.optimization_barrier((block_order, *send))
    got = [lax.ppermute(send[way], "replica", ways[way]) for way in range(2)]
    own = list(
        call(
            slice_kernel, "own_blocks", (), (), (grad_parts[0],), [chunk] * (2 * steps),
            sems=[2 * steps],
        )
    )
    state = ()
    for event in range(2 * steps):
        way = event % 2
        if 1 < event < 6:
            state = stage(event - 2, tied, state)
            own[event], *state = lax.optimization_barrier((own[event], *state))
        if event < 2 * steps - 2:
            (send[way],) = call(
                add_kernel, ("add_right", "add_left")[way], (), (got[way], own[event]), (), [chunk]
            )
            tied, send[way] = lax.optimization_barrier((block_order, send[way]))
            got[way] = lax.ppermute(send[way], "replica", ways[way])
        elif way == 0:
            tied, got[0] = lax.optimization_barrier((block_order, got[0]))
    (summed,) = call(
        finish_kernel, "finish", (block_order,), (*got, *own[-2:]), (),
        [((group_size, rows, width), BF16)],
    )
    gradient = lax.all_to_all(summed, "fsdp", split_axis=0, concat_axis=0, tiled=True)
    update, left_new, right_new = call(
        update_kernel, "update", slots,
        (gradient.reshape(square), *state, *state_arrays, moment[0], second_moment[0]), (),
        [(square, BF16)], [(square, F32)] * 2,
        scratch=[(pair, F32), (pair, BF16), (pair, BF16), (pair, BF16), (pair, F32)],
        sems=[2], flops=100 * width**3,
    )
    returned = lax.all_to_all(
        update.reshape(owners, rows, width), "fsdp", split_axis=0, concat_axis=0, tiled=True
    )
    (step_dir,) = call(
        place_kernel, "place", (block_order,), (returned,), (), (),
        [((group_size, rows, width), BF16)], sems=[group_size],
    )
    return step_dir, left_new[None], right_new[None]


def solution(mesh):
    placed = (
        P("replica", None, "fsdp", None),
        P(("replica", "fsdp"), None, None),
        P(("replica", "fsdp"), None, None),
        P(("replica", "fsdp"), None, None),
        P(("replica", "fsdp"), None, None),
        P(("replica", "fsdp"), None, None),
        P(("replica", "fsdp"), None, None),
        P(),
        P(),
    )
    return jax.shard_map(
        on_device,
        mesh=mesh,
        in_specs=placed,
        out_specs=(
            P("replica", "fsdp", None),
            P(("replica", "fsdp"), None, None),
            P(("replica", "fsdp"), None, None),
        ),
        check_vma=False,
    )
```

```python
import functools

import jax
import jax.numpy as jnp
from jax import lax
from jax.experimental import pallas as pl
from jax.experimental.pallas import tpu as pltpu
from jax.sharding import PartitionSpec as P

F32 = jnp.float32
BF16 = jnp.bfloat16
NN = (((1,), (0,)), ((), ()))
NT = (((1,), (1,)), ((), ()))
VMEM_LIMIT = 20 * 1024 * 1024

START_BOUND = 8.0
END_BOUND = 0.016


def dot(a, b, form=NN):
    return lax.dot_general(a, b, form, preferred_element_type=F32)


def split(x):
    hi = x.astype(BF16)
    return hi, (x - hi.astype(F32)).astype(BF16)


def store_split(hi_ref, lo_ref, x):
    hi, lo = split(x)
    hi_ref[...] = hi
    lo_ref[...] = lo


def ranges(width):
    return slice(0, width // 2), slice(width // 2, width)


def triangle(hi_ref, step_ref):
    first, last = ranges(hi_ref.shape[0])
    square = (first.stop, first.stop)
    rows = lax.broadcasted_iota(jnp.int32, square, 0)
    cols = lax.broadcasted_iota(jnp.int32, square, 1)
    weight = jnp.where(rows > cols, 1.0, jnp.where(rows == cols, 0.5, 0.0))
    half_eye = jnp.where(rows == cols, 0.5, 0.0)
    step = dot(hi_ref[last, :], hi_ref[first, :], NT)
    total = step * step
    step_ref[last, first] = step.astype(BF16)
    for part in (first, last):
        step = dot(hi_ref[part, :], hi_ref[part, :], NT) * weight - half_eye
        total += step * step
        step_ref[part, part] = step.astype(BF16)
    return total


def apply_step(q_ref, hi_ref, step_ref, keep=1.0, gain=1.0):
    first, last = ranges(q_ref.shape[0])
    for rows, reach in ((last, q_ref.shape[0]), (first, first.stop)):
        q_new = keep * q_ref[rows, :] - gain * dot(step_ref[rows, :reach], hi_ref[:reach, :])
        q_ref[rows, :] = q_new
        hi_ref[rows, :] = q_new.astype(BF16)


def apply_triangle(t_ref, hi_ref, step_ref, keep=1.0, gain=1.0):
    first, last = ranges(t_ref.shape[0])
    for rows, cols, reach in (
        (last, first, slice(0, last.stop)), (last, last, last), (first, first, first)
    ):
        new = keep * t_ref[rows, cols] - gain * dot(step_ref[rows, reach], hi_ref[reach, cols])
        t_ref[rows, cols] = new
        hi_ref[rows, cols] = new.astype(BF16)


def one_step(q2, h2, s2, t2, th2, keep=1.0, gain=1.0):
    totals = [triangle(h2.at[side], s2.at[side]) for side in range(2)]
    for side in range(2):
        apply_step(q2.at[side], h2.at[side], s2.at[side], keep, gain)
        if t2 is not None:
            apply_triangle(t2.at[side], th2.at[side], s2.at[side], keep, gain)
    return totals


def steps_until(bound, most, *refs):
    return lax.while_loop(
        lambda carry: (carry[0] < most) & (carry[1] > bound),
        lambda carry: (carry[0] + 1, jnp.maximum(*map(jnp.sum, one_step(*refs)))),
        (jnp.int32(0), jnp.float32(1e30)),
    )[1]


def own_flag(order_ref, refresh_ref):
    owners = lax.axis_size("fsdp")
    block = order_ref[lax.axis_index("replica") * owners + lax.axis_index("fsdp")]
    flag = block == refresh_ref[0]
    for j in range(1, refresh_ref.shape[0]):
        flag |= block == refresh_ref[j]
    return flag


def start_copies(pairs, sems):
    copies = [pltpu.make_async_copy(src, dst, sems.at[i]) for i, (src, dst) in enumerate(pairs)]
    for copy in copies:
        copy.start()
    return copies


def wait_copies(copies):
    for copy in copies:
        copy.wait()


def prepare_start(order_ref, refresh_ref, lf_ref, rf_ref, lb_ref, rb_ref, h2, th2):

    @pl.when(own_flag(order_ref, refresh_ref))
    def _():
        width = lf_ref.shape[0]
        eye = (
            lax.broadcasted_iota(jnp.int32, (width, width), 0)
            == lax.broadcasted_iota(jnp.int32, (width, width), 1)
        )
        for side, (factor, basis) in enumerate(((lf_ref, lb_ref), (rf_ref, rb_ref))):
            p = dot(factor[...].astype(BF16), basis[...].astype(BF16))
            scale = lax.rsqrt(jnp.sum(p * p, axis=0, keepdims=True))
            y = (p * scale).astype(BF16).T
            gram = dot(y, y, NT).astype(BF16)
            square = jnp.abs(dot(gram, gram))
            reach = jnp.max(jnp.sum(square, axis=0, keepdims=True), axis=1, keepdims=True)
            factor_all = lax.rsqrt(0.5 * jnp.sqrt(reach))
            h2[side] = (y.astype(F32) * factor_all).astype(BF16)
            th2[side] = jnp.where(eye, scale * (factor_all / 0.95), 0.0).astype(BF16)


def load_state(h_ref, th_ref, h2, th2, q2, t2):
    for side in range(2):
        h2[side] = h_ref[side]
        th2[side] = th_ref[side]
        q2[side] = h_ref[side].astype(F32)
        t2[side] = th_ref[side].astype(F32)


def prepare_boost(order_ref, refresh_ref, h_ref, th_ref, h2, th2, q2, t2, s2):
    @pl.when(own_flag(order_ref, refresh_ref))
    def _():
        load_state(h_ref, th_ref, h2, th2, q2, t2)
        for _ in range(2):
            one_step(q2, h2, s2, t2, th2, 1.3, 1.4)


def prepare_more(order_ref, refresh_ref, h_ref, th_ref, h2, th2, q2, t2, s2):
    @pl.when(own_flag(order_ref, refresh_ref))
    def _():
        load_state(h_ref, th_ref, h2, th2, q2, t2)
        one_step(q2, h2, s2, t2, th2)
        one_step(q2, h2, s2, t2, th2)
        steps_until(START_BOUND, 16, q2, h2, s2, t2, th2)


def prepare_last(order_ref, refresh_ref, h_ref, th_ref, lf_ref, rf_ref, lb_ref, rb_ref, w2, q_out):

    @pl.when(own_flag(order_ref, refresh_ref))
    def _():
        for side, (factor, basis) in enumerate(((lf_ref, lb_ref), (rf_ref, rb_ref))):
            basis_hi, basis_lo = split(basis[...])
            w = dot(th_ref[side], basis_hi, NT) + dot(th_ref[side], basis_lo, NT)
            w_hi, w_lo = split(w)
            factor_hi, factor_lo = split(factor[...])
            w2[side] = w_hi
            q_out[side] = 0.95 * (
                dot(w_hi, factor_hi, NT) + dot(w_hi, factor_lo, NT) + dot(w_lo, factor_hi, NT)
            )


def gram_schmidt(q_ref):
    width = q_ref.shape[0]
    rows = lax.broadcasted_iota(jnp.int32, (width, 1), 0)

    def one(at, carry):
        row = q_ref[pl.ds(at, 1), :]
        row = row * lax.rsqrt(jnp.sum(row * row))
        q = q_ref[...]
        share = jnp.sum(q * row, axis=1, keepdims=True)
        q_ref[...] = q - jnp.where(rows > at, share, 0.0) * row
        q_ref[pl.ds(at, 1), :] = row
        return carry

    lax.fori_loop(0, width, one, 0)


def slice_kernel(parts_hbm, *rest):
    outs, sems = rest[:-1], rest[-1]
    replicas = lax.axis_size("replica")
    slots, _, half = outs[0].shape
    pairs = []
    for event, out in enumerate(outs):
        step, way = divmod(event, 2)
        first = passing_group(step + 1, way, replicas) * slots
        pairs.append((parts_hbm.at[pl.ds(first, slots), :, pl.ds(way * half, half)], out))
    wait_copies(start_copies(pairs, sems))


def passing_group(step, way, replicas):
    ahead = (2 * replicas - 1 - step) if way == 0 else (1 + step)
    return lax.rem(lax.axis_index("replica") + ahead, replicas)


def add_kernel(got_ref, own_ref, out_ref):
    out_ref[...] = (got_ref[...].astype(F32) + own_ref[...].astype(F32)).astype(BF16)


def finish_kernel(order_ref, got_right_ref, got_left_ref, own_right_ref, own_left_ref, out_ref):
    slots = out_ref.shape[0]
    half = got_right_ref.shape[2]
    first = lax.axis_index("replica") * slots
    for i in range(slots):
        at = order_ref[first + i] - first
        for got_ref, own_ref, cols in (
            (got_right_ref, own_right_ref, slice(0, half)),
            (got_left_ref, own_left_ref, slice(half, 2 * half)),
        ):
            out_ref[i, :, cols] = (got_ref[at].astype(F32) + own_ref[at].astype(F32)).astype(BF16)


def place_kernel(order_ref, rows_ref, out_hbm, sems):
    slots = rows_ref.shape[0]
    first = lax.axis_index("replica") * slots
    wait_copies(start_copies(
        [(rows_ref.at[i], out_hbm.at[order_ref[first + i] - first]) for i in range(slots)], sems
    ))


def update_kernel(order_ref, refresh_ref, grad_ref, w_ref, q_ref, lf_ref, rf_ref, lb_ref, rb_ref,
                  moment_ref, second_ref, update_ref, left_hbm, right_hbm,
                  q2, h2, l2, s2, new2, out_sems):
    flag = own_flag(order_ref, refresh_ref)
    width = grad_ref.shape[0]
    weight = 0.05 / width
    grad = grad_ref[...]
    grad_t = grad.T
    new2[0] = 0.95 * lf_ref[...] + weight * dot(grad, grad, NT)
    new2[1] = 0.95 * rf_ref[...] + weight * dot(grad_t, grad_t, NT)
    out_copies = start_copies([(new2.at[0], left_hbm), (new2.at[1], right_hbm)], out_sems)

    @pl.when(jnp.logical_not(flag))
    def _():
        store_split(h2.at[0], l2.at[0], lb_ref[...].T)
        store_split(h2.at[1], l2.at[1], rb_ref[...].T)

    @pl.when(flag)
    def _():
        part = dot(w_ref[0], grad).astype(BF16)
        q_left = q_ref[0] + weight * dot(part, grad, NT)
        part = dot(w_ref[1], grad, NT).astype(BF16)
        q_right = q_ref[1] + weight * dot(part, grad)
        q2[0] = q_left
        h2[0] = q_left.astype(BF16)
        q2[1] = q_right
        h2[1] = q_right.astype(BF16)

        one_step(q2, h2, s2, None, None)
        one_step(q2, h2, s2, None, None)
        worst = steps_until(END_BOUND, 20, q2, h2, s2, None, None)

        @pl.when(jnp.logical_not(worst <= END_BOUND))
        def _():
            for side, basis in enumerate((lb_ref, rb_ref)):
                q2[side] = lax.dot_general(
                    new2[side], basis[...], NN,
                    precision=lax.Precision.HIGHEST, preferred_element_type=F32,
                ).T
                gram_schmidt(q2.at[side])

        for side in range(2):
            store_split(h2.at[side], l2.at[side], q2[side])

    left_hi = h2[0]
    left_lo = l2[0]
    right_hi = h2[1]
    right_lo = l2[1]
    rotated = dot(dot(left_hi, grad).astype(BF16), right_hi, NT)
    moment_hi, moment_lo = split(0.9 * moment_ref[...] + 0.1 * grad.astype(F32))
    part = dot(left_hi, moment_hi) + dot(left_lo, moment_hi) + dot(left_hi, moment_lo)
    part_hi, part_lo = split(part)
    moment = (
        dot(part_hi, right_hi, NT) + dot(part_hi, right_lo, NT) + dot(part_lo, right_hi, NT)
    )
    second = 0.95 * second_ref[...] + 0.05 * rotated * rotated
    root = second * lax.rsqrt(second) + 1e-8
    scaled = (moment * pl.reciprocal(root, approx=True)).astype(BF16)
    part = (dot(left_hi.T, scaled) + dot(left_lo.T, scaled)).astype(BF16)
    update_ref[...] = (dot(part, right_hi) + dot(part, right_lo)).astype(BF16)
    wait_copies(out_copies)


SMEM_SPEC = pl.BlockSpec(memory_space=pltpu.SMEM)
VMEM_SPEC = pl.BlockSpec(memory_space=pltpu.VMEM)
HBM_SPEC = pl.BlockSpec(memory_space=pltpu.HBM)


def call(kernel, name, in_smem, in_vmem, in_hbm, out_vmem, out_hbm=(), scratch=(), sems=(), flops=0):
    operands = (*in_smem, *in_vmem, *in_hbm)
    return pl.pallas_call(
        kernel,
        out_shape=[jax.ShapeDtypeStruct(shape, dtype) for shape, dtype in (*out_vmem, *out_hbm)],
        in_specs=[SMEM_SPEC] * len(in_smem) + [VMEM_SPEC] * len(in_vmem) + [HBM_SPEC] * len(in_hbm),
        out_specs=[VMEM_SPEC] * len(out_vmem) + [HBM_SPEC] * len(out_hbm),
        scratch_shapes=[pltpu.VMEM(shape, dtype) for shape, dtype in scratch]
        + [pltpu.SemaphoreType.DMA((count,)) for count in sems],
        compiler_params=pltpu.CompilerParams(vmem_limit_bytes=VMEM_LIMIT),
        cost_estimate=pl.CostEstimate(
            flops=flops,
            bytes_accessed=sum(x.size * x.dtype.itemsize for x in in_vmem),
            transcendentals=0,
        ),
        name=name,
    )(*operands)


def on_device(
    grad_parts,
    moment,
    second_moment,
    left_factor,
    right_factor,
    left_basis,
    right_basis,
    block_order,
    refresh_ids,
):
    replicas = lax.axis_size("replica")
    owners = lax.axis_size("fsdp")
    group_size = grad_parts.shape[1] // replicas
    rows = grad_parts.shape[2]
    width = grad_parts.shape[3]
    square = (width, width)
    pair = (2,) + square
    work = [(pair, F32), (pair, F32), (pair, BF16)]
    slots = (block_order, refresh_ids)
    state_arrays = (left_factor[0], right_factor[0], left_basis[0], right_basis[0])
    steps = replicas - 1

    chunk = ((group_size, rows, width // 2), BF16)

    def stage(at, tied, state):
        flops = 20 * width**3
        given = (tied, refresh_ids)
        if at == 0:
            return call(
                prepare_start, "prepare_start", given, state_arrays, (),
                [(pair, BF16)] * 2, flops=flops,
            )
        if at == 3:
            return call(
                prepare_last, "prepare_last", given, (*state, *state_arrays), (),
                [(pair, BF16), (pair, F32)], flops=flops,
            )
        return call(
            prepare_boost if at == 1 else prepare_more, "prepare_boost" if at == 1 else "prepare_more",
            given, state, (), [(pair, BF16)] * 2, scratch=work, flops=flops,
        )

    ways = (
        [(i, (i + 1) % replicas) for i in range(replicas)],
        [(i, (i - 1) % replicas) for i in range(replicas)],
    )
    half = width // 2
    send = [
        lax.dynamic_slice(
            grad_parts[0],
            (passing_group(0, way, replicas) * group_size, 0, way * half),
            (group_size, rows, half),
        )
        for way in range(2)
    ]
    tied, *send = lax.optimization_barrier((block_order, *send))
    got = [lax.ppermute(send[way], "replica", ways[way]) for way in range(2)]
    own = list(
        call(
            slice_kernel, "own_blocks", (), (), (grad_parts[0],), [chunk] * (2 * steps),
            sems=[2 * steps],
        )
    )
    state = ()
    for event in range(2 * steps):
        way = event % 2
        if 1 < event < 6:
            state = stage(event - 2, tied, state)
            own[event], *state = lax.optimization_barrier((own[event], *state))
        if event < 2 * steps - 2:
            (send[way],) = call(
                add_kernel, ("add_right", "add_left")[way], (), (got[way], own[event]), (), [chunk]
            )
            tied, send[way] = lax.optimization_barrier((block_order, send[way]))
            got[way] = lax.ppermute(send[way], "replica", ways[way])
        elif way == 0:
            tied, got[0] = lax.optimization_barrier((block_order, got[0]))
    (summed,) = call(
        finish_kernel, "finish", (block_order,), (*got, *own[-2:]), (),
        [((group_size, rows, width), BF16)],
    )
    gradient = lax.all_to_all(summed, "fsdp", split_axis=0, concat_axis=0, tiled=True)
    update, left_new, right_new = call(
        update_kernel, "update", slots,
        (gradient.reshape(square), *state, *state_arrays, moment[0], second_moment[0]), (),
        [(square, BF16)], [(square, F32)] * 2,
        scratch=[(pair, F32), (pair, BF16), (pair, BF16), (pair, BF16), (pair, F32)],
        sems=[2], flops=100 * width**3,
    )
    returned = lax.all_to_all(
        update.reshape(owners, rows, width), "fsdp", split_axis=0, concat_axis=0, tiled=True
    )
    (step_dir,) = call(
        place_kernel, "place", (block_order,), (returned,), (), (),
        [((group_size, rows, width), BF16)], sems=[group_size],
    )
    return step_dir, left_new[None], right_new[None]


def solution(mesh):
    placed = (
        P("replica", None, "fsdp", None),
        P(("replica", "fsdp"), None, None),
        P(("replica", "fsdp"), None, None),
        P(("replica", "fsdp"), None, None),
        P(("replica", "fsdp"), None, None),
        P(("replica", "fsdp"), None, None),
        P(("replica", "fsdp"), None, None),
        P(),
        P(),
    )
    return jax.shard_map(
        on_device,
        mesh=mesh,
        in_specs=placed,
        out_specs=(
            P("replica", "fsdp", None),
            P(("replica", "fsdp"), None, None),
            P(("replica", "fsdp"), None, None),
        ),
        check_vma=False,
    )
```

```python
import functools

import jax
import jax.numpy as jnp
from jax import lax
from jax.experimental import pallas as pl
from jax.experimental.pallas import tpu as pltpu
from jax.sharding import PartitionSpec as P

F32 = jnp.float32
BF16 = jnp.bfloat16
NN = (((1,), (0,)), ((), ()))
NT = (((1,), (1,)), ((), ()))
VMEM_LIMIT = 20 * 1024 * 1024

START_BOUND = 8.0
END_BOUND = 0.016


def dot(a, b, form=NN):
    return lax.dot_general(a, b, form, preferred_element_type=F32)


def split(x):
    hi = x.astype(BF16)
    return hi, (x - hi.astype(F32)).astype(BF16)


def store_split(hi_ref, lo_ref, x):
    hi, lo = split(x)
    hi_ref[...] = hi
    lo_ref[...] = lo


def ranges(width):
    return slice(0, width // 2), slice(width // 2, width)


def triangle(hi_ref, step_ref):
    first, last = ranges(hi_ref.shape[0])
    square = (first.stop, first.stop)
    rows = lax.broadcasted_iota(jnp.int32, square, 0)
    cols = lax.broadcasted_iota(jnp.int32, square, 1)
    weight = jnp.where(rows > cols, 1.0, jnp.where(rows == cols, 0.5, 0.0))
    half_eye = jnp.where(rows == cols, 0.5, 0.0)
    step = dot(hi_ref[last, :], hi_ref[first, :], NT)
    total = step * step
    step_ref[last, first] = step.astype(BF16)
    for part in (first, last):
        step = dot(hi_ref[part, :], hi_ref[part, :], NT) * weight - half_eye
        total += step * step
        step_ref[part, part] = step.astype(BF16)
    return total


def apply_step(q_ref, hi_ref, step_ref, keep=1.0, gain=1.0):
    first, last = ranges(q_ref.shape[0])
    for rows, reach in ((last, q_ref.shape[0]), (first, first.stop)):
        q_new = keep * q_ref[rows, :] - gain * dot(step_ref[rows, :reach], hi_ref[:reach, :])
        q_ref[rows, :] = q_new
        hi_ref[rows, :] = q_new.astype(BF16)


def apply_triangle(t_ref, hi_ref, step_ref, keep=1.0, gain=1.0):
    first, last = ranges(t_ref.shape[0])
    for rows, cols, reach in (
        (last, first, slice(0, last.stop)), (last, last, last), (first, first, first)
    ):
        new = keep * t_ref[rows, cols] - gain * dot(step_ref[rows, reach], hi_ref[reach, cols])
        t_ref[rows, cols] = new
        hi_ref[rows, cols] = new.astype(BF16)


def one_step(q2, h2, s2, t2, th2, keep=1.0, gain=1.0):
    totals = [triangle(h2.at[side], s2.at[side]) for side in range(2)]
    for side in range(2):
        apply_step(q2.at[side], h2.at[side], s2.at[side], keep, gain)
        if t2 is not None:
            apply_triangle(t2.at[side], th2.at[side], s2.at[side], keep, gain)
    return totals


def steps_until(bound, most, *refs):
    return lax.while_loop(
        lambda carry: (carry[0] < most) & (carry[1] > bound),
        lambda carry: (carry[0] + 1, jnp.maximum(*map(jnp.sum, one_step(*refs)))),
        (jnp.int32(0), jnp.float32(1e30)),
    )[1]


def own_flag(order_ref, refresh_ref):
    owners = lax.axis_size("fsdp")
    block = order_ref[lax.axis_index("replica") * owners + lax.axis_index("fsdp")]
    flag = block == refresh_ref[0]
    for j in range(1, refresh_ref.shape[0]):
        flag |= block == refresh_ref[j]
    return flag


def start_copies(pairs, sems):
    copies = [pltpu.make_async_copy(src, dst, sems.at[i]) for i, (src, dst) in enumerate(pairs)]
    for copy in copies:
        copy.start()
    return copies


def wait_copies(copies):
    for copy in copies:
        copy.wait()


def prepare_start(order_ref, refresh_ref, lf_ref, rf_ref, lb_ref, rb_ref, h2, th2):

    @pl.when(own_flag(order_ref, refresh_ref))
    def _():
        width = lf_ref.shape[0]
        eye = (
            lax.broadcasted_iota(jnp.int32, (width, width), 0)
            == lax.broadcasted_iota(jnp.int32, (width, width), 1)
        )
        for side, (factor, basis) in enumerate(((lf_ref, lb_ref), (rf_ref, rb_ref))):
            p = dot(factor[...].astype(BF16), basis[...].astype(BF16))
            scale = lax.rsqrt(jnp.sum(p * p, axis=0, keepdims=True))
            y = (p * scale).astype(BF16).T
            gram = dot(y, y, NT).astype(BF16)
            square = jnp.abs(dot(gram, gram))
            reach = jnp.max(jnp.sum(square, axis=0, keepdims=True), axis=1, keepdims=True)
            factor_all = lax.rsqrt(0.5 * jnp.sqrt(reach))
            h2[side] = (y.astype(F32) * factor_all).astype(BF16)
            th2[side] = jnp.where(eye, scale * (factor_all / 0.95), 0.0).astype(BF16)


def load_state(h_ref, th_ref, h2, th2, q2, t2):
    for side in range(2):
        h2[side] = h_ref[side]
        th2[side] = th_ref[side]
        q2[side] = h_ref[side].astype(F32)
        t2[side] = th_ref[side].astype(F32)


def prepare_boost(order_ref, refresh_ref, h_ref, th_ref, h2, th2, q2, t2, s2):
    @pl.when(own_flag(order_ref, refresh_ref))
    def _():
        load_state(h_ref, th_ref, h2, th2, q2, t2)
        for _ in range(2):
            one_step(q2, h2, s2, t2, th2, 1.3, 1.4)


def prepare_more(order_ref, refresh_ref, h_ref, th_ref, h2, th2, q2, t2, s2):
    @pl.when(own_flag(order_ref, refresh_ref))
    def _():
        load_state(h_ref, th_ref, h2, th2, q2, t2)
        one_step(q2, h2, s2, t2, th2)
        one_step(q2, h2, s2, t2, th2)
        steps_until(START_BOUND, 16, q2, h2, s2, t2, th2)


def prepare_last(order_ref, refresh_ref, h_ref, th_ref, lf_ref, rf_ref, lb_ref, rb_ref, w2, q_out):

    @pl.when(own_flag(order_ref, refresh_ref))
    def _():
        for side, (factor, basis) in enumerate(((lf_ref, lb_ref), (rf_ref, rb_ref))):
            basis_hi, basis_lo = split(basis[...])
            w = dot(th_ref[side], basis_hi, NT) + dot(th_ref[side], basis_lo, NT)
            w_hi, w_lo = split(w)
            factor_hi, factor_lo = split(factor[...])
            w2[side] = w_hi
            q_out[side] = 0.95 * (
                dot(w_hi, factor_hi, NT) + dot(w_hi, factor_lo, NT) + dot(w_lo, factor_hi, NT)
            )


def gram_schmidt(q_ref):
    width = q_ref.shape[0]
    rows = lax.broadcasted_iota(jnp.int32, (width, 1), 0)

    def one(at, carry):
        row = q_ref[pl.ds(at, 1), :]
        row = row * lax.rsqrt(jnp.sum(row * row))
        q = q_ref[...]
        share = jnp.sum(q * row, axis=1, keepdims=True)
        q_ref[...] = q - jnp.where(rows > at, share, 0.0) * row
        q_ref[pl.ds(at, 1), :] = row
        return carry

    lax.fori_loop(0, width, one, 0)


def slice_kernel(parts_hbm, *rest):
    outs, sems = rest[:-1], rest[-1]
    replicas = lax.axis_size("replica")
    slots, _, half = outs[0].shape
    pairs = []
    for event, out in enumerate(outs):
        step, way = divmod(event, 2)
        first = passing_group(step + 1, way, replicas) * slots
        pairs.append((parts_hbm.at[pl.ds(first, slots), :, pl.ds(way * half, half)], out))
    wait_copies(start_copies(pairs, sems))


def passing_group(step, way, replicas):
    ahead = (2 * replicas - 1 - step) if way == 0 else (1 + step)
    return lax.rem(lax.axis_index("replica") + ahead, replicas)


def add_kernel(got_ref, own_ref, out_ref):
    out_ref[...] = (got_ref[...].astype(F32) + own_ref[...].astype(F32)).astype(BF16)


def finish_kernel(order_ref, got_right_ref, got_left_ref, own_right_ref, own_left_ref, out_ref):
    slots = out_ref.shape[0]
    half = got_right_ref.shape[2]
    first = lax.axis_index("replica") * slots
    for i in range(slots):
        at = order_ref[first + i] - first
        for got_ref, own_ref, cols in (
            (got_right_ref, own_right_ref, slice(0, half)),
            (got_left_ref, own_left_ref, slice(half, 2 * half)),
        ):
            out_ref[i, :, cols] = (got_ref[at].astype(F32) + own_ref[at].astype(F32)).astype(BF16)


def place_kernel(order_ref, rows_ref, out_hbm, sems):
    slots = rows_ref.shape[0]
    first = lax.axis_index("replica") * slots
    wait_copies(start_copies(
        [(rows_ref.at[i], out_hbm.at[order_ref[first + i] - first]) for i in range(slots)], sems
    ))


def update_kernel(order_ref, refresh_ref, grad_ref, w_ref, q_ref, lf_ref, rf_ref, lb_ref, rb_ref,
                  moment_ref, second_ref, update_ref, left_hbm, right_hbm,
                  q2, h2, l2, s2, new2, out_sems):
    flag = own_flag(order_ref, refresh_ref)
    width = grad_ref.shape[0]
    weight = 0.05 / width
    grad = grad_ref[...]
    grad_t = grad.T
    new2[0] = 0.95 * lf_ref[...] + weight * dot(grad, grad, NT)
    new2[1] = 0.95 * rf_ref[...] + weight * dot(grad_t, grad_t, NT)
    out_copies = start_copies([(new2.at[0], left_hbm), (new2.at[1], right_hbm)], out_sems)

    @pl.when(jnp.logical_not(flag))
    def _():
        store_split(h2.at[0], l2.at[0], lb_ref[...].T)
        store_split(h2.at[1], l2.at[1], rb_ref[...].T)

    @pl.when(flag)
    def _():
        part = dot(w_ref[0], grad).astype(BF16)
        q_left = q_ref[0] + weight * dot(part, grad, NT)
        part = dot(w_ref[1], grad, NT).astype(BF16)
        q_right = q_ref[1] + weight * dot(part, grad)
        q2[0] = q_left
        h2[0] = q_left.astype(BF16)
        q2[1] = q_right
        h2[1] = q_right.astype(BF16)

        one_step(q2, h2, s2, None, None)
        one_step(q2, h2, s2, None, None)
        worst = steps_until(END_BOUND, 20, q2, h2, s2, None, None)

        @pl.when(jnp.logical_not(worst <= END_BOUND))
        def _():
            for side, basis in enumerate((lb_ref, rb_ref)):
                q2[side] = lax.dot_general(
                    new2[side], basis[...], NN,
                    precision=lax.Precision.HIGHEST, preferred_element_type=F32,
                ).T
                gram_schmidt(q2.at[side])

        for side in range(2):
            store_split(h2.at[side], l2.at[side], q2[side])

    left_hi = h2[0]
    left_lo = l2[0]
    right_hi = h2[1]
    right_lo = l2[1]
    rotated = dot(dot(left_hi, grad).astype(BF16), right_hi, NT)
    moment_hi, moment_lo = split(0.9 * moment_ref[...] + 0.1 * grad.astype(F32))
    part = dot(left_hi, moment_hi) + dot(left_lo, moment_hi) + dot(left_hi, moment_lo)
    part_hi, part_lo = split(part)
    moment = (
        dot(part_hi, right_hi, NT) + dot(part_hi, right_lo, NT) + dot(part_lo, right_hi, NT)
    )
    second = 0.95 * second_ref[...] + 0.05 * rotated * rotated
    root = second * lax.rsqrt(second) + 1e-8
    scaled = (moment * pl.reciprocal(root, approx=True)).astype(BF16)
    part = (dot(left_hi.T, scaled) + dot(left_lo.T, scaled)).astype(BF16)
    update_ref[...] = (dot(part, right_hi) + dot(part, right_lo)).astype(BF16)
    wait_copies(out_copies)


SMEM_SPEC = pl.BlockSpec(memory_space=pltpu.SMEM)
VMEM_SPEC = pl.BlockSpec(memory_space=pltpu.VMEM)
HBM_SPEC = pl.BlockSpec(memory_space=pltpu.HBM)


def call(kernel, name, in_smem, in_vmem, in_hbm, out_vmem, out_hbm=(), scratch=(), sems=(), flops=0):
    operands = (*in_smem, *in_vmem, *in_hbm)
    return pl.pallas_call(
        kernel,
        out_shape=[jax.ShapeDtypeStruct(shape, dtype) for shape, dtype in (*out_vmem, *out_hbm)],
        in_specs=[SMEM_SPEC] * len(in_smem) + [VMEM_SPEC] * len(in_vmem) + [HBM_SPEC] * len(in_hbm),
        out_specs=[VMEM_SPEC] * len(out_vmem) + [HBM_SPEC] * len(out_hbm),
        scratch_shapes=[pltpu.VMEM(shape, dtype) for shape, dtype in scratch]
        + [pltpu.SemaphoreType.DMA((count,)) for count in sems],
        compiler_params=pltpu.CompilerParams(vmem_limit_bytes=VMEM_LIMIT),
        cost_estimate=pl.CostEstimate(
            flops=flops,
            bytes_accessed=sum(x.size * x.dtype.itemsize for x in in_vmem),
            transcendentals=0,
        ),
        name=name,
    )(*operands)


def on_device(
    grad_parts,
    moment,
    second_moment,
    left_factor,
    right_factor,
    left_basis,
    right_basis,
    block_order,
    refresh_ids,
):
    replicas = lax.axis_size("replica")
    owners = lax.axis_size("fsdp")
    group_size = grad_parts.shape[1] // replicas
    rows = grad_parts.shape[2]
    width = grad_parts.shape[3]
    square = (width, width)
    pair = (2,) + square
    work = [(pair, F32), (pair, F32), (pair, BF16)]
    slots = (block_order, refresh_ids)
    state_arrays = (left_factor[0], right_factor[0], left_basis[0], right_basis[0])
    steps = replicas - 1

    chunk = ((group_size, rows, width // 2), BF16)

    def stage(at, tied, state):
        flops = 20 * width**3
        given = (tied, refresh_ids)
        if at == 0:
            return call(
                prepare_start, "prepare_start", given, state_arrays, (),
                [(pair, BF16)] * 2, flops=flops,
            )
        if at == 3:
            return call(
                prepare_last, "prepare_last", given, (*state, *state_arrays), (),
                [(pair, BF16), (pair, F32)], flops=flops,
            )
        return call(
            prepare_boost if at == 1 else prepare_more, "prepare_boost" if at == 1 else "prepare_more",
            given, state, (), [(pair, BF16)] * 2, scratch=work, flops=flops,
        )

    ways = (
        [(i, (i + 1) % replicas) for i in range(replicas)],
        [(i, (i - 1) % replicas) for i in range(replicas)],
    )
    half = width // 2
    send = [None, None]
    start = passing_group(0, 1, replicas) * group_size
    for way in range(2):
        first = passing_group(0, 0, replicas) * group_size if way == 0 else start
        send[way] = lax.dynamic_slice(
            grad_parts[0], (first, 0, way * half), (group_size, rows, half)
        )
        if way == 0:
            start, send[0] = lax.optimization_barrier((start, send[0]))
    tied, send[1] = lax.optimization_barrier((block_order, send[1]))
    got = [lax.ppermute(send[way], "replica", ways[way]) for way in range(2)]
    own = list(
        call(
            slice_kernel, "own_blocks", (), (), (grad_parts[0],), [chunk] * (2 * steps),
            sems=[2 * steps],
        )
    )
    state = ()
    for event in range(2 * steps):
        way = event % 2
        if 1 < event < 6:
            state = stage(event - 2, tied, state)
            own[event], *state = lax.optimization_barrier((own[event], *state))
        if event < 2 * steps - 2:
            (send[way],) = call(
                add_kernel, ("add_right", "add_left")[way], (), (got[way], own[event]), (), [chunk]
            )
            tied, send[way] = lax.optimization_barrier((block_order, send[way]))
            got[way] = lax.ppermute(send[way], "replica", ways[way])
        elif way == 0:
            tied, got[0] = lax.optimization_barrier((block_order, got[0]))
    (summed,) = call(
        finish_kernel, "finish", (block_order,), (*got, *own[-2:]), (),
        [((group_size, rows, width), BF16)],
    )
    gradient = lax.all_to_all(summed, "fsdp", split_axis=0, concat_axis=0, tiled=True)
    update, left_new, right_new = call(
        update_kernel, "update", slots,
        (gradient.reshape(square), *state, *state_arrays, moment[0], second_moment[0]), (),
        [(square, BF16)], [(square, F32)] * 2,
        scratch=[(pair, F32), (pair, BF16), (pair, BF16), (pair, BF16), (pair, F32)],
        sems=[2], flops=100 * width**3,
    )
    returned = lax.all_to_all(
        update.reshape(owners, rows, width), "fsdp", split_axis=0, concat_axis=0, tiled=True
    )
    (step_dir,) = call(
        place_kernel, "place", (block_order,), (returned,), (), (),
        [((group_size, rows, width), BF16)], sems=[group_size],
    )
    return step_dir, left_new[None], right_new[None]


def solution(mesh):
    placed = (
        P("replica", None, "fsdp", None),
        P(("replica", "fsdp"), None, None),
        P(("replica", "fsdp"), None, None),
        P(("replica", "fsdp"), None, None),
        P(("replica", "fsdp"), None, None),
        P(("replica", "fsdp"), None, None),
        P(("replica", "fsdp"), None, None),
        P(),
        P(),
    )
    return jax.shard_map(
        on_device,
        mesh=mesh,
        in_specs=placed,
        out_specs=(
            P("replica", "fsdp", None),
            P(("replica", "fsdp"), None, None),
            P(("replica", "fsdp"), None, None),
        ),
        check_vma=False,
    )
```
